32 devices in a mesh: patch: 16 (over z, y, x), head: 2 (over core).
Axes of the slice: x: 2, y: 2, z: 4, core: 2. Of those that a mesh axis runs over, the one named last changes fastest.
Arguments:
- inputs: bfloat16 [2, 512, 3072], P(None, 'patch', 'head'), may hold values from -111 to 111
- stale_kv: bfloat16 [2, 512, 512], P(None, 'patch', 'head'), may hold values from -16 to 16
- w_qkv: bfloat16 [3072, 3, 512], P(None, None, 'head'), may hold values from -4 to 4
- w_out: bfloat16 [512, 3072], P('head', 'patch'), may hold values from -0.375 to 0.375
- mod_table: float32 [4, 3, 3072], P(None, None, 'head'), may hold values from -2 to 2
- step_ids: int32 [2], replicated, may hold values from 0 to 3
- slab_order: int32 [16], P('patch'), may hold values from 0 to 15, each once
Outputs:
- branch: bfloat16 [2, 512, 3072], P(None, 'patch', 'head')
The draws below stay inside these ranges and needn't reach their ends.
Inputs may be any that keep to these rules, and one draw needn't show every extreme that they name: `slab_order`: every slab number once.
All inputs are finite; a program needn't handle non-finite values.
Results may differ from the reference program's by a relative error of at most 0.02.
Values may be sent and summed in bfloat16 or wider, within the bound.
No kernel may reach another device: no remote copies, remote signals or barrier semaphores. Data moves between devices by JAX's collectives and lax.ppermute only.
A program may use at most 64 MiB of HBM per device.

```python
import math
import jax
import jax.numpy as jnp
from jax import lax

D = 3072
DH = 128
TOK_DEV = 32
STEPS = 2
TABLE = 4
HEADS = 4
TOKENS = 512
N_PATCH = 16


def draw_inputs(key, part):
    key = jax.random.fold_in(key, 11)
    key_base = jax.random.fold_in(key, 0)
    col_ramp = 3.0 ** (jnp.arange(D, dtype=jnp.float32) / (D - 1))
    drawn = jnp.clip(jax.random.normal(key_base, (STEPS, TOKENS, D), jnp.float32), -4.0, 4.0) * col_ramp
    return drawn.astype(jnp.bfloat16)


def draw_stale_kv(key, part):
    key = jax.random.fold_in(key, 37)
    key_keys, key_rows, key_vals = jax.random.split(key, 3)
    head_shape = (TOKENS, HEADS, DH)
    row_scale = jnp.exp(jax.random.uniform(key_rows, (TOKENS, HEADS, 1), jnp.float32, math.log(0.08), math.log(0.8)))
    key_part = jnp.clip(jax.random.normal(key_keys, head_shape, jnp.float32), -4.0, 4.0) * row_scale
    value_part = 8.0 * jnp.clip(jax.random.normal(key_vals, head_shape, jnp.float32), -2.0, 2.0)
    drawn = jnp.stack([key_part.reshape(TOKENS, HEADS * DH), value_part.reshape(TOKENS, HEADS * DH)])
    return drawn.astype(jnp.bfloat16)


def draw_w_qkv(key, part):
    key = jax.random.fold_in(key, 53)
    key_base = jax.random.fold_in(key, 0)
    base_vals = jnp.clip(jax.random.normal(key_base, (D, 3, HEADS * DH), jnp.float32), -4.0, 4.0) / D ** 0.5
    slot_gain = jnp.array([1.0, 0.8, 8.0], jnp.float32)[None, :, None]
    gain_all = slot_gain
    return (base_vals * gain_all).astype(jnp.bfloat16)


def draw_mod_table(key, part):
    key = jax.random.fold_in(key, 23)
    key_shift, key_scale, key_gate, key_sign = jax.random.split(key, 4)
    shifting = 0.5 * jnp.clip(jax.random.normal(key_shift, (TABLE, 1, D), jnp.float32), -2.0, 2.0)
    signs = 2.0 * jax.random.randint(key_sign, (TABLE, 1, D), 0, 2).astype(jnp.float32) - 1.0
    scaling = 0.5 * jnp.clip(jax.random.normal(key_scale, (TABLE, 1, D), jnp.float32), -2.0, 2.0)
    gating = signs * jax.random.uniform(key_gate, (TABLE, 1, D), jnp.float32, 0.4, 2.0)
    return jnp.concatenate([shifting, scaling, gating], axis=1)


def strengthened(entries, stream_key, source, target, parts, factor):
    def block_of(dim):
        return (jnp.arange(entries.shape[dim]) // (entries.shape[dim] // parts)).reshape((-1,) + (1,) * (entries.ndim - 1 - dim))

    first = jax.random.permutation(stream_key, parts)[block_of(target)]
    far = (block_of(target) + parts // 2) % parts
    return jnp.where((block_of(source) == first) | (block_of(source) == far), factor * entries, entries)


def levels(key, shape, cuts, low, top_value):
    gain = 1.0
    for position, parts in cuts:
        draws = jax.random.uniform(jax.random.fold_in(jax.random.fold_in(key, 6), position), (parts,), jnp.float32, low / len(cuts), top_value / len(cuts))
        gain = gain * jnp.repeat(jnp.exp(draws), shape[position] // parts).reshape((-1,) + (1,) * (len(shape) - 1 - position))
    return gain


def gaussian_with(stream_key, shape, width, limit, cuts, heavy, kind=jnp.bfloat16):
    entries = width * jax.random.normal(stream_key, shape, jnp.float32)
    if cuts:
        entries = entries * levels(stream_key, shape, cuts, -0.22, 0.18)
    return jnp.clip(strengthened(entries, jax.random.fold_in(stream_key, 3), *heavy), -limit, limit).astype(kind)


def setup_inputs(seed: int = 0) -> dict:
    splits = jax.random.split(jax.random.key(seed), 8)
    inputs = draw_inputs(jax.random.fold_in(splits[7], 71), 0)
    stale_kv = draw_stale_kv(jax.random.fold_in(splits[7], 71), 0)
    w_qkv = draw_w_qkv(jax.random.fold_in(splits[7], 71), 0)
    w_out = gaussian_with(splits[3], (HEADS * DH, D), (HEADS * DH) ** -0.5, 0.375, ((0, 2), (1, 16)), (0, 1, 16, 2.0))
    mod_table = draw_mod_table(jax.random.fold_in(splits[7], 71), 0)
    step_ids = jax.random.randint(splits[5], (STEPS,), 0, TABLE).astype(jnp.int32)
    slab_order = jax.random.permutation(splits[6], N_PATCH).astype(jnp.int32)
    return dict(inputs=inputs, stale_kv=stale_kv, w_qkv=w_qkv, w_out=w_out, mod_table=mod_table, step_ids=step_ids, slab_order=slab_order)


def angle_tables(positions, head_size):
    half_size = head_size // 2
    frequency = 10000.0 ** (-(2.0 * jnp.arange(half_size, dtype=jnp.float32)) / head_size)
    angle_grid = positions.astype(jnp.float32)[:, None] * frequency[None, :]
    return (jnp.cos(angle_grid)[:, None, :], jnp.sin(angle_grid)[:, None, :])

def rotate(values, cos_table, sin_table):
    half_size = values.shape[-1] // 2
    front_half = values[..., :half_size]
    back_half = values[..., half_size:]
    return jnp.concatenate([front_half * cos_table - back_half * sin_table, front_half * sin_table + back_half * cos_table], axis=-1)

def reference(inputs, stale_kv, w_qkv, w_out, mod_table, step_ids, slab_order):
    row_ids = jnp.arange(TOKENS, dtype=jnp.int32)
    positions = slab_order[row_ids // TOK_DEV] * TOK_DEV + row_ids % TOK_DEV
    cos_table, sin_table = angle_tables(positions, DH)
    inv_root = 1.0 / math.sqrt(DH)
    previous_k = stale_kv[0].reshape(TOKENS, HEADS, DH)
    previous_v = stale_kv[1].reshape(TOKENS, HEADS, DH)
    w_flat = w_qkv.reshape(D, 3 * HEADS * DH)
    results = []
    for step in range(STEPS):
        modulation = mod_table[step_ids[step]]
        hidden = inputs[step].astype(jnp.float32)
        row_mean = lax.optimization_barrier(jnp.sum(hidden, axis=1, keepdims=True)) / D
        row_square = lax.optimization_barrier(jnp.sum(hidden * hidden, axis=1, keepdims=True)) / D
        inv_scale = lax.rsqrt(row_square - row_mean * row_mean + 1e-06)
        normed = ((hidden - row_mean) * inv_scale * (1.0 + modulation[1]) + modulation[0]).astype(jnp.bfloat16)
        projected = jnp.dot(normed, w_flat, preferred_element_type=jnp.float32).reshape(TOKENS, 3, HEADS, DH)
        queries = rotate(projected[:, 0], cos_table, sin_table).astype(jnp.bfloat16)
        fresh_k = rotate(projected[:, 1], cos_table, sin_table).astype(jnp.bfloat16)
        fresh_v = projected[:, 2].astype(jnp.bfloat16)

        def attend_slab(slab_rank):
            offset = slab_rank * TOK_DEV
            slab_q = lax.dynamic_slice_in_dim(queries, offset, TOK_DEV, 0)
            key_rows = lax.dynamic_update_slice_in_dim(previous_k, lax.dynamic_slice_in_dim(fresh_k, offset, TOK_DEV, 0), offset, 0)
            value_rows = lax.dynamic_update_slice_in_dim(previous_v, lax.dynamic_slice_in_dim(fresh_v, offset, TOK_DEV, 0), offset, 0)
            scores = jnp.einsum('qhd,khd->hqk', slab_q.astype(jnp.float32), key_rows.astype(jnp.float32)) * inv_root
            row_max = lax.optimization_barrier(jnp.max(scores, axis=2, keepdims=True))
            weights = jnp.exp(scores - row_max)
            totals = lax.optimization_barrier(jnp.sum(weights, axis=2))
            rounded = lax.optimization_barrier(weights.astype(jnp.bfloat16))
            mixed = jnp.einsum('hqk,khd->qhd', rounded.astype(jnp.float32), value_rows.astype(jnp.float32))
            return (mixed / jnp.transpose(totals)[:, :, None]).astype(jnp.bfloat16)
        attended = lax.map(attend_slab, jnp.arange(N_PATCH, dtype=jnp.int32)).reshape(TOKENS, HEADS * DH)
        projected_out = jnp.dot(attended, w_out, preferred_element_type=jnp.float32)
        results.append((modulation[2] * projected_out).astype(jnp.bfloat16))
        previous_k, previous_v = (fresh_k, fresh_v)
    return jnp.stack(results)
```

```python
import functools
import math

import jax
import jax.numpy as jnp
from jax import lax
from jax.experimental import pallas as pl
from jax.experimental.pallas import tpu as pltpu
from jax.sharding import PartitionSpec as P

DH = 128
STEPS = 2
PLANE = 4
VMEM_KERNEL = 16 * 1024 * 1024
VMEM = pl.BlockSpec(memory_space=pltpu.VMEM)
SMEM = pl.BlockSpec(memory_space=pltpu.SMEM)


def angle_tables(positions):
    half = DH // 2
    frequency = 10000.0 ** (-(2.0 * jnp.arange(half, dtype=jnp.float32)) / DH)
    grid = positions.astype(jnp.float32)[:, None] * frequency[None, :]
    cos, sin = jnp.cos(grid), jnp.sin(grid)
    return jnp.concatenate([cos, cos], axis=1), jnp.concatenate([-sin, sin], axis=1)


def swap(values, axis, count, bit):
    return lax.ppermute(values, axis, [(i, i ^ bit) for i in range(count)])


def qkv_kernel(n_head, ids, head, *refs):
    x_refs, mod_refs = refs[:n_head], refs[n_head : 2 * n_head]
    w_ref, cos_ref, sin_ref, q_ref, kv0_ref, kv1_ref, a_ref = refs[2 * n_head :]
    rows, feats = x_refs[0].shape[1:]
    width = n_head * feats
    cols = w_ref.shape[2]
    for step in range(STEPS):
        total, square = 0.0, 0.0
        for x_ref in x_refs:
            hidden = x_ref[step].astype(jnp.float32)
            total += jnp.sum(hidden, axis=1, keepdims=True)
            square += jnp.sum(hidden * hidden, axis=1, keepdims=True)
        mean = total / width
        inv = lax.rsqrt(square / width - mean * mean + 1e-06)
        for part in range(n_head):
            shift = mod_refs[part][0, pl.ds(ids[step], 1), :]
            scale = mod_refs[part][1, pl.ds(ids[step], 1), :]
            hidden = x_refs[part][step].astype(jnp.float32)
            a = (hidden - mean) * inv * (1.0 + scale) + shift
            a_ref[part, step * rows : (step + 1) * rows, :] = a.astype(jnp.bfloat16)
    cos, sin = cos_ref[...], sin_ref[...]
    for slot in range(3):
        total = jnp.zeros((STEPS * rows, cols), jnp.float32)
        for part in range(n_head):
            start = pl.multiple_of((head[0] ^ part) * feats, feats)
            total += jnp.dot(
                a_ref[part], w_ref[slot, pl.ds(start, feats), :], preferred_element_type=jnp.float32
            )
        for step in range(STEPS):
            for block in range(cols // DH):
                lanes = slice(block * DH, (block + 1) * DH)
                u = total[step * rows : (step + 1) * rows, lanes]
                if slot < 2:
                    u = u * cos + pltpu.roll(u, DH // 2, 1) * sin
                u = u.astype(jnp.bfloat16)
                if slot == 0:
                    q_ref[step, :, lanes] = u
                else:
                    (kv0_ref, kv1_ref)[step][slot - 1, :, lanes] = u


def attend_kernel(step, q_ref, own_ref, *refs):
    quad_refs, o_ref = refs[:-1], refs[-1]
    cols = q_ref.shape[2]
    for block in range(cols // DH):
        lanes = slice(block * DH, (block + 1) * DH)

        def rows_of(kind):
            pieces = [own_ref[kind, :, lanes]]
            for number, ref in enumerate(quad_refs):
                for place in range(1 if number == 0 else 0, ref.shape[0]):
                    pieces.append(ref[place, kind, :, lanes])
            return jnp.concatenate(pieces, axis=0)

        scores = lax.dot_general(
            q_ref[step, :, lanes],
            rows_of(0),
            (((1,), (1,)), ((), ())),
            preferred_element_type=jnp.float32,
        ) * (1.0 / math.sqrt(DH))
        weights = jnp.exp(scores - jnp.max(scores, axis=1, keepdims=True))
        totals = jnp.sum(weights, axis=1, keepdims=True)
        mixed = jnp.dot(
            weights.astype(jnp.bfloat16), rows_of(1), preferred_element_type=jnp.float32
        )
        o_ref[:, lanes] = (mixed / totals).astype(jnp.bfloat16)


def out_kernel(n_head, ids, patch, head, *refs):
    o_refs = refs[: STEPS * n_head]
    mod_ref = refs[STEPS * n_head]
    quad_refs = refs[STEPS * n_head + 1 : -3]
    out_ref, o_all, sums = refs[-3:]
    rows = o_refs[0].shape[0]
    high = quad_refs[0].shape[0]
    piece = quad_refs[0].shape[1]
    n_patch = high * len(quad_refs)
    blocks = n_patch // n_head
    for part in range(n_head):
        for step in range(STEPS):
            o_all[head[0] ^ part, step * rows : (step + 1) * rows, :] = o_refs[
                part * STEPS + step
            ][...]
    for low in range(blocks):
        total = 0.0
        for part in range(n_head):
            number = part * blocks + low
            source = patch[0] ^ number
            w = quad_refs[number % len(quad_refs)][number // len(quad_refs)]
            total += lax.dot_general(
                o_all[source // blocks], w, (((1,), (1,)), ((), ())), preferred_element_type=jnp.float32
            )
        sums[(patch[0] ^ low) % blocks] = total
    for step in range(STEPS):
        gate = mod_ref[2, pl.ds(ids[step], 1), :]
        out = jnp.concatenate(
            [sums[c, step * rows : (step + 1) * rows, :] for c in range(blocks)], axis=1
        )
        out_ref[step] = (gate * out).astype(jnp.bfloat16)


def call(kernel, shapes, n_smem, n_vmem, scratch=(), flops=0, size=0):
    return pl.pallas_call(
        kernel,
        out_shape=shapes,
        in_specs=[SMEM] * n_smem + [VMEM] * n_vmem,
        out_specs=jax.tree.map(lambda _: VMEM, shapes),
        scratch_shapes=scratch,
        compiler_params=pltpu.CompilerParams(vmem_limit_bytes=VMEM_KERNEL),
        cost_estimate=pl.CostEstimate(flops=flops, bytes_accessed=size, transcendentals=0),
    )


def body(n_patch, n_head, inputs, stale_kv, w_qkv, w_out, mod_table, step_ids, slab_order):
    rows, feats = inputs.shape[1:]
    cols = w_qkv.shape[2]
    patch = lax.axis_index("patch").astype(jnp.int32)[None]
    head = lax.axis_index("head").astype(jnp.int32)[None]
    bf16 = jnp.bfloat16

    def gather(own):
        quad = jnp.stack(
            [own] + [swap(own, "patch", n_patch, PLANE * k) for k in range(1, n_patch // PLANE)]
        )
        return [quad] + [swap(quad, "patch", n_patch, k) for k in range(1, PLANE)]

    x_parts = [inputs] + [swap(inputs, "head", n_head, k) for k in range(1, n_head)]
    mod_parts = [mod_table] + [swap(mod_table, "head", n_head, k) for k in range(1, n_head)]
    mod_parts = [jnp.transpose(part, (1, 0, 2)) for part in mod_parts]
    stale = gather(stale_kv)
    blocks = n_patch // n_head
    turned = lax.ppermute(
        w_out.T,
        ("patch", "head"),
        [
            ((hi * blocks + lo) * n_head + h, (h * blocks + lo) * n_head + hi)
            for hi in range(n_head)
            for lo in range(blocks)
            for h in range(n_head)
        ],
    )
    w_quads = gather(turned)

    positions = slab_order[0] * rows + jnp.arange(rows, dtype=jnp.int32)
    cos, sin = angle_tables(positions)
    kv_shape = jax.ShapeDtypeStruct((2, rows, cols), bf16)
    q, kv0, kv1 = call(
        functools.partial(qkv_kernel, n_head),
        (jax.ShapeDtypeStruct((STEPS, rows, cols), bf16), kv_shape, kv_shape),
        2,
        2 * n_head + 3,
        [pltpu.VMEM((n_head, STEPS * rows, feats), bf16)],
        2 * STEPS * rows * w_qkv.size,
        2 * w_qkv.size,
    )(step_ids, head, *x_parts, *mod_parts, jnp.transpose(w_qkv, (1, 0, 2)), cos, sin)
    o_shape = jax.ShapeDtypeStruct((rows, cols), bf16)

    def attend(step, own, quads):
        size = n_patch * rows * cols
        return call(
            functools.partial(attend_kernel, step), o_shape, 0, 2 + len(quads), (), 4 * rows * size, 4 * size
        )(q, own, *quads)

    fresh = gather(kv0)
    o0 = attend(0, kv0, stale)
    o1 = attend(1, kv1, fresh)
    o_parts = [o0, o1]
    for k in range(1, n_head):
        o_parts += [swap(o0, "head", n_head, k), swap(o1, "head", n_head, k)]
    piece = w_out.shape[1]
    return call(
        functools.partial(out_kernel, n_head),
        jax.ShapeDtypeStruct((STEPS, rows, feats), bf16),
        3,
        STEPS * n_head + 1 + PLANE,
        [
            pltpu.VMEM((n_head, STEPS * rows, cols), bf16),
            pltpu.VMEM((blocks, STEPS * rows, piece), jnp.float32),
        ],
        2 * STEPS * rows * n_patch * w_out.size,
        2 * n_patch * w_out.size,
    )(step_ids, patch, head, *o_parts, mod_parts[0], *w_quads)


def solution(mesh):
    in_specs = (
        P(None, "patch", "head"),
        P(None, "patch", "head"),
        P(None, None, "head"),
        P("head", "patch"),
        P(None, None, "head"),
        P(),
        P("patch"),
    )
    run = functools.partial(body, mesh.shape["patch"], mesh.shape["head"])
    return jax.shard_map(
        run, mesh=mesh, in_specs=in_specs, out_specs=P(None, "patch", "head"), check_vma=False
    )
```

```python
import functools
import math

import jax
import jax.numpy as jnp
from jax import lax
from jax.experimental import pallas as pl
from jax.experimental.pallas import tpu as pltpu
from jax.sharding import PartitionSpec as P

DH = 128
STEPS = 2
PLANE = 4
MIB = 1024 * 1024
VMEM = pl.BlockSpec(memory_space=pltpu.VMEM)
SMEM = pl.BlockSpec(memory_space=pltpu.SMEM)
ANY = pl.BlockSpec(memory_space=pl.ANY)
BF16, F32 = jnp.bfloat16, jnp.float32
NT = (((1,), (1,)), ((), ()))


def angle_tables(positions):
    half = DH // 2
    frequency = 10000.0 ** (-(2.0 * jnp.arange(half, dtype=F32)) / DH)
    grid = positions.astype(F32)[:, None] * frequency[None, :]
    cos, sin = jnp.cos(grid), jnp.sin(grid)
    return jnp.concatenate([cos, cos], axis=1), jnp.concatenate([-sin, sin], axis=1)


def swap(values, axis, count, bit):
    return lax.ppermute(values, axis, [(i, i ^ bit) for i in range(count)])


def load_kernel(*refs):
    count = len(refs) // 2
    sems = refs[-1]
    copies = [
        pltpu.make_async_copy(refs[i], refs[count + i], sems.at[i]) for i in range(count)
    ]
    for copy in copies:
        copy.start()
    for copy in copies:
        copy.wait()


def qkv_kernel(n_head, ids, head, *refs):
    x_refs, mod_refs = refs[:n_head], refs[n_head : 2 * n_head]
    w_ref, cos_ref, sin_ref, q_ref, kv0_ref, kv1_ref, a_ref = refs[2 * n_head :]
    rows, feats = x_refs[0].shape[1:]
    width = n_head * feats
    cols = w_ref.shape[2]
    for step in range(STEPS):
        total, square = 0.0, 0.0
        for x_ref in x_refs:
            hidden = x_ref[step].astype(F32)
            total += jnp.sum(hidden, axis=1, keepdims=True)
            square += jnp.sum(hidden * hidden, axis=1, keepdims=True)
        mean = total / width
        inv = lax.rsqrt(square / width - mean * mean + 1e-06)
        for part in range(n_head):
            shift = mod_refs[part][0, pl.ds(ids[step], 1), :]
            scale = mod_refs[part][1, pl.ds(ids[step], 1), :]
            hidden = x_refs[part][step].astype(F32)
            a = (hidden - mean) * inv * (1.0 + scale) + shift
            a_ref[part, step * rows : (step + 1) * rows, :] = a.astype(BF16)
    cos, sin = cos_ref[...], sin_ref[...]
    for slot in range(3):
        total = jnp.zeros((STEPS * rows, cols), F32)
        for part in range(n_head):
            start = pl.multiple_of((head[0] ^ part) * feats, feats)
            total += jnp.dot(
                a_ref[part], w_ref[slot, pl.ds(start, feats), :], preferred_element_type=F32
            )
        for step in range(STEPS):
            for block in range(cols // DH):
                lanes = slice(block * DH, (block + 1) * DH)
                u = total[step * rows : (step + 1) * rows, lanes]
                if slot < 2:
                    u = u * cos + pltpu.roll(u, DH // 2, 1) * sin
                u = u.astype(BF16)
                if slot == 0:
                    q_ref[step, :, lanes] = u
                else:
                    (kv0_ref, kv1_ref)[step][slot - 1, :, lanes] = u


def split3(values):
    high = values.astype(BF16).astype(F32)
    middle = (values - high).astype(BF16).astype(F32)
    return [high, middle, values - high - middle]


def attend_kernel(line, *refs):
    q_refs, refs = refs[:PLANE], refs[PLANE:]
    kv1_ref, kv0_refs, stale_refs = refs[0], refs[1 : 1 + line], refs[1 + line : 1 + 2 * line]
    own_out, peer_outs = refs[1 + 2 * line], refs[2 + 2 * line :]
    rows, cols = q_refs[0].shape[1:]
    heads = cols // DH
    for step in range(STEPS):
        before = (stale_refs, kv0_refs)[step]
        mine = (kv0_refs[0], kv1_ref)[step]
        for own in (True, False):
            queries = q_refs[:1] if own else q_refs[1:]
            keys = (mine if own else before[0], *before[1:])
            lane = lax.broadcasted_iota(jnp.int32, (rows * len(queries), DH), 1)
            stats = jnp.zeros((rows * len(queries), DH), F32)
            mixed = []
            for block in range(heads):
                lanes = slice(block * DH, (block + 1) * DH)
                scores = lax.dot_general(
                    jnp.concatenate([ref[step, :, lanes] for ref in queries], axis=0),
                    jnp.concatenate([ref[0, :, lanes] for ref in keys], axis=0),
                    NT,
                    preferred_element_type=F32,
                ) * (1.0 / math.sqrt(DH))
                top = jnp.max(scores, axis=1, keepdims=True)
                weights = jnp.exp(scores - top)
                totals = jnp.sum(weights, axis=1, keepdims=True)
                values = jnp.concatenate([ref[1, :, lanes] for ref in keys], axis=0)
                mixed.append(
                    jnp.dot(weights.astype(BF16), values, preferred_element_type=F32) / totals
                )
                for place, piece in enumerate(split3(top) + split3(totals)):
                    stats = jnp.where(lane == block * 8 + place, piece, stats)
            packed = jnp.concatenate([*mixed, stats], axis=1)
            spot = slice(step * rows, (step + 1) * rows)
            if own:
                own_out[spot, :] = packed
            else:
                for number, ref in enumerate(peer_outs):
                    ref[spot, :] = packed[number * rows : (number + 1) * rows].astype(BF16)


def merge_kernel(*refs):
    parts, o_ref = [ref[...].astype(F32) for ref in refs[:-1]], refs[-1]
    cols = o_ref.shape[1]
    for block in range(cols // DH):
        place = cols + block * 8
        tops = [jnp.sum(p[:, place : place + 3], axis=1, keepdims=True) for p in parts]
        sums = [jnp.sum(p[:, place + 3 : place + 6], axis=1, keepdims=True) for p in parts]
        best = functools.reduce(jnp.maximum, tops)
        scales = [s * jnp.exp(t - best) for s, t in zip(sums, tops)]
        lanes = slice(block * DH, (block + 1) * DH)
        mixed = sum(s * p[:, lanes] for s, p in zip(scales, parts))
        o_ref[:, lanes] = (mixed / sum(scales)).astype(BF16)


def out_kernel(n_head, n_patch, ids, patch, head, *refs):
    o_refs, refs = refs[: 2 * n_head], refs[2 * n_head :]
    mod_ref, w_refs = refs[0], refs[1 : 1 + PLANE]
    own_out, mate_out, o_all, sums = refs[1 + PLANE :]
    rows = o_refs[0].shape[0]
    piece = w_refs[0].shape[1]
    per_head = n_patch // n_head
    for part in range(n_head):
        for mate in range(2):
            spot = slice(mate * rows, (mate + 1) * rows)
            o_all[head[0] ^ part, spot, :] = o_refs[2 * part + mate][...]
    for near in range(PLANE):
        total = jnp.zeros((2 * rows, piece), F32)
        for part in range(n_head):
            o = o_all[(patch[0] // per_head) ^ part]
            total += lax.dot_general(o, w_refs[near][part], NT, preferred_element_type=F32)
        sums[(patch[0] % PLANE) ^ near] = total
    out = jnp.concatenate([sums[c] for c in range(PLANE)], axis=1)
    second = (patch[0] // PLANE) % 2 == 1
    for step in range(STEPS):
        gate = mod_ref[2, pl.ds(ids[step], 1), :]
        gate = jnp.where(second, gate[:, PLANE * piece :], gate[:, : PLANE * piece])
        each = rows // STEPS
        for mate, ref in enumerate((own_out, mate_out)):
            start = mate * rows + step * each
            ref[step] = (gate * out[start : start + each]).astype(BF16)


def call(kernel, shapes, ins, scratch=(), flops=0, size=0, limit=16):
    return pl.pallas_call(
        kernel,
        out_shape=shapes,
        in_specs=ins,
        out_specs=jax.tree.map(lambda _: VMEM, shapes),
        scratch_shapes=scratch,
        compiler_params=pltpu.CompilerParams(vmem_limit_bytes=limit * MIB),
        cost_estimate=pl.CostEstimate(flops=flops, bytes_accessed=size, transcendentals=0),
    )


def body(n_patch, n_head, inputs, stale_kv, w_qkv, w_out, mod_table, step_ids, slab_order):
    rows, feats = inputs.shape[1:]
    cols = w_qkv.shape[2]
    piece = w_out.shape[1]
    line = n_patch // PLANE
    per_head = n_patch // n_head
    patch = lax.axis_index("patch").astype(jnp.int32)
    head = lax.axis_index("head").astype(jnp.int32)
    shaped = jax.ShapeDtypeStruct

    x_parts = [swap(inputs, "head", n_head, k) for k in range(1, n_head)]
    mod_parts = [swap(mod_table, "head", n_head, k) for k in range(1, n_head)]
    first = (jnp.transpose(w_qkv, (1, 0, 2)), inputs, mod_table, stale_kv, w_out.T)
    w, x_own, mod_own, stale, w_mine = call(
        load_kernel,
        tuple(shaped(v.shape, v.dtype) for v in first),
        [ANY] * len(first),
        [pltpu.SemaphoreType.DMA((len(first),))],
        size=2 * w_qkv.size,
        limit=50,
    )(*first)
    x_parts = [x_own] + x_parts
    mod_parts = [jnp.transpose(part, (1, 0, 2)) for part in [mod_own] + mod_parts]

    stale_line = [stale] + [swap(stale, "patch", n_patch, PLANE * k) for k in range(1, line)]
    w_quad = jnp.stack(
        [
            lax.ppermute(
                w_mine,
                ("patch", "head"),
                [
                    ((hi * per_head + lo) * n_head + h, ((h ^ k) * per_head + lo) * n_head + hi)
                    for hi in range(n_head)
                    for lo in range(per_head)
                    for h in range(n_head)
                ],
            )
            for k in range(n_head)
        ]
    )
    w_quads = [w_quad] + [swap(w_quad, "patch", n_patch, k) for k in range(1, PLANE)]

    positions = slab_order[0] * rows + jnp.arange(rows, dtype=jnp.int32)
    cos, sin = angle_tables(positions)
    kv_shape = shaped((2, rows, cols), BF16)
    q, kv0, kv1 = call(
        functools.partial(qkv_kernel, n_head),
        (shaped((STEPS, rows, cols), BF16), kv_shape, kv_shape),
        [SMEM] * 2 + [VMEM] * (2 * n_head + 3),
        [pltpu.VMEM((n_head, STEPS * rows, feats), BF16)],
        2 * STEPS * rows * w_qkv.size,
        2 * w_qkv.size,
    )(step_ids, head[None], *x_parts, *mod_parts, w, cos, sin)

    kv0_line = [kv0] + [swap(kv0, "patch", n_patch, PLANE * k) for k in range(1, line)]
    q_plane = [q] + [swap(q, "patch", n_patch, k) for k in range(1, PLANE)]
    packed = (STEPS * rows, cols + DH)
    own, *peers = call(
        functools.partial(attend_kernel, line),
        (shaped(packed, F32),) + (shaped(packed, BF16),) * (PLANE - 1),
        [VMEM] * (PLANE + 1 + 2 * line),
        flops=8 * STEPS * rows * n_patch * rows * cols,
    )(*q_plane, kv1, *kv0_line, *stale_line)
    peers = [swap(peer, "patch", n_patch, k + 1) for k, peer in enumerate(peers)]
    o = call(merge_kernel, shaped((STEPS * rows, cols), BF16), [VMEM] * PLANE)(own, *peers)

    o_parts = []
    for k in range(n_head):
        for mate in range(2):
            pairs = [
                (p * n_head + h, (p ^ (PLANE * mate)) * n_head + (h ^ k))
                for p in range(n_patch)
                for h in range(n_head)
            ]
            o_parts.append(lax.ppermute(o, ("patch", "head"), pairs) if k or mate else o)
    half = shaped((STEPS, rows, PLANE * piece), BF16)
    out_own, out_mate = call(
        functools.partial(out_kernel, n_head, n_patch),
        (half, half),
        [SMEM] * 3 + [VMEM] * (2 * n_head + 1 + PLANE),
        [
            pltpu.VMEM((n_head, 2 * STEPS * rows, cols), BF16),
            pltpu.VMEM((PLANE, 2 * STEPS * rows, piece), F32),
        ],
        2 * STEPS * rows * n_patch * w_out.size,
        n_patch * w_out.size,
    )(step_ids, patch[None], head[None], *o_parts, mod_parts[0], *w_quads)
    out_back = swap(out_mate, "patch", n_patch, PLANE)
    second = (patch // PLANE) % 2 == 1
    return jnp.concatenate(
        [jnp.where(second, out_back, out_own), jnp.where(second, out_own, out_back)], axis=2
    )


def solution(mesh):
    in_specs = (
        P(None, "patch", "head"),
        P(None, "patch", "head"),
        P(None, None, "head"),
        P("head", "patch"),
        P(None, None, "head"),
        P(),
        P("patch"),
    )
    run = functools.partial(body, mesh.shape["patch"], mesh.shape["head"])
    return jax.shard_map(
        run, mesh=mesh, in_specs=in_specs, out_specs=P(None, "patch", "head"), check_vma=False
    )
```

```python
import functools
import math

import jax
import jax.numpy as jnp
from jax import lax
from jax.experimental import pallas as pl
from jax.experimental.pallas import tpu as pltpu
from jax.sharding import PartitionSpec as P

DH = 128
STEPS = 2
PLANE = 4
MIB = 1024 * 1024
VMEM = pl.BlockSpec(memory_space=pltpu.VMEM)
SMEM = pl.BlockSpec(memory_space=pltpu.SMEM)
ANY = pl.BlockSpec(memory_space=pl.ANY)
BF16, F32 = jnp.bfloat16, jnp.float32
NT = (((1,), (1,)), ((), ()))


def angle_tables(positions):
    half = DH // 2
    frequency = 10000.0 ** (-(2.0 * jnp.arange(half, dtype=F32)) / DH)
    grid = positions.astype(F32)[:, None] * frequency[None, :]
    cos, sin = jnp.cos(grid), jnp.sin(grid)
    return jnp.concatenate([cos, cos], axis=1), jnp.concatenate([-sin, sin], axis=1)


def swap(values, axis, count, bit):
    return lax.ppermute(values, axis, [(i, i ^ bit) for i in range(count)])


def load_kernel(*refs):
    count = len(refs) // 2
    sems = refs[-1]
    copies = [
        pltpu.make_async_copy(refs[i], refs[count + i], sems.at[i]) for i in range(count)
    ]
    for copy in copies:
        copy.start()
    for copy in copies:
        copy.wait()


def qkv_kernel(n_head, head, ids_ref, *refs):
    x_refs, mod_refs = refs[:n_head], refs[n_head : 2 * n_head]
    w_ref, cos_ref, sin_ref, q_ref, kv0_ref, kv1_ref, a_ref, ids, sem = refs[2 * n_head :]
    copy = pltpu.make_async_copy(ids_ref, ids, sem)
    copy.start()
    rows, feats = x_refs[0].shape[1:]
    width = n_head * feats
    cols = w_ref.shape[2]
    stats = []
    for step in range(STEPS):
        total, square = 0.0, 0.0
        for x_ref in x_refs:
            hidden = x_ref[step].astype(F32)
            total += jnp.sum(hidden, axis=1, keepdims=True)
            square += jnp.sum(hidden * hidden, axis=1, keepdims=True)
        mean = total / width
        stats.append((mean, lax.rsqrt(square / width - mean * mean + 1e-06)))
    copy.wait()
    for step in range(STEPS):
        mean, inv = stats[step]
        for part in range(n_head):
            shift = mod_refs[part][0, pl.ds(ids[step], 1), :]
            scale = mod_refs[part][1, pl.ds(ids[step], 1), :]
            hidden = x_refs[part][step].astype(F32)
            a = (hidden - mean) * inv * (1.0 + scale) + shift
            a_ref[part, step * rows : (step + 1) * rows, :] = a.astype(BF16)
    cos, sin = cos_ref[...], sin_ref[...]
    for slot in range(3):
        total = jnp.zeros((STEPS * rows, cols), F32)
        for part in range(n_head):
            start = pl.multiple_of((head[0] ^ part) * feats, feats)
            total += jnp.dot(
                a_ref[part], w_ref[slot, pl.ds(start, feats), :], preferred_element_type=F32
            )
        for step in range(STEPS):
            for block in range(cols // DH):
                lanes = slice(block * DH, (block + 1) * DH)
                u = total[step * rows : (step + 1) * rows, lanes]
                if slot < 2:
                    u = u * cos + pltpu.roll(u, DH // 2, 1) * sin
                u = u.astype(BF16)
                if slot == 0:
                    for place in range(q_ref.shape[0]):
                        q_ref[place, step, :, lanes] = u
                elif step == 0:
                    for place in range(kv0_ref.shape[0]):
                        kv0_ref[place, slot - 1, :, lanes] = u
                else:
                    kv1_ref[slot - 1, :, lanes] = u


def split3(values):
    high = values.astype(BF16).astype(F32)
    middle = (values - high).astype(BF16).astype(F32)
    return [high, middle, values - high - middle]


def attend_kernel(patch, q_ref, kv1_ref, kv0_sent, kv0_ref, stale_ref, out_ref):
    line = kv0_ref.shape[0]
    rows, cols = q_ref.shape[2:]
    near, far = patch[0] % PLANE, patch[0] // PLANE
    shape = (PLANE * rows, line * rows + rows)
    mine = lax.broadcasted_iota(jnp.int32, shape, 0) // rows == near
    spot = lax.broadcasted_iota(jnp.int32, shape, 1) // rows
    drop = jnp.where(mine, spot, line - spot) == jnp.where(mine, far, 0)
    lane = lax.broadcasted_iota(jnp.int32, (PLANE * rows, DH), 1)
    for step in range(STEPS):
        before = (stale_ref, kv0_ref)[step]
        fresh = (kv0_sent.at[0], kv1_ref)[step]
        stats = jnp.zeros((PLANE * rows, DH), F32)
        mixed = []
        for block in range(cols // DH):
            lanes = slice(block * DH, (block + 1) * DH)

            def rows_of(kind):
                old = before[:, kind, :, lanes].reshape(line * rows, DH)
                return jnp.concatenate([old, fresh[kind, :, lanes]], axis=0)

            queries = q_ref[:, step, :, lanes].reshape(PLANE * rows, DH)
            scores = lax.dot_general(queries, rows_of(0), NT, preferred_element_type=F32)
            scores = jnp.where(drop, -1e30, scores * (1.0 / math.sqrt(DH)))
            top = jnp.max(scores, axis=1, keepdims=True)
            weights = jnp.exp(scores - top)
            totals = jnp.sum(weights, axis=1, keepdims=True)
            mixed.append(
                jnp.dot(weights.astype(BF16), rows_of(1), preferred_element_type=F32) / totals
            )
            for place, piece in enumerate(split3(top) + split3(totals)):
                stats = jnp.where(lane == block * 8 + place, piece, stats)
        packed = jnp.concatenate([*mixed, stats], axis=1).astype(BF16)
        out_ref[:, step * rows : (step + 1) * rows, :] = packed.reshape(PLANE, rows, cols + DH)


def merge_kernel(parts_ref, o_ref):
    parts = [parts_ref[k].astype(F32) for k in range(PLANE)]
    cols = o_ref.shape[1]
    for block in range(cols // DH):
        place = cols + block * 8
        tops = [jnp.sum(p[:, place : place + 3], axis=1, keepdims=True) for p in parts]
        sums = [jnp.sum(p[:, place + 3 : place + 6], axis=1, keepdims=True) for p in parts]
        best = functools.reduce(jnp.maximum, tops)
        scales = [s * jnp.exp(t - best) for s, t in zip(sums, tops)]
        lanes = slice(block * DH, (block + 1) * DH)
        mixed = sum(s * p[:, lanes] for s, p in zip(scales, parts))
        o_ref[:, lanes] = (mixed / sum(scales)).astype(BF16)


def out_kernel(n_head, n_patch, ids, patch, head, *refs):
    o_refs, refs = refs[: 2 * n_head], refs[2 * n_head :]
    mod_ref, w_refs = refs[0], refs[1 : 1 + PLANE]
    own_out, mate_out, o_all, sums = refs[1 + PLANE :]
    rows = o_refs[0].shape[0]
    piece = w_refs[0].shape[1]
    per_head = n_patch // n_head
    for part in range(n_head):
        for mate in range(2):
            spot = slice(mate * rows, (mate + 1) * rows)
            o_all[head[0] ^ part, spot, :] = o_refs[2 * part + mate][...]
    for near in range(PLANE):
        total = jnp.zeros((2 * rows, piece), F32)
        for part in range(n_head):
            o = o_all[(patch[0] // per_head) ^ part]
            total += lax.dot_general(o, w_refs[near][part], NT, preferred_element_type=F32)
        sums[(patch[0] % PLANE) ^ near] = total
    out = jnp.concatenate([sums[c] for c in range(PLANE)], axis=1)
    second = (patch[0] // PLANE) % 2 == 1
    for step in range(STEPS):
        gate = mod_ref[2, pl.ds(ids[step], 1), :]
        gate = jnp.where(second, gate[:, PLANE * piece :], gate[:, : PLANE * piece])
        each = rows // STEPS
        for mate, ref in enumerate((own_out, mate_out)):
            start = mate * rows + step * each
            ref[step] = (gate * out[start : start + each]).astype(BF16)


def in_hbm(values):
    return pltpu.with_memory_space_constraint(values, pltpu.HBM)


def call(kernel, shapes, ins, scratch=(), flops=0, size=0, limit=16):
    return pl.pallas_call(
        kernel,
        out_shape=shapes,
        in_specs=ins,
        out_specs=jax.tree.map(lambda _: VMEM, shapes),
        scratch_shapes=scratch,
        compiler_params=pltpu.CompilerParams(vmem_limit_bytes=limit * MIB),
        cost_estimate=pl.CostEstimate(flops=flops, bytes_accessed=size, transcendentals=0),
    )


def body(n_patch, n_head, inputs, stale_kv, w_qkv, w_out, mod_table, step_ids, slab_order):
    rows, feats = inputs.shape[1:]
    cols = w_qkv.shape[2]
    piece = w_out.shape[1]
    line = n_patch // PLANE
    per_head = n_patch // n_head
    patch = lax.axis_index("patch").astype(jnp.int32)
    head = lax.axis_index("head").astype(jnp.int32)
    shaped = jax.ShapeDtypeStruct

    x_parts = [swap(inputs, "head", n_head, k) for k in range(1, n_head)]
    mod_parts = [swap(mod_table, "head", n_head, k) for k in range(1, n_head)]
    first = (jnp.transpose(w_qkv, (1, 0, 2)), inputs, jnp.transpose(mod_table, (1, 0, 2)))
    w, x_own, mod_own = call(
        load_kernel,
        tuple(pltpu.VMEM(v.shape, v.dtype) for v in first),
        [ANY] * len(first),
        [pltpu.SemaphoreType.DMA((len(first),))],
        size=2 * w_qkv.size,
    )(*map(in_hbm, first))
    x_parts = [x_own] + x_parts
    mod_parts = [mod_own] + [jnp.transpose(part, (1, 0, 2)) for part in mod_parts]

    lines = [[PLANE * i + j for i in range(line)] for j in range(PLANE)]
    planes = [[PLANE * i + j for j in range(PLANE)] for i in range(line)]

    def exchange(values, groups):
        return lax.all_to_all(values, "patch", 0, 0, axis_index_groups=groups)

    stale = exchange(jnp.broadcast_to(stale_kv[None], (line, *stale_kv.shape)), lines)
    w_quad = jnp.stack(
        [
            lax.ppermute(
                w_out.T,
                ("patch", "head"),
                [
                    ((hi * per_head + lo) * n_head + h, ((h ^ k) * per_head + lo) * n_head + hi)
                    for hi in range(n_head)
                    for lo in range(per_head)
                    for h in range(n_head)
                ],
            )
            for k in range(n_head)
        ]
    )
    w_quads = [w_quad] + [swap(w_quad, "patch", n_patch, k) for k in range(1, PLANE)]

    positions = slab_order[0] * rows + jnp.arange(rows, dtype=jnp.int32)
    cos, sin = angle_tables(positions)
    kv_shape = (2, rows, cols)
    q, kv0, kv1 = call(
        functools.partial(qkv_kernel, n_head),
        (shaped((PLANE, *kv_shape), BF16), shaped((line, *kv_shape), BF16), shaped(kv_shape, BF16)),
        [SMEM, ANY] + [VMEM] * (2 * n_head + 3),
        [
            pltpu.VMEM((n_head, STEPS * rows, feats), BF16),
            pltpu.SMEM(step_ids.shape, jnp.int32),
            pltpu.SemaphoreType.DMA,
        ],
        2 * STEPS * rows * w_qkv.size,
        2 * w_qkv.size,
    )(head[None], in_hbm(step_ids), *x_parts, *mod_parts, w, cos, sin)

    kv0_line = exchange(kv0, lines)
    q_plane = exchange(q, planes)
    parts = call(
        attend_kernel,
        shaped((PLANE, STEPS * rows, cols + DH), BF16),
        [SMEM] + [VMEM] * 5,
        flops=8 * STEPS * rows * n_patch * rows * cols,
    )(patch[None], q_plane, kv1, kv0, kv0_line, stale)
    parts = exchange(parts, planes)
    o = call(merge_kernel, shaped((STEPS * rows, cols), BF16), [VMEM])(parts)

    o_parts = []
    for k in range(n_head):
        for mate in range(2):
            pairs = [
                (p * n_head + h, (p ^ (PLANE * mate)) * n_head + (h ^ k))
                for p in range(n_patch)
                for h in range(n_head)
            ]
            o_parts.append(lax.ppermute(o, ("patch", "head"), pairs) if k or mate else o)
    half = shaped((STEPS, rows, PLANE * piece), BF16)
    out_own, out_mate = call(
        functools.partial(out_kernel, n_head, n_patch),
        (half, half),
        [SMEM] * 3 + [VMEM] * (2 * n_head + 1 + PLANE),
        [
            pltpu.VMEM((n_head, 2 * STEPS * rows, cols), BF16),
            pltpu.VMEM((PLANE, 2 * STEPS * rows, piece), F32),
        ],
        2 * STEPS * rows * n_patch * w_out.size,
        n_patch * w_out.size,
    )(step_ids, patch[None], head[None], *o_parts, mod_own, *w_quads)
    out_back = swap(out_mate, "patch", n_patch, PLANE)
    second = (patch // PLANE) % 2 == 1
    return jnp.concatenate(
        [jnp.where(second, out_back, out_own), jnp.where(second, out_own, out_back)], axis=2
    )


def solution(mesh):
    in_specs = (
        P(None, "patch", "head"),
        P(None, "patch", "head"),
        P(None, None, "head"),
        P("head", "patch"),
        P(None, None, "head"),
        P(),
        P("patch"),
    )
    run = functools.partial(body, mesh.shape["patch"], mesh.shape["head"])
    return jax.shard_map(
        run, mesh=mesh, in_specs=in_specs, out_specs=P(None, "patch", "head"), check_vma=False
    )
```

```python
import functools
import math

import jax
import jax.numpy as jnp
from jax import lax
from jax.experimental import pallas as pl
from jax.experimental.pallas import tpu as pltpu
from jax.sharding import PartitionSpec as P

DH = 128
STEPS = 2
PLANE = 4
MIB = 1024 * 1024
VMEM = pl.BlockSpec(memory_space=pltpu.VMEM)
SMEM = pl.BlockSpec(memory_space=pltpu.SMEM)
ANY = pl.BlockSpec(memory_space=pl.ANY)
BF16, F32 = jnp.bfloat16, jnp.float32
NT = (((1,), (1,)), ((), ()))


def angle_tables(positions):
    half = DH // 2
    frequency = 10000.0 ** (-(2.0 * jnp.arange(half, dtype=F32)) / DH)
    grid = positions.astype(F32)[:, None] * frequency[None, :]
    cos, sin = jnp.cos(grid), jnp.sin(grid)
    return jnp.concatenate([cos, cos], axis=1), jnp.concatenate([-sin, sin], axis=1)


def swap(values, axis, count, bit):
    return lax.ppermute(values, axis, [(i, i ^ bit) for i in range(count)])


def load_kernel(ids, *refs):
    count = len(refs) // 2 - 1
    ids_out, sems = refs[-2:]
    copies = [
        pltpu.make_async_copy(refs[i], refs[count + i], sems.at[i]) for i in range(count)
    ]
    for copy in copies:
        copy.start()
    row = lax.broadcasted_iota(jnp.int32, ids_out.shape, 0)
    tile = jnp.zeros(ids_out.shape, jnp.int32)
    for step in range(STEPS):
        tile = jnp.where(row == step, ids[step], tile)
    ids_out[...] = tile
    for copy in copies:
        copy.wait()


def table_row(mod_ref, kind, ids_ref, step):
    chosen = ids_ref[step : step + 1, :1]
    table = mod_ref[kind]
    return sum(
        jnp.where(chosen == r, table[r : r + 1], 0.0) for r in range(table.shape[0])
    )


def qkv_kernel(n_head, head, ids_ref, *refs):
    x_refs, mod_refs = refs[:n_head], refs[n_head : 2 * n_head]
    w_ref, cos_ref, sin_ref = refs[2 * n_head : 2 * n_head + 3]
    q_ref, kv0_ref, kv1_ref, a_ref = refs[-4:]
    rows, feats = x_refs[0].shape[1:]
    width = n_head * feats
    cols = w_ref.shape[2]
    for step in range(STEPS):
        total, square = 0.0, 0.0
        for x_ref in x_refs:
            hidden = x_ref[step].astype(F32)
            total += jnp.sum(hidden, axis=1, keepdims=True)
            square += jnp.sum(hidden * hidden, axis=1, keepdims=True)
        mean = total / width
        inv = lax.rsqrt(square / width - mean * mean + 1e-06)
        for part in range(n_head):
            shift = table_row(mod_refs[part], 0, ids_ref, step)
            scale = table_row(mod_refs[part], 1, ids_ref, step)
            hidden = x_refs[part][step].astype(F32)
            a = (hidden - mean) * inv * (1.0 + scale) + shift
            a_ref[part, step * rows : (step + 1) * rows, :] = a.astype(BF16)
    cos, sin = cos_ref[...], sin_ref[...]
    for slot in range(3):
        total = jnp.zeros((STEPS * rows, cols), F32)
        for part in range(n_head):
            start = pl.multiple_of((head[0] ^ part) * feats, feats)
            total += jnp.dot(
                a_ref[part], w_ref[slot, pl.ds(start, feats), :], preferred_element_type=F32
            )
        for step in range(STEPS):
            for block in range(cols // DH):
                lanes = slice(block * DH, (block + 1) * DH)
                u = total[step * rows : (step + 1) * rows, lanes]
                if slot < 2:
                    u = u * cos + pltpu.roll(u, DH // 2, 1) * sin
                u = u.astype(BF16)
                if slot == 0:
                    q_ref[step, :, lanes] = u
                else:
                    (kv0_ref, kv1_ref)[step][slot - 1, :, lanes] = u


def split3(values):
    high = values.astype(BF16).astype(F32)
    middle = (values - high).astype(BF16).astype(F32)
    return [high, middle, values - high - middle]


def attend_kernel(line, *refs):
    q_refs, refs = refs[:line], refs[line:]
    kv1_ref, kv0_refs, stale_refs = refs[0], refs[1 : 1 + PLANE], refs[1 + PLANE : 1 + 2 * PLANE]
    outs = refs[1 + 2 * PLANE :]
    rows, cols = q_refs[0].shape[1:]
    shape = (line * rows, PLANE * rows + rows)
    stray = jnp.where(lax.broadcasted_iota(jnp.int32, shape, 0) < rows, 0, PLANE)
    drop = lax.broadcasted_iota(jnp.int32, shape, 1) // rows == stray
    lane = lax.broadcasted_iota(jnp.int32, (line * rows, DH), 1)
    for step in range(STEPS):
        keys = ((*stale_refs, kv0_refs[0]), (*kv0_refs, kv1_ref))[step]
        stats = jnp.zeros((line * rows, DH), F32)
        mixed = []
        for block in range(cols // DH):
            lanes = slice(block * DH, (block + 1) * DH)
            scores = lax.dot_general(
                jnp.concatenate([ref[step, :, lanes] for ref in q_refs], axis=0),
                jnp.concatenate([ref[0, :, lanes] for ref in keys], axis=0),
                NT,
                preferred_element_type=F32,
            )
            scores = jnp.where(drop, -1e30, scores * (1.0 / math.sqrt(DH)))
            top = jnp.max(scores, axis=1, keepdims=True)
            weights = jnp.exp(scores - top)
            totals = jnp.sum(weights, axis=1, keepdims=True)
            values = jnp.concatenate([ref[1, :, lanes] for ref in keys], axis=0)
            mixed.append(
                jnp.dot(weights.astype(BF16), values, preferred_element_type=F32) / totals
            )
            for place, piece in enumerate(split3(top) + split3(totals)):
                stats = jnp.where(lane == block * 8 + place, piece, stats)
        packed = jnp.concatenate([*mixed, stats], axis=1).astype(BF16)
        for number, ref in enumerate(outs):
            ref[step * rows : (step + 1) * rows, :] = packed[number * rows : (number + 1) * rows]


def merge_kernel(*refs):
    part_refs, o_ref = refs[:-1], refs[-1]
    cols = o_ref.shape[1]
    source = lax.broadcasted_iota(jnp.int32, (DH, DH), 0)
    for block in range(cols // DH):
        lanes = slice(block * DH, (block + 1) * DH)

        def spread(ref, first):
            pick = (source >= block * 8 + first) & (source < block * 8 + first + 3)
            return jnp.dot(ref[:, cols:], pick.astype(F32).astype(BF16), preferred_element_type=F32)

        tops = [spread(ref, 0) for ref in part_refs]
        best = functools.reduce(jnp.maximum, tops)
        scales = [spread(ref, 3) * jnp.exp(t - best) for ref, t in zip(part_refs, tops)]
        mixed = sum(s * ref[:, lanes].astype(F32) for s, ref in zip(scales, part_refs))
        o_ref[:, lanes] = (mixed / sum(scales)).astype(BF16)


def out_kernel(n_head, n_patch, patch, head, ids_ref, *refs):
    o_refs, refs = refs[: 2 * n_head], refs[2 * n_head :]
    mod_ref, w_refs = refs[0], refs[1 : 1 + PLANE]
    own_out, mate_out, o_all, sums = refs[1 + PLANE :]
    rows = o_refs[0].shape[0]
    piece = w_refs[0].shape[1]
    per_head = n_patch // n_head
    for part in range(n_head):
        for mate in range(2):
            spot = slice(mate * rows, (mate + 1) * rows)
            o_all[head[0] ^ part, spot, :] = o_refs[2 * part + mate][...]
    for near in range(PLANE):
        total = jnp.zeros((2 * rows, piece), F32)
        for part in range(n_head):
            o = o_all[(patch[0] // per_head) ^ part]
            total += lax.dot_general(o, w_refs[near][part], NT, preferred_element_type=F32)
        sums[(patch[0] % PLANE) ^ near] = total
    out = jnp.concatenate([sums[c] for c in range(PLANE)], axis=1)
    second = (patch[0] // PLANE) % 2 == 1
    for step in range(STEPS):
        gate = table_row(mod_ref, 2, ids_ref, step)
        gate = jnp.where(second, gate[:, PLANE * piece :], gate[:, : PLANE * piece])
        each = rows // STEPS
        for mate, ref in enumerate((own_out, mate_out)):
            start = mate * rows + step * each
            ref[step] = (gate * out[start : start + each]).astype(BF16)


def in_hbm(values):
    return pltpu.with_memory_space_constraint(values, pltpu.HBM)


def call(kernel, shapes, ins, scratch=(), flops=0, size=0, limit=16):
    return pl.pallas_call(
        kernel,
        out_shape=shapes,
        in_specs=ins,
        out_specs=jax.tree.map(lambda _: VMEM, shapes),
        scratch_shapes=scratch,
        compiler_params=pltpu.CompilerParams(vmem_limit_bytes=limit * MIB),
        cost_estimate=pl.CostEstimate(flops=flops, bytes_accessed=size, transcendentals=0),
    )


def body(n_patch, n_head, inputs, stale_kv, w_qkv, w_out, mod_table, step_ids, slab_order):
    rows, feats = inputs.shape[1:]
    cols = w_qkv.shape[2]
    piece = w_out.shape[1]
    line = n_patch // PLANE
    per_head = n_patch // n_head
    patch = lax.axis_index("patch").astype(jnp.int32)
    head = lax.axis_index("head").astype(jnp.int32)
    shaped = jax.ShapeDtypeStruct

    x_parts = [swap(inputs, "head", n_head, k) for k in range(1, n_head)]
    mod_parts = [swap(mod_table, "head", n_head, k) for k in range(1, n_head)]
    first = (jnp.transpose(w_qkv, (1, 0, 2)), inputs, jnp.transpose(mod_table, (1, 0, 2)))
    w, x_own, mod_own, ids = call(
        load_kernel,
        tuple(pltpu.VMEM(v.shape, v.dtype) for v in first) + (shaped((8, DH), jnp.int32),),
        [SMEM] + [ANY] * len(first),
        [pltpu.SemaphoreType.DMA((len(first),))],
        size=2 * w_qkv.size,
    )(*map(in_hbm, (step_ids, *first)))
    x_parts = [x_own] + x_parts
    mod_parts = [mod_own] + [jnp.transpose(part, (1, 0, 2)) for part in mod_parts]

    def plane_of(values):
        return [values] + [swap(values, "patch", n_patch, k) for k in range(1, PLANE)]

    def line_of(values):
        return [values] + [swap(values, "patch", n_patch, PLANE * k) for k in range(1, line)]

    stale_plane = plane_of(stale_kv)
    w_quad = jnp.stack(
        [
            lax.ppermute(
                w_out.T,
                ("patch", "head"),
                [
                    ((hi * per_head + lo) * n_head + h, ((h ^ k) * per_head + lo) * n_head + hi)
                    for hi in range(n_head)
                    for lo in range(per_head)
                    for h in range(n_head)
                ],
            )
            for k in range(n_head)
        ]
    )
    w_quads = plane_of(w_quad)

    positions = slab_order[0] * rows + jnp.arange(rows, dtype=jnp.int32)
    cos, sin = angle_tables(positions)
    kv_shape = shaped((2, rows, cols), BF16)
    q, kv0, kv1 = call(
        functools.partial(qkv_kernel, n_head),
        (kv_shape,) * 3,
        [SMEM] + [VMEM] * (2 * n_head + 4) + [ANY] * PLANE,
        [pltpu.VMEM((n_head, STEPS * rows, feats), BF16)],
        2 * STEPS * rows * w_qkv.size,
        2 * w_qkv.size,
    )(head[None], ids, *x_parts, *mod_parts, w, cos, sin, w_quad, *stale_plane[1:])

    kv0_plane = plane_of(kv0)
    parts = call(
        functools.partial(attend_kernel, line),
        (shaped((STEPS * rows, cols + DH), BF16),) * line,
        [VMEM] * (line + 1 + 2 * PLANE),
        flops=8 * STEPS * rows * n_patch * rows * cols,
    )(*line_of(q), kv1, *kv0_plane, *stale_plane)
    parts = [
        swap(part, "patch", n_patch, PLANE * k) if k else part for k, part in enumerate(parts)
    ]
    o = call(merge_kernel, shaped((STEPS * rows, cols), BF16), [VMEM] * line)(*parts)

    o_parts = []
    for k in range(n_head):
        for mate in range(2):
            pairs = [
                (p * n_head + h, (p ^ (PLANE * mate)) * n_head + (h ^ k))
                for p in range(n_patch)
                for h in range(n_head)
            ]
            o_parts.append(lax.ppermute(o, ("patch", "head"), pairs) if k or mate else o)
    half = shaped((STEPS, rows, PLANE * piece), BF16)
    out_own, out_mate = call(
        functools.partial(out_kernel, n_head, n_patch),
        (half, half),
        [SMEM] * 2 + [VMEM] * (2 * n_head + 2 + PLANE),
        [
            pltpu.VMEM((n_head, 2 * STEPS * rows, cols), BF16),
            pltpu.VMEM((PLANE, 2 * STEPS * rows, piece), F32),
        ],
        2 * STEPS * rows * n_patch * w_out.size,
        n_patch * w_out.size,
    )(patch[None], head[None], ids, *o_parts, mod_own, *w_quads)
    out_back = swap(out_mate, "patch", n_patch, PLANE)
    second = (patch // PLANE) % 2 == 1
    return jnp.concatenate(
        [jnp.where(second, out_back, out_own), jnp.where(second, out_own, out_back)], axis=2
    )


def solution(mesh):
    in_specs = (
        P(None, "patch", "head"),
        P(None, "patch", "head"),
        P(None, None, "head"),
        P("head", "patch"),
        P(None, None, "head"),
        P(),
        P("patch"),
    )
    run = functools.partial(body, mesh.shape["patch"], mesh.shape["head"])
    return jax.shard_map(
        run, mesh=mesh, in_specs=in_specs, out_specs=P(None, "patch", "head"), check_vma=False
    )
```

```python
import functools
import math

import jax
import jax.numpy as jnp
from jax import lax
from jax.experimental import pallas as pl
from jax.experimental.pallas import tpu as pltpu
from jax.sharding import PartitionSpec as P

DH = 128
STEPS = 2
PLANE = 4
MIB = 1024 * 1024
VMEM = pl.BlockSpec(memory_space=pltpu.VMEM)
SMEM = pl.BlockSpec(memory_space=pltpu.SMEM)
ANY = pl.BlockSpec(memory_space=pl.ANY)
BF16, F32 = jnp.bfloat16, jnp.float32
NT = (((1,), (1,)), ((), ()))


def angle_tables(positions):
    half = DH // 2
    frequency = 10000.0 ** (-(2.0 * jnp.arange(half, dtype=F32)) / DH)
    grid = positions.astype(F32)[:, None] * frequency[None, :]
    cos, sin = jnp.cos(grid), jnp.sin(grid)
    return jnp.concatenate([cos, cos], axis=1), jnp.concatenate([-sin, sin], axis=1)


def swap(values, axis, count, bit):
    return lax.ppermute(values, axis, [(i, i ^ bit) for i in range(count)])


def load_kernel(ids, *refs):
    count = len(refs) // 2 - 1
    ids_out, sems = refs[-2:]
    copies = [
        pltpu.make_async_copy(refs[i], refs[count + i], sems.at[i]) for i in range(count)
    ]
    for copy in copies:
        copy.start()
    row = lax.broadcasted_iota(jnp.int32, ids_out.shape, 0)
    tile = jnp.zeros(ids_out.shape, jnp.int32)
    for step in range(STEPS):
        tile = jnp.where(row == step, ids[step], tile)
    ids_out[...] = tile
    for copy in copies:
        copy.wait()


def table_row(mod_ref, kind, ids_ref, step):
    chosen = ids_ref[step : step + 1, :1]
    table = mod_ref[kind]
    return sum(
        jnp.where(chosen == r, table[r : r + 1], 0.0) for r in range(table.shape[0])
    )


def qkv_kernel(n_head, head, ids_ref, *refs):
    x_refs, mod_refs = refs[:n_head], refs[n_head : 2 * n_head]
    w_ref, cos_ref, sin_ref, stale_ref = refs[2 * n_head : 2 * n_head + 4]
    q_ref, kv0_ref, kv1_ref, a_ref = refs[-4:]
    rows, feats = x_refs[0].shape[1:]
    width = n_head * feats
    cols = w_ref.shape[2]
    kv0_ref[:2] = stale_ref[...]
    for step in range(STEPS):
        total, square = 0.0, 0.0
        for x_ref in x_refs:
            hidden = x_ref[step].astype(F32)
            total += jnp.sum(hidden, axis=1, keepdims=True)
            square += jnp.sum(hidden * hidden, axis=1, keepdims=True)
        mean = total / width
        inv = lax.rsqrt(square / width - mean * mean + 1e-06)
        for part in range(n_head):
            shift = table_row(mod_refs[part], 0, ids_ref, step)
            scale = table_row(mod_refs[part], 1, ids_ref, step)
            hidden = x_refs[part][step].astype(F32)
            a = (hidden - mean) * inv * (1.0 + scale) + shift
            a_ref[part, step * rows : (step + 1) * rows, :] = a.astype(BF16)
    cos, sin = cos_ref[...], sin_ref[...]
    for slot in range(3):
        total = jnp.zeros((STEPS * rows, cols), F32)
        for part in range(n_head):
            start = pl.multiple_of((head[0] ^ part) * feats, feats)
            total += jnp.dot(
                a_ref[part], w_ref[slot, pl.ds(start, feats), :], preferred_element_type=F32
            )
        for step in range(STEPS):
            for block in range(cols // DH):
                lanes = slice(block * DH, (block + 1) * DH)
                u = total[step * rows : (step + 1) * rows, lanes]
                if slot < 2:
                    u = u * cos + pltpu.roll(u, DH // 2, 1) * sin
                u = u.astype(BF16)
                if slot == 0:
                    for place in range(q_ref.shape[0]):
                        q_ref[place, step, :, lanes] = u
                elif step == 0:
                    kv0_ref[slot + 1, :, lanes] = u
                else:
                    kv1_ref[slot - 1, :, lanes] = u


def split3(values):
    high = values.astype(BF16).astype(F32)
    middle = (values - high).astype(BF16).astype(F32)
    return [high, middle, values - high - middle]


def attend_kernel(patch, q_ref, kv1_ref, *refs):
    kv_refs, out_ref = refs[:PLANE], refs[PLANE]
    line, _, rows, cols = q_ref.shape
    shape = (line * rows, PLANE * rows + rows)
    mine = lax.broadcasted_iota(jnp.int32, shape, 0) // rows == patch[0] // PLANE
    drop = lax.broadcasted_iota(jnp.int32, shape, 1) // rows == jnp.where(mine, 0, PLANE)
    lane = lax.broadcasted_iota(jnp.int32, (line * rows, DH), 1)
    for step in range(STEPS):
        fresh = (kv_refs[0].at[2:], kv1_ref)[step]
        stats = jnp.zeros((line * rows, DH), F32)
        mixed = []
        for block in range(cols // DH):
            lanes = slice(block * DH, (block + 1) * DH)

            def rows_of(kind):
                old = [ref[2 * step + kind, :, lanes] for ref in kv_refs]
                return jnp.concatenate([*old, fresh[kind, :, lanes]], axis=0)

            queries = q_ref[:, step, :, lanes].reshape(line * rows, DH)
            scores = lax.dot_general(queries, rows_of(0), NT, preferred_element_type=F32)
            scores = jnp.where(drop, -1e30, scores * (1.0 / math.sqrt(DH)))
            top = jnp.max(scores, axis=1, keepdims=True)
            weights = jnp.exp(scores - top)
            totals = jnp.sum(weights, axis=1, keepdims=True)
            mixed.append(
                jnp.dot(weights.astype(BF16), rows_of(1), preferred_element_type=F32) / totals
            )
            for place, piece in enumerate(split3(top) + split3(totals)):
                stats = jnp.where(lane == block * 8 + place, piece, stats)
        packed = jnp.concatenate([*mixed, stats], axis=1).astype(BF16)
        out_ref[:, step * rows : (step + 1) * rows, :] = packed.reshape(line, rows, cols + DH)


def merge_kernel(*refs):
    parts_ref, o_ref = refs
    part_refs = [parts_ref.at[k] for k in range(parts_ref.shape[0])]
    cols = o_ref.shape[1]
    source = lax.broadcasted_iota(jnp.int32, (DH, DH), 0)
    for block in range(cols // DH):
        lanes = slice(block * DH, (block + 1) * DH)

        def spread(ref, first):
            pick = (source >= block * 8 + first) & (source < block * 8 + first + 3)
            return jnp.dot(ref[:, cols:], pick.astype(F32).astype(BF16), preferred_element_type=F32)

        tops = [spread(ref, 0) for ref in part_refs]
        best = functools.reduce(jnp.maximum, tops)
        scales = [spread(ref, 3) * jnp.exp(t - best) for ref, t in zip(part_refs, tops)]
        mixed = sum(s * ref[:, lanes].astype(F32) for s, ref in zip(scales, part_refs))
        o_ref[:, lanes] = (mixed / sum(scales)).astype(BF16)


def project_kernel(n_head, n_patch, bit, patch, head, *refs):
    o_refs, w_refs, (out_ref, sums) = refs[:2], refs[2 : 2 + PLANE], refs[2 + PLANE :]
    rows = o_refs[0].shape[0]
    slot = head[0] ^ bit ^ (patch[0] // (n_patch // n_head))
    o = jnp.concatenate([ref[...] for ref in o_refs], axis=0)
    for near in range(PLANE):
        sums[(patch[0] % PLANE) ^ near] = lax.dot_general(
            o, w_refs[near][slot], NT, preferred_element_type=F32
        )
    out = jnp.concatenate([sums[c] for c in range(PLANE)], axis=1)
    out_ref[...] = out.astype(out_ref.dtype)


def gate_kernel(n_patch, patch, ids_ref, mod_ref, *refs):
    sum_refs, (own_out, mate_out) = refs[:-2], refs[-2:]
    total = sum(ref[...].astype(F32) for ref in sum_refs)
    rows, width = total.shape
    each = rows // 2 // STEPS
    second = (patch[0] // PLANE) % 2 == 1
    for step in range(STEPS):
        gate = table_row(mod_ref, 2, ids_ref, step)
        gate = jnp.where(second, gate[:, width:], gate[:, :width])
        for mate, ref in enumerate((own_out, mate_out)):
            start = mate * (rows // 2) + step * each
            ref[step] = (gate * total[start : start + each]).astype(BF16)


def in_hbm(values):
    return pltpu.with_memory_space_constraint(values, pltpu.HBM)


def call(kernel, shapes, ins, scratch=(), flops=0, size=0, limit=16):
    return pl.pallas_call(
        kernel,
        out_shape=shapes,
        in_specs=ins,
        out_specs=jax.tree.map(lambda _: VMEM, shapes),
        scratch_shapes=scratch,
        compiler_params=pltpu.CompilerParams(vmem_limit_bytes=limit * MIB),
        cost_estimate=pl.CostEstimate(flops=flops, bytes_accessed=size, transcendentals=0),
    )


def body(n_patch, n_head, inputs, stale_kv, w_qkv, w_out, mod_table, step_ids, slab_order):
    rows, feats = inputs.shape[1:]
    cols = w_qkv.shape[2]
    piece = w_out.shape[1]
    line = n_patch // PLANE
    patch = lax.axis_index("patch").astype(jnp.int32)
    head = lax.axis_index("head").astype(jnp.int32)
    shaped = jax.ShapeDtypeStruct

    x_parts = [swap(inputs, "head", n_head, k) for k in range(1, n_head)]
    mod_parts = [swap(mod_table, "head", n_head, k) for k in range(1, n_head)]
    first = (jnp.transpose(w_qkv, (1, 0, 2)), inputs, jnp.transpose(mod_table, (1, 0, 2)), stale_kv)
    w, x_own, mod_own, stale, ids = call(
        load_kernel,
        tuple(pltpu.VMEM(v.shape, v.dtype) for v in first) + (shaped((8, DH), jnp.int32),),
        [SMEM] + [ANY] * len(first),
        [pltpu.SemaphoreType.DMA((len(first),))],
        size=2 * w_qkv.size,
    )(*map(in_hbm, (step_ids, *first)))
    x_parts = [x_own] + x_parts
    mod_parts = [mod_own] + [jnp.transpose(part, (1, 0, 2)) for part in mod_parts]

    def plane_of(values):
        return [values] + [swap(values, "patch", n_patch, k) for k in range(1, PLANE)]

    lines = [[PLANE * i + j for i in range(line)] for j in range(PLANE)]

    def trade(values):
        return lax.all_to_all(values, "patch", 0, 0, axis_index_groups=lines)

    rise = 2 * PLANE
    w_pair = jnp.stack(
        [w_out.T] + [swap(w_out.T, "patch", n_patch, rise * k) for k in range(1, n_head)]
    )

    positions = slab_order[0] * rows + jnp.arange(rows, dtype=jnp.int32)
    cos, sin = angle_tables(positions)
    q, kv0, kv1 = call(
        functools.partial(qkv_kernel, n_head),
        tuple(shaped((*n, rows, cols), BF16) for n in ((line, STEPS), (4,), (2,))),
        [SMEM] + [VMEM] * (2 * n_head + 5),
        [pltpu.VMEM((n_head, STEPS * rows, feats), BF16)],
        2 * STEPS * rows * w_qkv.size,
        2 * w_qkv.size,
    )(head[None], ids, *x_parts, *mod_parts, w, cos, sin, stale)

    kv_plane = plane_of(kv0)
    q_line = trade(q)
    w_pair, q_line = lax.optimization_barrier((w_pair, q_line))
    w_plane = plane_of(w_pair)
    parts = call(
        attend_kernel,
        shaped((line, STEPS * rows, cols + DH), BF16),
        [SMEM] + [VMEM] * (PLANE + 2),
        flops=8 * STEPS * rows * n_patch * rows * cols,
    )(patch[None], q_line, kv1, *kv_plane)
    o = call(merge_kernel, shaped((STEPS * rows, cols), BF16), [VMEM])(trade(parts))
    o_mate = swap(o, "patch", n_patch, PLANE)

    wide = (2 * STEPS * rows, PLANE * piece)

    def project(bit, dtype):
        return call(
            functools.partial(project_kernel, n_head, n_patch, bit),
            shaped(wide, dtype),
            [SMEM] * 2 + [VMEM] * (2 + PLANE),
            [pltpu.VMEM((PLANE, 2 * STEPS * rows, piece), F32)],
            2 * wide[0] * wide[1] * cols,
            2 * wide[1] * cols,
        )(patch[None], head[None], o, o_mate, *w_plane)

    sums = [swap(project(k, BF16), "head", n_head, k) for k in range(1, n_head)]
    sums = [project(0, F32)] + sums
    out_half = shaped((STEPS, rows, PLANE * piece), BF16)
    out_own, out_mate = call(
        functools.partial(gate_kernel, n_patch),
        (out_half, out_half),
        [SMEM] + [VMEM] * (2 + n_head),
    )(patch[None], ids, mod_own, *sums)
    out_back = swap(out_mate, "patch", n_patch, PLANE)
    second = (patch // PLANE) % 2 == 1
    return jnp.concatenate(
        [jnp.where(second, out_back, out_own), jnp.where(second, out_own, out_back)], axis=2
    )


def solution(mesh):
    in_specs = (
        P(None, "patch", "head"),
        P(None, "patch", "head"),
        P(None, None, "head"),
        P("head", "patch"),
        P(None, None, "head"),
        P(),
        P("patch"),
    )
    run = functools.partial(body, mesh.shape["patch"], mesh.shape["head"])
    return jax.shard_map(
        run, mesh=mesh, in_specs=in_specs, out_specs=P(None, "patch", "head"), check_vma=False
    )
```

```python
import functools
import math

import jax
import jax.numpy as jnp
from jax import lax
from jax.experimental import pallas as pl
from jax.experimental.pallas import tpu as pltpu
from jax.sharding import PartitionSpec as P

DH = 128
STEPS = 2
PLANE = 4
MIB = 1024 * 1024
VMEM = pl.BlockSpec(memory_space=pltpu.VMEM)
SMEM = pl.BlockSpec(memory_space=pltpu.SMEM)
ANY = pl.BlockSpec(memory_space=pl.ANY)
BF16, F32 = jnp.bfloat16, jnp.float32
NT = (((1,), (1,)), ((), ()))


def angle_tables(positions):
    half = DH // 2
    frequency = 10000.0 ** (-(2.0 * jnp.arange(half, dtype=F32)) / DH)
    grid = positions.astype(F32)[:, None] * frequency[None, :]
    cos, sin = jnp.cos(grid), jnp.sin(grid)
    return jnp.concatenate([cos, cos], axis=1), jnp.concatenate([-sin, sin], axis=1)


def swap(values, axis, count, bit):
    return lax.ppermute(values, axis, [(i, i ^ bit) for i in range(count)])


def load_kernel(ids, *refs):
    count = len(refs) // 2 - 1
    ids_out, sems = refs[-2:]
    copies = [
        pltpu.make_async_copy(refs[i], refs[count + i], sems.at[i]) for i in range(count)
    ]
    for copy in copies:
        copy.start()
    row = lax.broadcasted_iota(jnp.int32, ids_out.shape, 0)
    tile = jnp.zeros(ids_out.shape, jnp.int32)
    for step in range(STEPS):
        tile = jnp.where(row == step, ids[step], tile)
    ids_out[...] = tile
    for copy in copies:
        copy.wait()


def table_row(mod_ref, kind, ids_ref, step):
    chosen = ids_ref[step : step + 1, :1]
    table = mod_ref[kind]
    return sum(
        jnp.where(chosen == r, table[r : r + 1], 0.0) for r in range(table.shape[0])
    )


def qkv_kernel(n_head, head, ids_ref, *refs):
    x_refs, mod_refs = refs[:n_head], refs[n_head : 2 * n_head]
    w_ref, cos_ref, sin_ref = refs[2 * n_head : 2 * n_head + 3]
    q_ref, kv0_ref, kv1_ref, a_ref = refs[-4:]
    rows, feats = x_refs[0].shape[1:]
    width = n_head * feats
    cols = w_ref.shape[2]
    for step in range(STEPS):
        total, square = 0.0, 0.0
        for x_ref in x_refs:
            hidden = x_ref[step].astype(F32)
            total += jnp.sum(hidden, axis=1, keepdims=True)
            square += jnp.sum(hidden * hidden, axis=1, keepdims=True)
        mean = total / width
        inv = lax.rsqrt(square / width - mean * mean + 1e-06)
        for part in range(n_head):
            shift = table_row(mod_refs[part], 0, ids_ref, step)
            scale = table_row(mod_refs[part], 1, ids_ref, step)
            hidden = x_refs[part][step].astype(F32)
            a = (hidden - mean) * inv * (1.0 + scale) + shift
            a_ref[part, step * rows : (step + 1) * rows, :] = a.astype(BF16)
    cos, sin = cos_ref[...], sin_ref[...]
    for slot in range(3):
        total = jnp.zeros((STEPS * rows, cols), F32)
        for part in range(n_head):
            start = pl.multiple_of((head[0] ^ part) * feats, feats)
            total += jnp.dot(
                a_ref[part], w_ref[slot, pl.ds(start, feats), :], preferred_element_type=F32
            )
        for step in range(STEPS):
            for block in range(cols // DH):
                lanes = slice(block * DH, (block + 1) * DH)
                u = total[step * rows : (step + 1) * rows, lanes]
                if slot < 2:
                    u = u * cos + pltpu.roll(u, DH // 2, 1) * sin
                u = u.astype(BF16)
                if slot == 0:
                    q_ref[step, :, lanes] = u
                else:
                    (kv0_ref, kv1_ref)[step][slot - 1, :, lanes] = u


def split3(values):
    high = values.astype(BF16).astype(F32)
    middle = (values - high).astype(BF16).astype(F32)
    return [high, middle, values - high - middle]


def attend_kernel(q_ref, mate_ref, kv1_ref, *refs):
    kv_refs, out_ref = refs[:PLANE], refs[PLANE]
    blocks, _, rows, cols = kv_refs[0].shape
    blocks = blocks // STEPS
    old_rows = PLANE * blocks * rows
    shape = (2 * rows, old_rows + rows)
    mine = lax.broadcasted_iota(jnp.int32, shape, 0) < rows
    drop = lax.broadcasted_iota(jnp.int32, shape, 1) // rows == jnp.where(mine, 0, PLANE * blocks)
    lane = lax.broadcasted_iota(jnp.int32, (2 * rows, DH), 1)
    for step in range(STEPS):
        spot = slice(step * blocks, (step + 1) * blocks)
        fresh = (kv_refs[0].at[blocks], kv1_ref)[step]
        stats = jnp.zeros((2 * rows, DH), F32)
        mixed = []
        for head in range(cols // DH):
            lanes = slice(head * DH, (head + 1) * DH)

            def rows_of(kind):
                old = [ref[spot, kind, :, lanes].reshape(blocks * rows, DH) for ref in kv_refs]
                return jnp.concatenate([*old, fresh[kind, :, lanes]], axis=0)

            queries = jnp.concatenate([q_ref[step, :, lanes], mate_ref[step, :, lanes]], axis=0)
            scores = lax.dot_general(queries, rows_of(0), NT, preferred_element_type=F32)
            scores = jnp.where(drop, -1e30, scores * (1.0 / math.sqrt(DH)))
            top = jnp.max(scores, axis=1, keepdims=True)
            weights = jnp.exp(scores - top)
            totals = jnp.sum(weights, axis=1, keepdims=True)
            mixed.append(
                jnp.dot(weights.astype(BF16), rows_of(1), preferred_element_type=F32) / totals
            )
            for place, piece in enumerate(split3(top) + split3(totals)):
                stats = jnp.where(lane == head * 8 + place, piece, stats)
        packed = jnp.concatenate([*mixed, stats], axis=1).astype(BF16)
        for mate in range(2):
            start = (mate * STEPS + step) * rows
            out_ref[start : start + rows, :] = packed[mate * rows : (mate + 1) * rows]


def merge_kernel(part_ref, other_ref, o_ref):
    rows = part_ref.shape[0] // 2
    cols = o_ref.shape[1]
    source = lax.broadcasted_iota(jnp.int32, (DH, DH), 0)
    parts = [
        part_ref[...],
        jnp.concatenate([other_ref[rows:], other_ref[:rows]], axis=0),
    ]
    for head in range(cols // DH):
        lanes = slice(head * DH, (head + 1) * DH)

        def spread(part, first):
            pick = (source >= head * 8 + first) & (source < head * 8 + first + 3)
            return jnp.dot(part[:, cols:], pick.astype(F32).astype(BF16), preferred_element_type=F32)

        tops = [spread(part, 0) for part in parts]
        best = functools.reduce(jnp.maximum, tops)
        scales = [spread(part, 3) * jnp.exp(t - best) for part, t in zip(parts, tops)]
        mixed = sum(s * part[:, lanes].astype(F32) for s, part in zip(scales, parts))
        o_ref[:, lanes] = (mixed / sum(scales)).astype(BF16)


def project_kernel(n_head, n_patch, bit, patch, head, *refs):
    o_ref, w_refs, (out_ref, sums) = refs[0], refs[1 : 1 + PLANE], refs[1 + PLANE :]
    slot = head[0] ^ bit ^ (patch[0] // (n_patch // n_head))
    for near in range(PLANE):
        sums[(patch[0] % PLANE) ^ near] = lax.dot_general(
            o_ref[...], w_refs[near][slot], NT, preferred_element_type=F32
        )
    out = jnp.concatenate([sums[c] for c in range(PLANE)], axis=1)
    out_ref[...] = out.astype(out_ref.dtype)


def gate_kernel(n_patch, patch, ids_ref, mod_ref, *refs):
    sum_refs, (own_out, mate_out) = refs[:-2], refs[-2:]
    total = sum(ref[...].astype(F32) for ref in sum_refs)
    rows, width = total.shape
    each = rows // 2 // STEPS
    second = (patch[0] // PLANE) % 2 == 1
    for step in range(STEPS):
        gate = table_row(mod_ref, 2, ids_ref, step)
        gate = jnp.where(second, gate[:, width:], gate[:, :width])
        for mate, ref in enumerate((own_out, mate_out)):
            start = mate * (rows // 2) + step * each
            ref[step] = (gate * total[start : start + each]).astype(BF16)


def in_hbm(values):
    return pltpu.with_memory_space_constraint(values, pltpu.HBM)


def call(kernel, shapes, ins, scratch=(), flops=0, size=0, limit=16):
    return pl.pallas_call(
        kernel,
        out_shape=shapes,
        in_specs=ins,
        out_specs=jax.tree.map(lambda _: VMEM, shapes),
        scratch_shapes=scratch,
        compiler_params=pltpu.CompilerParams(vmem_limit_bytes=limit * MIB),
        cost_estimate=pl.CostEstimate(flops=flops, bytes_accessed=size, transcendentals=0),
    )


def body(n_patch, n_head, inputs, stale_kv, w_qkv, w_out, mod_table, step_ids, slab_order):
    rows, feats = inputs.shape[1:]
    cols = w_qkv.shape[2]
    piece = w_out.shape[1]
    patch = lax.axis_index("patch").astype(jnp.int32)
    head = lax.axis_index("head").astype(jnp.int32)
    shaped = jax.ShapeDtypeStruct

    x_parts = [swap(inputs, "head", n_head, k) for k in range(1, n_head)]
    mod_parts = [swap(mod_table, "head", n_head, k) for k in range(1, n_head)]
    first = (jnp.transpose(w_qkv, (1, 0, 2)), inputs, jnp.transpose(mod_table, (1, 0, 2)))
    w, x_own, mod_own, ids = call(
        load_kernel,
        tuple(pltpu.VMEM(v.shape, v.dtype) for v in first) + (shaped((8, DH), jnp.int32),),
        [SMEM] + [ANY] * len(first),
        [pltpu.SemaphoreType.DMA((len(first),))],
        size=2 * w_qkv.size,
    )(*map(in_hbm, (step_ids, *first)))
    x_parts = [x_own] + x_parts
    mod_parts = [mod_own] + [jnp.transpose(part, (1, 0, 2)) for part in mod_parts]

    def across(values, k):
        return swap(values, "patch", n_patch, k)

    def line_of(values):
        return [values] + [across(values, k) for k in range(2 * PLANE, n_patch, 2 * PLANE)]

    def plane_of(values):
        return [values] + [across(values, k) for k in range(1, PLANE)]

    stale_pair = line_of(stale_kv)
    w_pair = line_of(w_out.T)

    positions = slab_order[0] * rows + jnp.arange(rows, dtype=jnp.int32)
    cos, sin = angle_tables(positions)
    kv_shape = shaped((2, rows, cols), BF16)
    q, kv0, kv1 = call(
        functools.partial(qkv_kernel, n_head),
        (kv_shape,) * 3,
        [SMEM] + [VMEM] * (2 * n_head + 4) + [ANY] * (n_head - 1),
        [pltpu.VMEM((n_head, STEPS * rows, feats), BF16)],
        2 * STEPS * rows * w_qkv.size,
        2 * w_qkv.size,
    )(head[None], ids, *x_parts, *mod_parts, w, cos, sin, *stale_pair[1:])

    kv_pair = line_of(kv0)
    q_mate = across(q, PLANE)
    w_pair, kv_pair = lax.optimization_barrier((w_pair, kv_pair))
    kv_plane = plane_of(jnp.stack(stale_pair + kv_pair))
    w_plane = plane_of(jnp.stack(w_pair))
    tall = 2 * STEPS * rows
    part = call(
        attend_kernel,
        shaped((tall, cols + DH), BF16),
        [VMEM] * (3 + PLANE),
        flops=4 * STEPS * rows * n_patch * rows * cols,
    )(q, q_mate, kv1, *kv_plane)
    o = call(merge_kernel, shaped((tall, cols), BF16), [VMEM] * 2)(part, across(part, PLANE))
    wide = PLANE * piece

    def project(bit, dtype):
        return call(
            functools.partial(project_kernel, n_head, n_patch, bit),
            shaped((tall, wide), dtype),
            [SMEM] * 2 + [VMEM] * (1 + PLANE),
            [pltpu.VMEM((PLANE, tall, piece), F32)],
            2 * tall * wide * cols,
            2 * wide * cols,
        )(patch[None], head[None], o, *w_plane)

    sums = [swap(project(k, BF16), "head", n_head, k) for k in range(1, n_head)]
    sums = [project(0, F32)] + sums
    out_half = shaped((STEPS, rows, wide), BF16)
    out_own, out_mate = call(
        functools.partial(gate_kernel, n_patch),
        (out_half, out_half),
        [SMEM] + [VMEM] * (2 + n_head),
    )(patch[None], ids, mod_own, *sums)
    out_back = across(out_mate, PLANE)
    second = (patch // PLANE) % 2 == 1
    return jnp.concatenate(
        [jnp.where(second, out_back, out_own), jnp.where(second, out_own, out_back)], axis=2
    )


def solution(mesh):
    in_specs = (
        P(None, "patch", "head"),
        P(None, "patch", "head"),
        P(None, None, "head"),
        P("head", "patch"),
        P(None, None, "head"),
        P(),
        P("patch"),
    )
    run = functools.partial(body, mesh.shape["patch"], mesh.shape["head"])
    return jax.shard_map(
        run, mesh=mesh, in_specs=in_specs, out_specs=P(None, "patch", "head"), check_vma=False
    )
```

```python
import functools
import math

import jax
import jax.numpy as jnp
from jax import lax
from jax.experimental import pallas as pl
from jax.experimental.pallas import tpu as pltpu
from jax.sharding import PartitionSpec as P

DH = 128
STEPS = 2
PLANE = 4
SPLIT = 4
MIB = 1024 * 1024
VMEM = pl.BlockSpec(memory_space=pltpu.VMEM)
SMEM = pl.BlockSpec(memory_space=pltpu.SMEM)
ANY = pl.BlockSpec(memory_space=pl.ANY)
BF16, F32 = jnp.bfloat16, jnp.float32
NT = (((1,), (1,)), ((), ()))


def swap(values, axis, count, bit):
    return lax.ppermute(values, axis, [(i, i ^ bit) for i in range(count)])


def load_kernel(ids, slab, w_ref, x_ref, mod_ref, w_out, x_out, mod_out, ids_out, cos_ref, sin_ref, sems):
    part = w_ref.shape[1] // SPLIT
    copies = [
        pltpu.make_async_copy(
            w_ref.at[slot, pl.ds(k * part, part)],
            w_out.at[slot, pl.ds(k * part, part)],
            sems.at[slot * SPLIT + k],
        )
        for slot in range(3)
        for k in range(SPLIT)
    ]
    copies.append(pltpu.make_async_copy(x_ref, x_out, sems.at[3 * SPLIT]))
    copies.append(pltpu.make_async_copy(mod_ref, mod_out, sems.at[3 * SPLIT + 1]))
    for copy in copies:
        copy.start()
    row = lax.broadcasted_iota(jnp.int32, ids_out.shape, 0)
    tile = jnp.zeros(ids_out.shape, jnp.int32)
    for step in range(STEPS):
        tile = jnp.where(row == step, ids[step], tile)
    ids_out[...] = tile
    rows, half = cos_ref.shape[0], DH // 2
    lane = lax.broadcasted_iota(jnp.int32, cos_ref.shape, 1)
    spot = slab[0] * rows + lax.broadcasted_iota(jnp.int32, cos_ref.shape, 0)
    power = jnp.where(lane < half, lane, lane - half).astype(F32) * (-2.0 / DH)
    angle = spot.astype(F32) * jnp.exp(power * math.log(10000.0))
    cos_ref[...] = jnp.cos(angle)
    sin = jnp.sin(angle)
    sin_ref[...] = jnp.where(lane < half, -sin, sin)
    for copy in copies:
        copy.wait()


def table_row(mod_ref, kind, ids_ref, step):
    chosen = ids_ref[step : step + 1, :1]
    table = mod_ref[kind]
    return sum(
        jnp.where(chosen == r, table[r : r + 1], 0.0) for r in range(table.shape[0])
    )


def normalized(step, x_refs, mod_refs, ids_ref):
    hidden = [ref[step].astype(F32) for ref in x_refs]
    width = sum(part.shape[1] for part in hidden)
    mean = sum(jnp.sum(part, axis=1, keepdims=True) for part in hidden) / width
    square = sum(jnp.sum(part * part, axis=1, keepdims=True) for part in hidden) / width
    inv = lax.rsqrt(square - mean * mean + 1e-06)
    parts = []
    for part, mod_ref in zip(hidden, mod_refs):
        shift = table_row(mod_ref, 0, ids_ref, step)
        scale = table_row(mod_ref, 1, ids_ref, step)
        parts.append(((part - mean) * inv * (1.0 + scale) + shift).astype(BF16))
    return parts


def projected(parts, w_ref, slot, head):
    feats = parts[0].shape[1]
    total = jnp.zeros((parts[0].shape[0], w_ref.shape[2]), F32)
    for number, part in enumerate(parts):
        start = pl.multiple_of((head[0] ^ number) * feats, feats)
        w = w_ref[slot, pl.ds(start, feats), :]
        total += jnp.dot(part, w, preferred_element_type=F32)
    return total


def rotated(values, cos, sin):
    blocks = []
    for start in range(0, values.shape[1], DH):
        u = values[:, start : start + DH]
        blocks.append(u * cos + pltpu.roll(u, DH // 2, 1) * sin)
    return jnp.concatenate(blocks, axis=1)


def fresh_kernel(n_head, head, ids_ref, *refs):
    x_refs, mod_refs = refs[:n_head], refs[n_head : 2 * n_head]
    w_ref, cos_ref, sin_ref = refs[2 * n_head : 2 * n_head + 3]
    a_ref, kv0_ref = refs[-2:]
    parts = normalized(0, x_refs, mod_refs, ids_ref)
    for number, part in enumerate(parts):
        a_ref[number] = part
    keys = rotated(projected(parts, w_ref, 1, head), cos_ref[...], sin_ref[...])
    kv0_ref[0] = keys.astype(BF16)
    kv0_ref[1] = projected(parts, w_ref, 2, head).astype(BF16)


def rest_kernel(n_head, head, ids_ref, *refs):
    x_refs, mod_refs = refs[:n_head], refs[n_head : 2 * n_head]
    w_ref, cos_ref, sin_ref, a_ref, q_ref, kv1_ref = refs[2 * n_head :]
    rows = a_ref.shape[1]
    parts = normalized(1, x_refs, mod_refs, ids_ref)
    cos, sin = cos_ref[...], sin_ref[...]
    both = [jnp.concatenate([a_ref[k], part], axis=0) for k, part in enumerate(parts)]
    queries = projected(both, w_ref, 0, head)
    for step in range(STEPS):
        spot = slice(step * rows, (step + 1) * rows)
        q_ref[step] = rotated(queries[spot], cos, sin).astype(BF16)
    kv1_ref[0] = rotated(projected(parts, w_ref, 1, head), cos, sin).astype(BF16)
    kv1_ref[1] = projected(parts, w_ref, 2, head).astype(BF16)


def split3(values):
    high = values.astype(BF16).astype(F32)
    middle = (values - high).astype(BF16).astype(F32)
    return [high, middle, values - high - middle]


def attend_kernel(q_ref, mate_ref, kv1_ref, *refs):
    stale_refs, kv0_refs, out_ref = refs[:PLANE], refs[PLANE : 2 * PLANE], refs[2 * PLANE]
    blocks, _, rows, cols = kv0_refs[0].shape
    old_rows = PLANE * blocks * rows
    shape = (2 * rows, old_rows + rows)
    mine = lax.broadcasted_iota(jnp.int32, shape, 0) < rows
    drop = lax.broadcasted_iota(jnp.int32, shape, 1) // rows == jnp.where(mine, 0, PLANE * blocks)
    lane = lax.broadcasted_iota(jnp.int32, (2 * rows, DH), 1)
    for step in range(STEPS):
        before = (stale_refs, kv0_refs)[step]
        fresh = (kv0_refs[0].at[0], kv1_ref)[step]
        stats = jnp.zeros((2 * rows, DH), F32)
        mixed = []
        for head in range(cols // DH):
            lanes = slice(head * DH, (head + 1) * DH)

            def rows_of(kind):
                old = [ref[:, kind, :, lanes].reshape(blocks * rows, DH) for ref in before]
                return jnp.concatenate([*old, fresh[kind, :, lanes]], axis=0)

            queries = jnp.concatenate([q_ref[step, :, lanes], mate_ref[step, :, lanes]], axis=0)
            scores = lax.dot_general(queries, rows_of(0), NT, preferred_element_type=F32)
            scores = jnp.where(drop, -1e30, scores * (1.0 / math.sqrt(DH)))
            top = jnp.max(scores, axis=1, keepdims=True)
            weights = jnp.exp(scores - top)
            totals = jnp.sum(weights, axis=1, keepdims=True)
            mixed.append(
                jnp.dot(weights.astype(BF16), rows_of(1), preferred_element_type=F32) / totals
            )
            for place, piece in enumerate(split3(top) + split3(totals)):
                stats = jnp.where(lane == head * 8 + place, piece, stats)
        packed = jnp.concatenate([*mixed, stats], axis=1).astype(BF16)
        for mate in range(2):
            start = (mate * STEPS + step) * rows
            out_ref[start : start + rows, :] = packed[mate * rows : (mate + 1) * rows]


def merge_kernel(part_ref, other_ref, o_ref):
    rows = part_ref.shape[0] // 2
    cols = o_ref.shape[1]
    source = lax.broadcasted_iota(jnp.int32, (DH, DH), 0)
    parts = [
        part_ref[...],
        jnp.concatenate([other_ref[rows:], other_ref[:rows]], axis=0),
    ]
    for head in range(cols // DH):
        lanes = slice(head * DH, (head + 1) * DH)

        def spread(part, first):
            pick = (source >= head * 8 + first) & (source < head * 8 + first + 3)
            return jnp.dot(part[:, cols:], pick.astype(F32).astype(BF16), preferred_element_type=F32)

        tops = [spread(part, 0) for part in parts]
        best = functools.reduce(jnp.maximum, tops)
        scales = [spread(part, 3) * jnp.exp(t - best) for part, t in zip(parts, tops)]
        mixed = sum(s * part[:, lanes].astype(F32) for s, part in zip(scales, parts))
        o_ref[:, lanes] = (mixed / sum(scales)).astype(BF16)


def project_kernel(n_head, n_patch, bit, patch, head, *refs):
    o_ref, w_refs, (out_ref, sums) = refs[0], refs[1 : 1 + PLANE], refs[1 + PLANE :]
    slot = head[0] ^ bit ^ (patch[0] // (n_patch // n_head))
    for near in range(PLANE):
        sums[(patch[0] % PLANE) ^ near] = lax.dot_general(
            o_ref[...], w_refs[near][slot], NT, preferred_element_type=F32
        )
    out = jnp.concatenate([sums[c] for c in range(PLANE)], axis=1)
    out_ref[...] = out.astype(out_ref.dtype)


def gate_kernel(n_patch, patch, ids_ref, mod_ref, *refs):
    sum_refs, (own_out, mate_out) = refs[:-2], refs[-2:]
    total = sum(ref[...].astype(F32) for ref in sum_refs)
    rows, width = total.shape
    each = rows // 2 // STEPS
    second = (patch[0] // PLANE) % 2 == 1
    for step in range(STEPS):
        gate = table_row(mod_ref, 2, ids_ref, step)
        gate = jnp.where(second, gate[:, width:], gate[:, :width])
        for mate, ref in enumerate((own_out, mate_out)):
            start = mate * (rows // 2) + step * each
            ref[step] = (gate * total[start : start + each]).astype(BF16)


def in_hbm(values):
    return pltpu.with_memory_space_constraint(values, pltpu.HBM)


def call(kernel, shapes, ins, scratch=(), flops=0, size=0, limit=16):
    return pl.pallas_call(
        kernel,
        out_shape=shapes,
        in_specs=ins,
        out_specs=jax.tree.map(lambda _: VMEM, shapes),
        scratch_shapes=scratch,
        compiler_params=pltpu.CompilerParams(vmem_limit_bytes=limit * MIB),
        cost_estimate=pl.CostEstimate(flops=flops, bytes_accessed=size, transcendentals=0),
    )


def body(n_patch, n_head, inputs, stale_kv, w_qkv, w_out, mod_table, step_ids, slab_order):
    rows, feats = inputs.shape[1:]
    cols = w_qkv.shape[2]
    piece = w_out.shape[1]
    patch = lax.axis_index("patch").astype(jnp.int32)
    head = lax.axis_index("head").astype(jnp.int32)
    shaped = jax.ShapeDtypeStruct

    x_parts = [swap(inputs, "head", n_head, k) for k in range(1, n_head)]
    mod_parts = [swap(mod_table, "head", n_head, k) for k in range(1, n_head)]
    first = (jnp.transpose(w_qkv, (1, 0, 2)), inputs, jnp.transpose(mod_table, (1, 0, 2)))
    w, x_own, mod_own, ids, cos, sin = call(
        load_kernel,
        tuple(pltpu.VMEM(v.shape, v.dtype) for v in first)
        + (shaped((8, DH), jnp.int32), shaped((rows, DH), F32), shaped((rows, DH), F32)),
        [SMEM] * 2 + [ANY] * len(first),
        [pltpu.SemaphoreType.DMA((3 * SPLIT + 2,))],
        size=2 * w_qkv.size,
    )(in_hbm(step_ids), slab_order, *map(in_hbm, first))
    x_parts = [x_own] + x_parts
    mod_parts = [mod_own] + [jnp.transpose(part, (1, 0, 2)) for part in mod_parts]

    def across(values, k):
        return swap(values, "patch", n_patch, k)

    def line_of(values):
        return [values] + [across(values, k) for k in range(2 * PLANE, n_patch, 2 * PLANE)]

    def plane_of(values):
        return [values] + [across(values, k) for k in range(1, PLANE)]

    stale_pair = line_of(stale_kv)
    w_pair = line_of(w_out.T)

    kv_shape = shaped((2, rows, cols), BF16)
    common = (head[None], ids, *x_parts, *mod_parts, w, cos, sin)
    specs = [SMEM] + [VMEM] * (2 * n_head + 4)
    a, kv0 = call(
        functools.partial(fresh_kernel, n_head),
        (shaped((n_head, rows, feats), BF16), kv_shape),
        specs + [ANY] * (n_head - 1),
        flops=4 * rows * w_qkv.size // 3,
        size=2 * w_qkv.size,
    )(*common, *stale_pair[1:])
    q, kv1 = call(
        functools.partial(rest_kernel, n_head),
        (kv_shape, kv_shape),
        specs + [VMEM],
        flops=8 * rows * w_qkv.size // 3,
        size=2 * w_qkv.size,
    )(*common, a)

    kv_pair = line_of(kv0)
    q_mate = across(q, PLANE)
    stale_pair, w_pair, kv0 = lax.optimization_barrier((stale_pair, w_pair, kv0))
    stale_plane = plane_of(jnp.stack(stale_pair))
    kv_pair, stale_plane, q_mate = lax.optimization_barrier((kv_pair, stale_plane, q_mate))
    kv_plane = plane_of(jnp.stack(kv_pair))
    w_pair, kv_plane = lax.optimization_barrier((w_pair, kv_plane))
    w_plane = plane_of(jnp.stack(w_pair))
    tall = 2 * STEPS * rows
    part = call(
        attend_kernel,
        shaped((tall, cols + DH), BF16),
        [VMEM] * (3 + 2 * PLANE),
        flops=4 * STEPS * rows * n_patch * rows * cols,
    )(q, q_mate, kv1, *stale_plane, *kv_plane)
    o = call(merge_kernel, shaped((tall, cols), BF16), [VMEM] * 2)(part, across(part, PLANE))
    wide = PLANE * piece

    def project(bit, dtype):
        return call(
            functools.partial(project_kernel, n_head, n_patch, bit),
            shaped((tall, wide), dtype),
            [SMEM] * 2 + [VMEM] * (1 + PLANE),
            [pltpu.VMEM((PLANE, tall, piece), F32)],
            2 * tall * wide * cols,
            2 * wide * cols,
        )(patch[None], head[None], o, *w_plane)

    sums = [swap(project(k, BF16), "head", n_head, k) for k in range(1, n_head)]
    sums = [project(0, F32)] + sums
    out_half = shaped((STEPS, rows, wide), BF16)
    out_own, out_mate = call(
        functools.partial(gate_kernel, n_patch),
        (out_half, out_half),
        [SMEM] + [VMEM] * (2 + n_head),
    )(patch[None], ids, mod_own, *sums)
    out_back = across(out_mate, PLANE)
    second = (patch // PLANE) % 2 == 1
    return jnp.concatenate(
        [jnp.where(second, out_back, out_own), jnp.where(second, out_own, out_back)], axis=2
    )


def solution(mesh):
    in_specs = (
        P(None, "patch", "head"),
        P(None, "patch", "head"),
        P(None, None, "head"),
        P("head", "patch"),
        P(None, None, "head"),
        P(),
        P("patch"),
    )
    run = functools.partial(body, mesh.shape["patch"], mesh.shape["head"])
    return jax.shard_map(
        run, mesh=mesh, in_specs=in_specs, out_specs=P(None, "patch", "head"), check_vma=False
    )
```

```python
import functools
import math

import jax
import jax.numpy as jnp
from jax import lax
from jax.experimental import pallas as pl
from jax.experimental.pallas import tpu as pltpu
from jax.sharding import PartitionSpec as P

DH = 128
STEPS = 2
PLANE = 4
MIB = 1024 * 1024
VMEM = pl.BlockSpec(memory_space=pltpu.VMEM)
SMEM = pl.BlockSpec(memory_space=pltpu.SMEM)
ANY = pl.BlockSpec(memory_space=pl.ANY)
BF16, F32 = jnp.bfloat16, jnp.float32
NT = (((1,), (1,)), ((), ()))


def swap(values, axis, count, bit):
    return lax.ppermute(values, axis, [(i, i ^ bit) for i in range(count)])


def load_kernel(ids, slab, w_ref, x_ref, mod_ref, w_out, x_out, mod_out, ids_out, cos_ref, sin_ref, sems):
    copies = [
        pltpu.make_async_copy(w_ref.at[slot + 1], w_out.at[slot], sems.at[slot])
        for slot in range(2)
    ]
    copies.append(pltpu.make_async_copy(x_ref, x_out, sems.at[2]))
    copies.append(pltpu.make_async_copy(mod_ref, mod_out, sems.at[3]))
    for copy in copies:
        copy.start()
    row = lax.broadcasted_iota(jnp.int32, ids_out.shape, 0)
    tile = jnp.zeros(ids_out.shape, jnp.int32)
    for step in range(STEPS):
        tile = jnp.where(row == step, ids[step], tile)
    ids_out[...] = tile
    rows, half = cos_ref.shape[0], DH // 2
    lane = lax.broadcasted_iota(jnp.int32, cos_ref.shape, 1)
    spot = slab[0] * rows + lax.broadcasted_iota(jnp.int32, cos_ref.shape, 0)
    power = jnp.where(lane < half, lane, lane - half).astype(F32) * (-2.0 / DH)
    angle = spot.astype(F32) * jnp.exp(power * math.log(10000.0))
    cos_ref[...] = jnp.cos(angle)
    sin = jnp.sin(angle)
    sin_ref[...] = jnp.where(lane < half, -sin, sin)
    for copy in copies:
        copy.wait()


def table_row(mod_ref, kind, ids_ref, step):
    chosen = ids_ref[step : step + 1, :1]
    table = mod_ref[kind]
    return sum(
        jnp.where(chosen == r, table[r : r + 1], 0.0) for r in range(table.shape[0])
    )


def normalized(step, x_refs, mod_refs, ids_ref):
    hidden = [ref[step].astype(F32) for ref in x_refs]
    width = sum(part.shape[1] for part in hidden)
    mean = sum(jnp.sum(part, axis=1, keepdims=True) for part in hidden) / width
    square = sum(jnp.sum(part * part, axis=1, keepdims=True) for part in hidden) / width
    inv = lax.rsqrt(square - mean * mean + 1e-06)
    parts = []
    for part, mod_ref in zip(hidden, mod_refs):
        shift = table_row(mod_ref, 0, ids_ref, step)
        scale = table_row(mod_ref, 1, ids_ref, step)
        parts.append(((part - mean) * inv * (1.0 + scale) + shift).astype(BF16))
    return parts


def projected(parts, w_ref, slot, head):
    feats = parts[0].shape[1]
    total = jnp.zeros((parts[0].shape[0], w_ref.shape[2]), F32)
    for number, part in enumerate(parts):
        start = pl.multiple_of((head[0] ^ number) * feats, feats)
        w = w_ref[slot, pl.ds(start, feats), :]
        total += jnp.dot(part, w, preferred_element_type=F32)
    return total


def rotated(values, cos, sin):
    blocks = []
    for start in range(0, values.shape[1], DH):
        u = values[:, start : start + DH]
        blocks.append(u * cos + pltpu.roll(u, DH // 2, 1) * sin)
    return jnp.concatenate(blocks, axis=1)


def fresh_kernel(n_head, head, ids_ref, *refs):
    x_refs, mod_refs = refs[:n_head], refs[n_head : 2 * n_head]
    w_ref, cos_ref, sin_ref = refs[2 * n_head : 2 * n_head + 3]
    a_ref, kv0_ref = refs[-2:]
    parts = normalized(0, x_refs, mod_refs, ids_ref)
    for number, part in enumerate(parts):
        a_ref[number] = part
    keys = rotated(projected(parts, w_ref, 0, head), cos_ref[...], sin_ref[...])
    kv0_ref[0] = keys.astype(BF16)
    kv0_ref[1] = projected(parts, w_ref, 1, head).astype(BF16)


def rest_kernel(n_head, head, ids_ref, *refs):
    x_refs, mod_refs = refs[:n_head], refs[n_head : 2 * n_head]
    w_ref, cos_ref, sin_ref, a_ref, w_far, q_ref, kv1_ref, wq_ref, sem = refs[2 * n_head :]
    copy = pltpu.make_async_copy(w_far.at[0], wq_ref.at[0], sem)
    copy.start()
    rows = a_ref.shape[1]
    parts = normalized(1, x_refs, mod_refs, ids_ref)
    cos, sin = cos_ref[...], sin_ref[...]
    both = [jnp.concatenate([a_ref[k], part], axis=0) for k, part in enumerate(parts)]
    kv1_ref[0] = rotated(projected(parts, w_ref, 0, head), cos, sin).astype(BF16)
    kv1_ref[1] = projected(parts, w_ref, 1, head).astype(BF16)
    copy.wait()
    queries = projected(both, wq_ref, 0, head)
    for step in range(STEPS):
        spot = slice(step * rows, (step + 1) * rows)
        q_ref[step] = rotated(queries[spot], cos, sin).astype(BF16)


def split3(values):
    high = values.astype(BF16).astype(F32)
    middle = (values - high).astype(BF16).astype(F32)
    return [high, middle, values - high - middle]


def attend_kernel(patch, q_ref, mate_ref, kv0_ref, kv1_ref, kv_ref, out_ref):
    rows, cols = kv0_ref.shape[1:]
    blocks = kv_ref.shape[0] // (2 * STEPS)
    old_rows = PLANE * blocks * rows
    shape = (2 * rows, old_rows + rows)
    mine = lax.broadcasted_iota(jnp.int32, shape, 0) < rows
    stray = jnp.where(mine, patch[0] % PLANE, PLANE * blocks)
    drop = lax.broadcasted_iota(jnp.int32, shape, 1) // rows == stray
    lane = lax.broadcasted_iota(jnp.int32, (2 * rows, DH), 1)
    for step in range(STEPS):
        first = 2 * blocks * step
        fresh = (kv0_ref, kv1_ref)[step]
        stats = jnp.zeros((2 * rows, DH), F32)
        mixed = []
        for head in range(cols // DH):
            lanes = slice(head * DH, (head + 1) * DH)

            def rows_of(kind):
                old = [kv_ref[first + 2 * k + kind, :, lanes] for k in range(blocks)]
                return jnp.concatenate([*old, fresh[kind, :, lanes]], axis=0)

            queries = jnp.concatenate([q_ref[step, :, lanes], mate_ref[step, :, lanes]], axis=0)
            scores = lax.dot_general(queries, rows_of(0), NT, preferred_element_type=F32)
            scores = jnp.where(drop, -1e30, scores * (1.0 / math.sqrt(DH)))
            top = jnp.max(scores, axis=1, keepdims=True)
            weights = jnp.exp(scores - top)
            totals = jnp.sum(weights, axis=1, keepdims=True)
            mixed.append(
                jnp.dot(weights.astype(BF16), rows_of(1), preferred_element_type=F32) / totals
            )
            for place, piece in enumerate(split3(top) + split3(totals)):
                stats = jnp.where(lane == head * 8 + place, piece, stats)
        packed = jnp.concatenate([*mixed, stats], axis=1).astype(BF16)
        for mate in range(2):
            start = (mate * STEPS + step) * rows
            out_ref[start : start + rows, :] = packed[mate * rows : (mate + 1) * rows]


def merge_kernel(part_ref, other_ref, o_ref):
    rows = part_ref.shape[0] // 2
    cols = o_ref.shape[1]
    source = lax.broadcasted_iota(jnp.int32, (DH, DH), 0)
    parts = [
        part_ref[...],
        jnp.concatenate([other_ref[rows:], other_ref[:rows]], axis=0),
    ]
    for head in range(cols // DH):
        lanes = slice(head * DH, (head + 1) * DH)

        def spread(part, first):
            pick = (source >= head * 8 + first) & (source < head * 8 + first + 3)
            return jnp.dot(part[:, cols:], pick.astype(F32).astype(BF16), preferred_element_type=F32)

        tops = [spread(part, 0) for part in parts]
        best = functools.reduce(jnp.maximum, tops)
        scales = [spread(part, 3) * jnp.exp(t - best) for part, t in zip(parts, tops)]
        mixed = sum(s * part[:, lanes].astype(F32) for s, part in zip(scales, parts))
        o_ref[:, lanes] = (mixed / sum(scales)).astype(BF16)


def project_kernel(n_head, n_patch, bit, patch, head, *refs):
    o_ref, w_refs, (out_ref, sums) = refs[0], refs[1 : 1 + PLANE], refs[1 + PLANE :]
    slot = head[0] ^ bit ^ (patch[0] // (n_patch // n_head))
    for near in range(PLANE):
        sums[(patch[0] % PLANE) ^ near] = lax.dot_general(
            o_ref[...], w_refs[near][slot], NT, preferred_element_type=F32
        )
    out = jnp.concatenate([sums[c] for c in range(PLANE)], axis=1)
    out_ref[...] = out.astype(out_ref.dtype)


def gate_kernel(n_patch, patch, ids_ref, mod_ref, *refs):
    sum_refs, (own_out, mate_out) = refs[:-2], refs[-2:]
    total = sum(ref[...].astype(F32) for ref in sum_refs)
    rows, width = total.shape
    each = rows // 2 // STEPS
    second = (patch[0] // PLANE) % 2 == 1
    for step in range(STEPS):
        gate = table_row(mod_ref, 2, ids_ref, step)
        gate = jnp.where(second, gate[:, width:], gate[:, :width])
        for mate, ref in enumerate((own_out, mate_out)):
            start = mate * (rows // 2) + step * each
            ref[step] = (gate * total[start : start + each]).astype(BF16)


def in_hbm(values):
    return pltpu.with_memory_space_constraint(values, pltpu.HBM)


def call(kernel, shapes, ins, scratch=(), flops=0, size=0, limit=16):
    return pl.pallas_call(
        kernel,
        out_shape=shapes,
        in_specs=ins,
        out_specs=jax.tree.map(lambda _: VMEM, shapes),
        scratch_shapes=scratch,
        compiler_params=pltpu.CompilerParams(vmem_limit_bytes=limit * MIB),
        cost_estimate=pl.CostEstimate(flops=flops, bytes_accessed=size, transcendentals=0),
    )


def body(n_patch, n_head, inputs, stale_kv, w_qkv, w_out, mod_table, step_ids, slab_order):
    rows, feats = inputs.shape[1:]
    cols = w_qkv.shape[2]
    piece = w_out.shape[1]
    patch = lax.axis_index("patch").astype(jnp.int32)
    head = lax.axis_index("head").astype(jnp.int32)
    shaped = jax.ShapeDtypeStruct

    x_parts = [swap(inputs, "head", n_head, k) for k in range(1, n_head)]
    mod_parts = [swap(mod_table, "head", n_head, k) for k in range(1, n_head)]
    first = (jnp.transpose(w_qkv, (1, 0, 2)), inputs, jnp.transpose(mod_table, (1, 0, 2)))
    w, x_own, mod_own, ids, cos, sin = call(
        load_kernel,
        (pltpu.VMEM((2, *first[0].shape[1:]), BF16),)
        + tuple(pltpu.VMEM(v.shape, v.dtype) for v in first[1:])
        + (shaped((8, DH), jnp.int32), shaped((rows, DH), F32), shaped((rows, DH), F32)),
        [SMEM] * 2 + [ANY] * len(first),
        [pltpu.SemaphoreType.DMA((4,))],
        size=2 * w_qkv.size,
    )(in_hbm(step_ids), slab_order, *map(in_hbm, first))
    x_parts = [x_own] + x_parts
    mod_parts = [mod_own] + [jnp.transpose(part, (1, 0, 2)) for part in mod_parts]

    def across(values, k):
        return swap(values, "patch", n_patch, k)

    def line_of(values):
        return [values] + [across(values, k) for k in range(2 * PLANE, n_patch, 2 * PLANE)]

    def plane_of(values):
        return [values] + [across(values, k) for k in range(1, PLANE)]

    stale_pair = line_of(stale_kv)
    w_pair = line_of(w_out.T)

    kv_shape = shaped((2, rows, cols), BF16)
    common = (head[None], ids, *x_parts, *mod_parts, w, cos, sin)
    specs = [SMEM] + [VMEM] * (2 * n_head + 4)
    a, kv0 = call(
        functools.partial(fresh_kernel, n_head),
        (shaped((n_head, rows, feats), BF16), kv_shape),
        specs,
        flops=4 * rows * w_qkv.size // 3,
        size=2 * w_qkv.size,
    )(*common)
    q, kv1 = call(
        functools.partial(rest_kernel, n_head),
        (kv_shape, kv_shape),
        specs + [VMEM, ANY],
        [pltpu.VMEM((1, *first[0].shape[1:]), BF16), pltpu.SemaphoreType.DMA],
        8 * rows * w_qkv.size // 3,
        2 * w_qkv.size,
    )(*common, a, in_hbm(first[0]))

    kv_pair = line_of(kv0)
    q_mate = across(q, PLANE)
    w_pair, kv0 = lax.optimization_barrier((w_pair, kv0))
    w_plane = plane_of(jnp.stack(w_pair))
    planes = [list(range(k, k + PLANE)) for k in range(0, n_patch, PLANE)]
    kv = lax.all_gather(
        jnp.concatenate(stale_pair + kv_pair), "patch", axis=1, axis_index_groups=planes, tiled=True
    )
    tall = 2 * STEPS * rows
    part = call(
        attend_kernel,
        shaped((tall, cols + DH), BF16),
        [SMEM] + [VMEM] * 5,
        flops=4 * STEPS * rows * n_patch * rows * cols,
    )(patch[None], q, q_mate, kv0, kv1, kv)
    o = call(merge_kernel, shaped((tall, cols), BF16), [VMEM] * 2)(part, across(part, PLANE))
    wide = PLANE * piece

    def project(bit, dtype):
        return call(
            functools.partial(project_kernel, n_head, n_patch, bit),
            shaped((tall, wide), dtype),
            [SMEM] * 2 + [VMEM] * (1 + PLANE),
            [pltpu.VMEM((PLANE, tall, piece), F32)],
            2 * tall * wide * cols,
            2 * wide * cols,
        )(patch[None], head[None], o, *w_plane)

    sums = [swap(project(k, BF16), "head", n_head, k) for k in range(1, n_head)]
    sums = [project(0, F32)] + sums
    out_half = shaped((STEPS, rows, wide), BF16)
    out_own, out_mate = call(
        functools.partial(gate_kernel, n_patch),
        (out_half, out_half),
        [SMEM] + [VMEM] * (2 + n_head),
    )(patch[None], ids, mod_own, *sums)
    out_back = across(out_mate, PLANE)
    second = (patch // PLANE) % 2 == 1
    return jnp.concatenate(
        [jnp.where(second, out_back, out_own), jnp.where(second, out_own, out_back)], axis=2
    )


def solution(mesh):
    in_specs = (
        P(None, "patch", "head"),
        P(None, "patch", "head"),
        P(None, None, "head"),
        P("head", "patch"),
        P(None, None, "head"),
        P(),
        P("patch"),
    )
    run = functools.partial(body, mesh.shape["patch"], mesh.shape["head"])
    return jax.shard_map(
        run, mesh=mesh, in_specs=in_specs, out_specs=P(None, "patch", "head"), check_vma=False
    )
```

```python
import functools
import math

import jax
import jax.numpy as jnp
from jax import lax
from jax.experimental import pallas as pl
from jax.experimental.pallas import tpu as pltpu
from jax.sharding import PartitionSpec as P

DH = 128
STEPS = 2
PLANE = 4
MIB = 1024 * 1024
VMEM = pl.BlockSpec(memory_space=pltpu.VMEM)
SMEM = pl.BlockSpec(memory_space=pltpu.SMEM)
ANY = pl.BlockSpec(memory_space=pl.ANY)
BF16, F32 = jnp.bfloat16, jnp.float32
NT = (((1,), (1,)), ((), ()))


def swap(values, axis, count, bit):
    return lax.ppermute(values, axis, [(i, i ^ bit) for i in range(count)])


def load_kernel(ids, slab, w_ref, x_ref, mod_ref, stale_ref, w_out, x_out, mod_out, stale_out, *refs):
    ids_out, cos_ref, sin_ref, sems = refs
    copies = [
        pltpu.make_async_copy(w_ref.at[slot + 1], w_out.at[slot], sems.at[slot])
        for slot in range(2)
    ]
    copies.append(pltpu.make_async_copy(x_ref, x_out, sems.at[2]))
    copies.append(pltpu.make_async_copy(mod_ref, mod_out, sems.at[3]))
    copies.append(pltpu.make_async_copy(stale_ref, stale_out, sems.at[4]))
    for copy in copies:
        copy.start()
    row = lax.broadcasted_iota(jnp.int32, ids_out.shape, 0)
    tile = jnp.zeros(ids_out.shape, jnp.int32)
    for step in range(STEPS):
        tile = jnp.where(row == step, ids[step], tile)
    ids_out[...] = tile
    rows, half = cos_ref.shape[0], DH // 2
    lane = lax.broadcasted_iota(jnp.int32, cos_ref.shape, 1)
    spot = slab[0] * rows + lax.broadcasted_iota(jnp.int32, cos_ref.shape, 0)
    power = jnp.where(lane < half, lane, lane - half).astype(F32) * (-2.0 / DH)
    angle = spot.astype(F32) * jnp.exp(power * math.log(10000.0))
    cos_ref[...] = jnp.cos(angle)
    sin = jnp.sin(angle)
    sin_ref[...] = jnp.where(lane < half, -sin, sin)
    for copy in copies:
        copy.wait()


def table_row(mod_ref, kind, ids_ref, step):
    chosen = ids_ref[step : step + 1, :1]
    table = mod_ref[kind]
    return sum(
        jnp.where(chosen == r, table[r : r + 1], 0.0) for r in range(table.shape[0])
    )


def normalized(step, x_refs, mod_refs, ids_ref):
    hidden = [ref[step].astype(F32) for ref in x_refs]
    width = sum(part.shape[1] for part in hidden)
    mean = sum(jnp.sum(part, axis=1, keepdims=True) for part in hidden) / width
    square = sum(jnp.sum(part * part, axis=1, keepdims=True) for part in hidden) / width
    inv = lax.rsqrt(square - mean * mean + 1e-06)
    parts = []
    for part, mod_ref in zip(hidden, mod_refs):
        shift = table_row(mod_ref, 0, ids_ref, step)
        scale = table_row(mod_ref, 1, ids_ref, step)
        parts.append(((part - mean) * inv * (1.0 + scale) + shift).astype(BF16))
    return parts


def projected(parts, w_ref, slot, head):
    feats = parts[0].shape[1]
    total = jnp.zeros((parts[0].shape[0], w_ref.shape[2]), F32)
    for number, part in enumerate(parts):
        start = pl.multiple_of((head[0] ^ number) * feats, feats)
        w = w_ref[slot, pl.ds(start, feats), :]
        total += jnp.dot(part, w, preferred_element_type=F32)
    return total


def rotated(values, cos, sin):
    blocks = []
    for start in range(0, values.shape[1], DH):
        u = values[:, start : start + DH]
        blocks.append(u * cos + pltpu.roll(u, DH // 2, 1) * sin)
    return jnp.concatenate(blocks, axis=1)


def fresh_kernel(n_head, head, ids_ref, *refs):
    x_refs, mod_refs = refs[:n_head], refs[n_head : 2 * n_head]
    w_ref, cos_ref, sin_ref = refs[2 * n_head : 2 * n_head + 3]
    stale_ref, a_ref, kv_ref = refs[2 * n_head + 3 :]
    kv_ref[:2] = stale_ref[...]
    parts = normalized(0, x_refs, mod_refs, ids_ref)
    for number, part in enumerate(parts):
        a_ref[number] = part
    keys = rotated(projected(parts, w_ref, 0, head), cos_ref[...], sin_ref[...])
    kv_ref[2] = keys.astype(BF16)
    kv_ref[3] = projected(parts, w_ref, 1, head).astype(BF16)


def rest_kernel(n_head, head, ids_ref, *refs):
    x_refs, mod_refs = refs[:n_head], refs[n_head : 2 * n_head]
    w_ref, cos_ref, sin_ref, a_ref, w_far, q_ref, kv1_ref, wq_ref, sem = refs[2 * n_head :]
    copy = pltpu.make_async_copy(w_far.at[0], wq_ref.at[0], sem)
    copy.start()
    rows = a_ref.shape[1]
    parts = normalized(1, x_refs, mod_refs, ids_ref)
    cos, sin = cos_ref[...], sin_ref[...]
    both = [jnp.concatenate([a_ref[k], part], axis=0) for k, part in enumerate(parts)]
    kv1_ref[0] = rotated(projected(parts, w_ref, 0, head), cos, sin).astype(BF16)
    kv1_ref[1] = projected(parts, w_ref, 1, head).astype(BF16)
    copy.wait()
    queries = projected(both, wq_ref, 0, head)
    for step in range(STEPS):
        spot = slice(step * rows, (step + 1) * rows)
        q_ref[step] = rotated(queries[spot], cos, sin).astype(BF16)


def split3(values):
    high = values.astype(BF16).astype(F32)
    middle = (values - high).astype(BF16).astype(F32)
    return [high, middle, values - high - middle]


def attend_kernel(q_ref, mate_ref, kv1_ref, *refs):
    kv_refs, out_ref = refs[:PLANE], refs[PLANE]
    blocks, _, rows, cols = kv_refs[0].shape
    old_rows = PLANE * blocks * rows
    shape = (2 * rows, old_rows + rows)
    mine = lax.broadcasted_iota(jnp.int32, shape, 0) < rows
    stray = jnp.where(mine, 0, PLANE * blocks)
    drop = lax.broadcasted_iota(jnp.int32, shape, 1) // rows == stray
    lane = lax.broadcasted_iota(jnp.int32, (2 * rows, DH), 1)
    for step in range(STEPS):
        fresh = (kv_refs[0].at[0, 2:], kv1_ref)[step]
        stats = jnp.zeros((2 * rows, DH), F32)
        mixed = []
        for head in range(cols // DH):
            lanes = slice(head * DH, (head + 1) * DH)

            def rows_of(kind):
                old = [ref[:, 2 * step + kind, :, lanes].reshape(blocks * rows, DH) for ref in kv_refs]
                return jnp.concatenate([*old, fresh[kind, :, lanes]], axis=0)

            queries = jnp.concatenate([q_ref[step, :, lanes], mate_ref[step, :, lanes]], axis=0)
            scores = lax.dot_general(queries, rows_of(0), NT, preferred_element_type=F32)
            scores = jnp.where(drop, -1e30, scores * (1.0 / math.sqrt(DH)))
            top = jnp.max(scores, axis=1, keepdims=True)
            weights = jnp.exp(scores - top)
            totals = jnp.sum(weights, axis=1, keepdims=True)
            mixed.append(
                jnp.dot(weights.astype(BF16), rows_of(1), preferred_element_type=F32) / totals
            )
            for place, piece in enumerate(split3(top) + split3(totals)):
                stats = jnp.where(lane == head * 8 + place, piece, stats)
        packed = jnp.concatenate([*mixed, stats], axis=1).astype(BF16)
        for mate in range(2):
            start = (mate * STEPS + step) * rows
            out_ref[start : start + rows, :] = packed[mate * rows : (mate + 1) * rows]


def merge_kernel(part_ref, other_ref, o_ref):
    rows = part_ref.shape[0] // 2
    cols = o_ref.shape[1]
    source = lax.broadcasted_iota(jnp.int32, (DH, DH), 0)
    parts = [
        part_ref[...],
        jnp.concatenate([other_ref[rows:], other_ref[:rows]], axis=0),
    ]
    for head in range(cols // DH):
        lanes = slice(head * DH, (head + 1) * DH)

        def spread(part, first):
            pick = (source >= head * 8 + first) & (source < head * 8 + first + 3)
            return jnp.dot(part[:, cols:], pick.astype(F32).astype(BF16), preferred_element_type=F32)

        tops = [spread(part, 0) for part in parts]
        best = functools.reduce(jnp.maximum, tops)
        scales = [spread(part, 3) * jnp.exp(t - best) for part, t in zip(parts, tops)]
        mixed = sum(s * part[:, lanes].astype(F32) for s, part in zip(scales, parts))
        o_ref[:, lanes] = (mixed / sum(scales)).astype(BF16)


def project_kernel(n_head, n_patch, bit, patch, head, *refs):
    o_ref, w_refs, (out_ref, sums) = refs[0], refs[1 : 1 + PLANE], refs[1 + PLANE :]
    slot = head[0] ^ bit ^ (patch[0] // (n_patch // n_head))
    for near in range(PLANE):
        sums[(patch[0] % PLANE) ^ near] = lax.dot_general(
            o_ref[...], w_refs[near][slot], NT, preferred_element_type=F32
        )
    out = jnp.concatenate([sums[c] for c in range(PLANE)], axis=1)
    out_ref[...] = out.astype(out_ref.dtype)


def gate_kernel(n_patch, patch, ids_ref, mod_ref, *refs):
    sum_refs, (own_out, mate_out) = refs[:-2], refs[-2:]
    total = sum(ref[...].astype(F32) for ref in sum_refs)
    rows, width = total.shape
    each = rows // 2 // STEPS
    second = (patch[0] // PLANE) % 2 == 1
    for step in range(STEPS):
        gate = table_row(mod_ref, 2, ids_ref, step)
        gate = jnp.where(second, gate[:, width:], gate[:, :width])
        for mate, ref in enumerate((own_out, mate_out)):
            start = mate * (rows // 2) + step * each
            ref[step] = (gate * total[start : start + each]).astype(BF16)


def in_hbm(values):
    return pltpu.with_memory_space_constraint(values, pltpu.HBM)


def call(kernel, shapes, ins, scratch=(), flops=0, size=0, limit=16):
    return pl.pallas_call(
        kernel,
        out_shape=shapes,
        in_specs=ins,
        out_specs=jax.tree.map(lambda _: VMEM, shapes),
        scratch_shapes=scratch,
        compiler_params=pltpu.CompilerParams(vmem_limit_bytes=limit * MIB),
        cost_estimate=pl.CostEstimate(flops=flops, bytes_accessed=size, transcendentals=0),
    )


def body(n_patch, n_head, inputs, stale_kv, w_qkv, w_out, mod_table, step_ids, slab_order):
    rows, feats = inputs.shape[1:]
    cols = w_qkv.shape[2]
    piece = w_out.shape[1]
    patch = lax.axis_index("patch").astype(jnp.int32)
    head = lax.axis_index("head").astype(jnp.int32)
    shaped = jax.ShapeDtypeStruct

    x_parts = [swap(inputs, "head", n_head, k) for k in range(1, n_head)]
    mod_parts = [swap(mod_table, "head", n_head, k) for k in range(1, n_head)]
    first = (jnp.transpose(w_qkv, (1, 0, 2)), inputs, jnp.transpose(mod_table, (1, 0, 2)), stale_kv)
    w, x_own, mod_own, stale, ids, cos, sin = call(
        load_kernel,
        (pltpu.VMEM((2, *first[0].shape[1:]), BF16),)
        + tuple(pltpu.VMEM(v.shape, v.dtype) for v in first[1:])
        + (shaped((8, DH), jnp.int32), shaped((rows, DH), F32), shaped((rows, DH), F32)),
        [SMEM] * 2 + [ANY] * len(first),
        [pltpu.SemaphoreType.DMA((5,))],
        size=2 * w_qkv.size,
    )(in_hbm(step_ids), slab_order, *map(in_hbm, first))
    x_parts = [x_own] + x_parts
    mod_parts = [mod_own] + [jnp.transpose(part, (1, 0, 2)) for part in mod_parts]

    def across(values, k):
        return swap(values, "patch", n_patch, k)

    def line_of(values):
        return [values] + [across(values, k) for k in range(2 * PLANE, n_patch, 2 * PLANE)]

    def plane_of(values):
        return [values] + [across(values, k) for k in range(1, PLANE)]

    w_pair = line_of(w_out.T)

    kv_shape = shaped((2, rows, cols), BF16)
    common = (head[None], ids, *x_parts, *mod_parts, w, cos, sin)
    specs = [SMEM] + [VMEM] * (2 * n_head + 4)
    a, kv = call(
        functools.partial(fresh_kernel, n_head),
        (shaped((n_head, rows, feats), BF16), shaped((4, rows, cols), BF16)),
        specs + [VMEM],
        flops=4 * rows * w_qkv.size // 3,
        size=2 * w_qkv.size,
    )(*common, stale)
    q, kv1 = call(
        functools.partial(rest_kernel, n_head),
        (kv_shape, kv_shape),
        specs + [VMEM, ANY],
        [pltpu.VMEM((1, *first[0].shape[1:]), BF16), pltpu.SemaphoreType.DMA],
        8 * rows * w_qkv.size // 3,
        2 * w_qkv.size,
    )(*common, a, in_hbm(first[0]))

    kv_pair = line_of(kv)
    q_mate = across(q, PLANE)
    w_pair, kv_pair, kv1 = lax.optimization_barrier((w_pair, kv_pair, kv1))
    kv_plane = plane_of(jnp.stack(kv_pair))
    w_plane = plane_of(jnp.stack(w_pair))
    tall = 2 * STEPS * rows
    part = call(
        attend_kernel,
        shaped((tall, cols + DH), BF16),
        [VMEM] * (3 + PLANE),
        flops=4 * STEPS * rows * n_patch * rows * cols,
    )(q, q_mate, kv1, *kv_plane)
    o = call(merge_kernel, shaped((tall, cols), BF16), [VMEM] * 2)(part, across(part, PLANE))
    wide = PLANE * piece

    def project(bit, dtype):
        return call(
            functools.partial(project_kernel, n_head, n_patch, bit),
            shaped((tall, wide), dtype),
            [SMEM] * 2 + [VMEM] * (1 + PLANE),
            [pltpu.VMEM((PLANE, tall, piece), F32)],
            2 * tall * wide * cols,
            2 * wide * cols,
        )(patch[None], head[None], o, *w_plane)

    sums = [swap(project(k, BF16), "head", n_head, k) for k in range(1, n_head)]
    sums = [project(0, F32)] + sums
    out_half = shaped((STEPS, rows, wide), BF16)
    out_own, out_mate = call(
        functools.partial(gate_kernel, n_patch),
        (out_half, out_half),
        [SMEM] + [VMEM] * (2 + n_head),
    )(patch[None], ids, mod_own, *sums)
    out_back = across(out_mate, PLANE)
    second = (patch // PLANE) % 2 == 1
    return jnp.concatenate(
        [jnp.where(second, out_back, out_own), jnp.where(second, out_own, out_back)], axis=2
    )


def solution(mesh):
    in_specs = (
        P(None, "patch", "head"),
        P(None, "patch", "head"),
        P(None, None, "head"),
        P("head", "patch"),
        P(None, None, "head"),
        P(),
        P("patch"),
    )
    run = functools.partial(body, mesh.shape["patch"], mesh.shape["head"])
    return jax.shard_map(
        run, mesh=mesh, in_specs=in_specs, out_specs=P(None, "patch", "head"), check_vma=False
    )
```

```python
import functools
import math

import jax
import jax.numpy as jnp
from jax import lax
from jax.experimental import pallas as pl
from jax.experimental.pallas import tpu as pltpu
from jax.sharding import PartitionSpec as P

DH = 128
STEPS = 2
PLANE = 4
MIB = 1024 * 1024
VMEM = pl.BlockSpec(memory_space=pltpu.VMEM)
SMEM = pl.BlockSpec(memory_space=pltpu.SMEM)
ANY = pl.BlockSpec(memory_space=pl.ANY)
BF16, F32 = jnp.bfloat16, jnp.float32
NT = (((1,), (1,)), ((), ()))


def swap(values, axis, count, bit):
    return lax.ppermute(values, axis, [(i, i ^ bit) for i in range(count)])


def load_kernel(ids, slab, w_ref, x_ref, mod_ref, stale_ref, w_out, x_out, mod_out, stale_out, *refs):
    ids_out, cos_ref, sin_ref, sems = refs
    copies = [
        pltpu.make_async_copy(w_ref.at[slot + 1], w_out.at[slot], sems.at[slot])
        for slot in range(2)
    ]
    copies.append(pltpu.make_async_copy(x_ref, x_out, sems.at[2]))
    copies.append(pltpu.make_async_copy(mod_ref, mod_out, sems.at[3]))
    copies.append(pltpu.make_async_copy(stale_ref, stale_out, sems.at[4]))
    for copy in copies:
        copy.start()
    row = lax.broadcasted_iota(jnp.int32, ids_out.shape, 0)
    tile = jnp.zeros(ids_out.shape, jnp.int32)
    for step in range(STEPS):
        tile = jnp.where(row == step, ids[step], tile)
    ids_out[...] = tile
    rows, half = cos_ref.shape[0], DH // 2
    lane = lax.broadcasted_iota(jnp.int32, cos_ref.shape, 1)
    spot = slab[0] * rows + lax.broadcasted_iota(jnp.int32, cos_ref.shape, 0)
    power = jnp.where(lane < half, lane, lane - half).astype(F32) * (-2.0 / DH)
    angle = spot.astype(F32) * jnp.exp(power * math.log(10000.0))
    cos_ref[...] = jnp.cos(angle)
    sin = jnp.sin(angle)
    sin_ref[...] = jnp.where(lane < half, -sin, sin)
    for copy in copies:
        copy.wait()


def table_row(mod_ref, kind, ids_ref, step):
    chosen = ids_ref[step : step + 1, :1]
    table = mod_ref[kind]
    return sum(
        jnp.where(chosen == r, table[r : r + 1], 0.0) for r in range(table.shape[0])
    )


def normalized(step, x_refs, mod_refs, ids_ref):
    hidden = [ref[step].astype(F32) for ref in x_refs]
    width = sum(part.shape[1] for part in hidden)
    mean = sum(jnp.sum(part, axis=1, keepdims=True) for part in hidden) / width
    square = sum(jnp.sum(part * part, axis=1, keepdims=True) for part in hidden) / width
    inv = lax.rsqrt(square - mean * mean + 1e-06)
    parts = []
    for part, mod_ref in zip(hidden, mod_refs):
        shift = table_row(mod_ref, 0, ids_ref, step)
        scale = table_row(mod_ref, 1, ids_ref, step)
        parts.append(((part - mean) * inv * (1.0 + scale) + shift).astype(BF16))
    return parts


def projected(parts, w_ref, slot, head):
    feats = parts[0].shape[1]
    total = jnp.zeros((parts[0].shape[0], w_ref.shape[2]), F32)
    for number, part in enumerate(parts):
        start = pl.multiple_of((head[0] ^ number) * feats, feats)
        w = w_ref[slot, pl.ds(start, feats), :]
        total += jnp.dot(part, w, preferred_element_type=F32)
    return total


def rotated(values, cos, sin):
    blocks = []
    for start in range(0, values.shape[1], DH):
        u = values[:, start : start + DH]
        blocks.append(u * cos + pltpu.roll(u, DH // 2, 1) * sin)
    return jnp.concatenate(blocks, axis=1)


def fresh_kernel(n_head, head, ids_ref, *refs):
    x_refs, mod_refs = refs[:n_head], refs[n_head : 2 * n_head]
    w_ref, cos_ref, sin_ref = refs[2 * n_head : 2 * n_head + 3]
    stale_ref, a_ref, kv_ref = refs[2 * n_head + 3 :]
    kv_ref[:2] = stale_ref[...]
    parts = normalized(0, x_refs, mod_refs, ids_ref)
    for number, part in enumerate(parts):
        a_ref[number] = part
    keys = rotated(projected(parts, w_ref, 0, head), cos_ref[...], sin_ref[...])
    kv_ref[2] = keys.astype(BF16)
    kv_ref[3] = projected(parts, w_ref, 1, head).astype(BF16)


def rest_kernel(n_head, head, ids_ref, *refs):
    x_refs, mod_refs = refs[:n_head], refs[n_head : 2 * n_head]
    w_ref, cos_ref, sin_ref, a_ref, w_far, q_ref, kv1_ref, wq_ref, sem = refs[2 * n_head :]
    copy = pltpu.make_async_copy(w_far.at[0], wq_ref.at[0], sem)
    copy.start()
    rows = a_ref.shape[1]
    parts = normalized(1, x_refs, mod_refs, ids_ref)
    cos, sin = cos_ref[...], sin_ref[...]
    both = [jnp.concatenate([a_ref[k], part], axis=0) for k, part in enumerate(parts)]
    kv1_ref[0] = rotated(projected(parts, w_ref, 0, head), cos, sin).astype(BF16)
    kv1_ref[1] = projected(parts, w_ref, 1, head).astype(BF16)
    copy.wait()
    queries = projected(both, wq_ref, 0, head)
    for step in range(STEPS):
        spot = slice(step * rows, (step + 1) * rows)
        q_ref[step] = rotated(queries[spot], cos, sin).astype(BF16)


def split3(values):
    high = values.astype(BF16).astype(F32)
    middle = (values - high).astype(BF16).astype(F32)
    return [high, middle, values - high - middle]


def attend_kernel(q_ref, mate_ref, kv1_ref, *refs):
    kv_refs, out_ref = refs[:PLANE], refs[PLANE]
    blocks, _, rows, cols = kv_refs[0].shape
    old_rows = PLANE * blocks * rows
    shape = (2 * rows, old_rows + rows)
    mine = lax.broadcasted_iota(jnp.int32, shape, 0) < rows
    stray = jnp.where(mine, 0, PLANE * blocks)
    drop = lax.broadcasted_iota(jnp.int32, shape, 1) // rows == stray
    lane = lax.broadcasted_iota(jnp.int32, (2 * rows, DH), 1)
    for step in range(STEPS):
        fresh = (kv_refs[0].at[0, 2:], kv1_ref)[step]
        stats = jnp.zeros((2 * rows, DH), F32)
        mixed = []
        for head in range(cols // DH):
            lanes = slice(head * DH, (head + 1) * DH)

            def rows_of(kind):
                old = [ref[:, 2 * step + kind, :, lanes].reshape(blocks * rows, DH) for ref in kv_refs]
                return jnp.concatenate([*old, fresh[kind, :, lanes]], axis=0)

            queries = jnp.concatenate([q_ref[step, :, lanes], mate_ref[step, :, lanes]], axis=0)
            scores = lax.dot_general(queries, rows_of(0), NT, preferred_element_type=F32)
            scores = jnp.where(drop, -1e30, scores * (1.0 / math.sqrt(DH)))
            top = jnp.max(scores, axis=1, keepdims=True)
            weights = jnp.exp(scores - top)
            totals = jnp.sum(weights, axis=1, keepdims=True)
            mixed.append(
                jnp.dot(weights.astype(BF16), rows_of(1), preferred_element_type=F32) / totals
            )
            for place, piece in enumerate(split3(top) + split3(totals)):
                stats = jnp.where(lane == head * 8 + place, piece, stats)
        packed = jnp.concatenate([*mixed, stats], axis=1).astype(BF16)
        for mate in range(2):
            start = (mate * STEPS + step) * rows
            out_ref[start : start + rows, :] = packed[mate * rows : (mate + 1) * rows]


def merge_kernel(part_ref, other_ref, o_ref):
    rows = part_ref.shape[0] // 2
    cols = o_ref.shape[1]
    source = lax.broadcasted_iota(jnp.int32, (DH, DH), 0)
    parts = [
        part_ref[...],
        jnp.concatenate([other_ref[rows:], other_ref[:rows]], axis=0),
    ]
    for head in range(cols // DH):
        lanes = slice(head * DH, (head + 1) * DH)

        def spread(part, first):
            pick = (source >= head * 8 + first) & (source < head * 8 + first + 3)
            return jnp.dot(part[:, cols:], pick.astype(F32).astype(BF16), preferred_element_type=F32)

        tops = [spread(part, 0) for part in parts]
        best = functools.reduce(jnp.maximum, tops)
        scales = [spread(part, 3) * jnp.exp(t - best) for part, t in zip(parts, tops)]
        mixed = sum(s * part[:, lanes].astype(F32) for s, part in zip(scales, parts))
        o_ref[:, lanes] = (mixed / sum(scales)).astype(BF16)


def project_kernel(n_head, n_patch, bit, patch, head, *refs):
    o_ref, w_refs, (out_ref, sums) = refs[0], refs[1 : 1 + PLANE], refs[1 + PLANE :]
    slot = head[0] ^ bit ^ (patch[0] // (n_patch // n_head))
    for near in range(PLANE):
        sums[(patch[0] % PLANE) ^ near] = lax.dot_general(
            o_ref[...], w_refs[near][slot], NT, preferred_element_type=F32
        )
    out = jnp.concatenate([sums[c] for c in range(PLANE)], axis=1)
    out_ref[...] = out.astype(out_ref.dtype)


def gate_kernel(n_patch, patch, ids_ref, mod_ref, *refs):
    sum_refs, (own_out, mate_out) = refs[:-2], refs[-2:]
    total = sum(ref[...].astype(F32) for ref in sum_refs)
    rows, width = total.shape
    each = rows // 2 // STEPS
    second = (patch[0] // PLANE) % 2 == 1
    for step in range(STEPS):
        gate = table_row(mod_ref, 2, ids_ref, step)
        gate = jnp.where(second, gate[:, width:], gate[:, :width])
        for mate, ref in enumerate((own_out, mate_out)):
            start = mate * (rows // 2) + step * each
            ref[step] = (gate * total[start : start + each]).astype(BF16)


def in_hbm(values):
    return pltpu.with_memory_space_constraint(values, pltpu.HBM)


def call(kernel, shapes, ins, scratch=(), flops=0, size=0, limit=16):
    return pl.pallas_call(
        kernel,
        out_shape=shapes,
        in_specs=ins,
        out_specs=jax.tree.map(lambda _: VMEM, shapes),
        scratch_shapes=scratch,
        compiler_params=pltpu.CompilerParams(vmem_limit_bytes=limit * MIB),
        cost_estimate=pl.CostEstimate(flops=flops, bytes_accessed=size, transcendentals=0),
    )


def body(n_patch, n_head, inputs, stale_kv, w_qkv, w_out, mod_table, step_ids, slab_order):
    rows, feats = inputs.shape[1:]
    cols = w_qkv.shape[2]
    piece = w_out.shape[1]
    patch = lax.axis_index("patch").astype(jnp.int32)
    head = lax.axis_index("head").astype(jnp.int32)
    shaped = jax.ShapeDtypeStruct

    x_parts = [swap(inputs, "head", n_head, k) for k in range(1, n_head)]
    mod_parts = [swap(mod_table, "head", n_head, k) for k in range(1, n_head)]
    first = (jnp.transpose(w_qkv, (1, 0, 2)), inputs, jnp.transpose(mod_table, (1, 0, 2)), stale_kv)
    w, x_own, mod_own, stale, ids, cos, sin = call(
        load_kernel,
        (pltpu.VMEM((2, *first[0].shape[1:]), BF16),)
        + tuple(pltpu.VMEM(v.shape, v.dtype) for v in first[1:])
        + (shaped((8, DH), jnp.int32), shaped((rows, DH), F32), shaped((rows, DH), F32)),
        [SMEM] * 2 + [ANY] * len(first),
        [pltpu.SemaphoreType.DMA((5,))],
        size=2 * w_qkv.size,
    )(in_hbm(step_ids), slab_order, *map(in_hbm, first))
    x_parts = [x_own] + x_parts
    mod_parts = [mod_own] + [jnp.transpose(part, (1, 0, 2)) for part in mod_parts]

    def across(values, k):
        return swap(values, "patch", n_patch, k)

    def line_of(values):
        return [values] + [across(values, k) for k in range(2 * PLANE, n_patch, 2 * PLANE)]

    def plane_of(values):
        return [values] + [across(values, k) for k in range(1, PLANE)]

    w_own, *w_rest = line_of(w_out.T)
    w_x = across(w_own, 1)

    kv_shape = shaped((2, rows, cols), BF16)
    common = (head[None], ids, *x_parts, *mod_parts, w, cos, sin)
    specs = [SMEM] + [VMEM] * (2 * n_head + 4)
    a, kv = call(
        functools.partial(fresh_kernel, n_head),
        (shaped((n_head, rows, feats), BF16), shaped((4, rows, cols), BF16)),
        specs + [VMEM],
        flops=4 * rows * w_qkv.size // 3,
        size=2 * w_qkv.size,
    )(*common, stale)
    q, kv1 = call(
        functools.partial(rest_kernel, n_head),
        (kv_shape, kv_shape),
        specs + [VMEM, ANY],
        [pltpu.VMEM((1, *first[0].shape[1:]), BF16), pltpu.SemaphoreType.DMA],
        8 * rows * w_qkv.size // 3,
        2 * w_qkv.size,
    )(*common, a, in_hbm(first[0]))

    kv_pair = line_of(kv)
    q_mate = across(q, PLANE)
    w_own, w_x, w_rest, kv = lax.optimization_barrier((w_own, w_x, w_rest, kv))
    w_y = across(jnp.stack([w_own, w_x]), 2)
    w_rest = jnp.stack(w_rest)
    rest_y = across(w_rest, 2)
    kv_pair, q_mate = lax.optimization_barrier((kv_pair, q_mate))
    kv_plane = plane_of(jnp.stack(kv_pair))
    w_y, rest_y, kv_plane[1] = lax.optimization_barrier((w_y, rest_y, kv_plane[1]))
    rest_x = across(jnp.stack([w_rest, rest_y]), 1)
    tall = 2 * STEPS * rows
    part = call(
        attend_kernel,
        shaped((tall, cols + DH), BF16),
        [VMEM] * (3 + PLANE),
        flops=4 * STEPS * rows * n_patch * rows * cols,
    )(q, q_mate, kv1, *kv_plane)
    o = call(merge_kernel, shaped((tall, cols), BF16), [VMEM] * 2)(part, across(part, PLANE))
    o, w_y, rest_x = lax.optimization_barrier((o, w_y, rest_x))
    near = [(w_own, w_rest), (w_x, rest_x[0]), (w_y[0], rest_y), (w_y[1], rest_x[1])]
    w_plane = [jnp.concatenate([first[None], others]) for first, others in near]
    wide = PLANE * piece

    def project(bit, dtype):
        return call(
            functools.partial(project_kernel, n_head, n_patch, bit),
            shaped((tall, wide), dtype),
            [SMEM] * 2 + [VMEM] * (1 + PLANE),
            [pltpu.VMEM((PLANE, tall, piece), F32)],
            2 * tall * wide * cols,
            2 * wide * cols,
        )(patch[None], head[None], o, *w_plane)

    sums = [swap(project(k, BF16), "head", n_head, k) for k in range(1, n_head)]
    sums = [project(0, F32)] + sums
    out_half = shaped((STEPS, rows, wide), BF16)
    out_own, out_mate = call(
        functools.partial(gate_kernel, n_patch),
        (out_half, out_half),
        [SMEM] + [VMEM] * (2 + n_head),
    )(patch[None], ids, mod_own, *sums)
    out_back = across(out_mate, PLANE)
    second = (patch // PLANE) % 2 == 1
    return jnp.concatenate(
        [jnp.where(second, out_back, out_own), jnp.where(second, out_own, out_back)], axis=2
    )


def solution(mesh):
    in_specs = (
        P(None, "patch", "head"),
        P(None, "patch", "head"),
        P(None, None, "head"),
        P("head", "patch"),
        P(None, None, "head"),
        P(),
        P("patch"),
    )
    run = functools.partial(body, mesh.shape["patch"], mesh.shape["head"])
    return jax.shard_map(
        run, mesh=mesh, in_specs=in_specs, out_specs=P(None, "patch", "head"), check_vma=False
    )
```

```python
import functools
import math

import jax
import jax.numpy as jnp
from jax import lax
from jax.experimental import pallas as pl
from jax.experimental.pallas import tpu as pltpu
from jax.sharding import PartitionSpec as P

DH = 128
STEPS = 2
PLANE = 4
MIB = 1024 * 1024
VMEM = pl.BlockSpec(memory_space=pltpu.VMEM)
SMEM = pl.BlockSpec(memory_space=pltpu.SMEM)
ANY = pl.BlockSpec(memory_space=pl.ANY)
BF16, F32 = jnp.bfloat16, jnp.float32
NT = (((1,), (1,)), ((), ()))


def swap(values, axis, count, bit):
    return lax.ppermute(values, axis, [(i, i ^ bit) for i in range(count)])


def load_kernel(ids, slab, w_ref, x_ref, mod_ref, stale_ref, w_out, x_out, mod_out, stale_out, *refs):
    ids_out, cos_ref, sin_ref, sems = refs
    copies = [
        pltpu.make_async_copy(w_ref.at[slot], w_out.at[slot], sems.at[slot])
        for slot in range(3)
    ]
    copies.append(pltpu.make_async_copy(x_ref, x_out, sems.at[3]))
    copies.append(pltpu.make_async_copy(mod_ref, mod_out, sems.at[4]))
    copies.append(pltpu.make_async_copy(stale_ref, stale_out, sems.at[5]))
    for copy in copies:
        copy.start()
    row = lax.broadcasted_iota(jnp.int32, ids_out.shape, 0)
    tile = jnp.zeros(ids_out.shape, jnp.int32)
    for step in range(STEPS):
        tile = jnp.where(row == step, ids[step], tile)
    ids_out[...] = tile
    rows, half = cos_ref.shape[0], DH // 2
    lane = lax.broadcasted_iota(jnp.int32, cos_ref.shape, 1)
    spot = slab[0] * rows + lax.broadcasted_iota(jnp.int32, cos_ref.shape, 0)
    power = jnp.where(lane < half, lane, lane - half).astype(F32) * (-2.0 / DH)
    angle = spot.astype(F32) * jnp.exp(power * math.log(10000.0))
    cos_ref[...] = jnp.cos(angle)
    sin = jnp.sin(angle)
    sin_ref[...] = jnp.where(lane < half, -sin, sin)
    for copy in copies:
        copy.wait()


def table_row(mod_ref, kind, ids_ref, step):
    chosen = ids_ref[step : step + 1, :1]
    table = mod_ref[kind]
    return sum(
        jnp.where(chosen == r, table[r : r + 1], 0.0) for r in range(table.shape[0])
    )


def normalized(step, x_refs, mod_refs, ids_ref):
    hidden = [ref[step].astype(F32) for ref in x_refs]
    width = sum(part.shape[1] for part in hidden)
    mean = sum(jnp.sum(part, axis=1, keepdims=True) for part in hidden) / width
    square = sum(jnp.sum(part * part, axis=1, keepdims=True) for part in hidden) / width
    inv = lax.rsqrt(square - mean * mean + 1e-06)
    parts = []
    for part, mod_ref in zip(hidden, mod_refs):
        shift = table_row(mod_ref, 0, ids_ref, step)
        scale = table_row(mod_ref, 1, ids_ref, step)
        parts.append(((part - mean) * inv * (1.0 + scale) + shift).astype(BF16))
    return parts


def projected(parts, w_ref, slot, head):
    feats = parts[0].shape[1]
    total = jnp.zeros((parts[0].shape[0], w_ref.shape[2]), F32)
    for number, part in enumerate(parts):
        start = pl.multiple_of((head[0] ^ number) * feats, feats)
        w = w_ref[slot, pl.ds(start, feats), :]
        total += jnp.dot(part, w, preferred_element_type=F32)
    return total


def rotated(values, cos, sin):
    blocks = []
    for start in range(0, values.shape[1], DH):
        u = values[:, start : start + DH]
        blocks.append(u * cos + pltpu.roll(u, DH // 2, 1) * sin)
    return jnp.concatenate(blocks, axis=1)


def qkv_kernel(n_head, head, ids_ref, *refs):
    x_refs, mod_refs = refs[:n_head], refs[n_head : 2 * n_head]
    w_ref, cos_ref, sin_ref, stale_ref, q_ref, kv_ref, kv1_ref = refs[2 * n_head :]
    rows = x_refs[0].shape[1]
    steps = [normalized(step, x_refs, mod_refs, ids_ref) for step in range(STEPS)]
    parts = [jnp.concatenate(pair, axis=0) for pair in zip(*steps)]
    cos = jnp.concatenate([cos_ref[...]] * STEPS, axis=0)
    sin = jnp.concatenate([sin_ref[...]] * STEPS, axis=0)
    queries = rotated(projected(parts, w_ref, 0, head), cos, sin).astype(BF16)
    keys = rotated(projected(parts, w_ref, 1, head), cos, sin).astype(BF16)
    values = projected(parts, w_ref, 2, head).astype(BF16)
    for step in range(STEPS):
        spot = slice(step * rows, (step + 1) * rows)
        q_ref[step] = queries[spot]
    kv_ref[:2] = stale_ref[...]
    kv_ref[2], kv_ref[3] = keys[:rows], values[:rows]
    kv1_ref[0], kv1_ref[1] = keys[rows:], values[rows:]


def split3(values):
    high = values.astype(BF16).astype(F32)
    middle = (values - high).astype(BF16).astype(F32)
    return [high, middle, values - high - middle]


def attend_kernel(q_ref, mate_ref, kv1_ref, *refs):
    kv_refs, out_ref = refs[:PLANE], refs[PLANE]
    blocks, _, rows, cols = kv_refs[0].shape
    old_rows = PLANE * blocks * rows
    shape = (2 * rows, old_rows + rows)
    mine = lax.broadcasted_iota(jnp.int32, shape, 0) < rows
    stray = jnp.where(mine, 0, PLANE * blocks)
    drop = lax.broadcasted_iota(jnp.int32, shape, 1) // rows == stray
    lane = lax.broadcasted_iota(jnp.int32, (2 * rows, DH), 1)
    for step in range(STEPS):
        fresh = (kv_refs[0].at[0, 2:], kv1_ref)[step]
        stats = jnp.zeros((2 * rows, DH), F32)
        mixed = []
        for head in range(cols // DH):
            lanes = slice(head * DH, (head + 1) * DH)

            def rows_of(kind):
                old = [ref[:, 2 * step + kind, :, lanes].reshape(blocks * rows, DH) for ref in kv_refs]
                return jnp.concatenate([*old, fresh[kind, :, lanes]], axis=0)

            queries = jnp.concatenate([q_ref[step, :, lanes], mate_ref[step, :, lanes]], axis=0)
            scores = lax.dot_general(queries, rows_of(0), NT, preferred_element_type=F32)
            scores = jnp.where(drop, -1e30, scores * (1.0 / math.sqrt(DH)))
            top = jnp.max(scores, axis=1, keepdims=True)
            weights = jnp.exp(scores - top)
            totals = jnp.sum(weights, axis=1, keepdims=True)
            mixed.append(
                jnp.dot(weights.astype(BF16), rows_of(1), preferred_element_type=F32) / totals
            )
            for place, piece in enumerate(split3(top) + split3(totals)):
                stats = jnp.where(lane == head * 8 + place, piece, stats)
        packed = jnp.concatenate([*mixed, stats], axis=1).astype(BF16)
        for mate in range(2):
            start = (mate * STEPS + step) * rows
            out_ref[start : start + rows, :] = packed[mate * rows : (mate + 1) * rows]


def merge_kernel(part_ref, other_ref, o_ref):
    rows = part_ref.shape[0] // 2
    cols = o_ref.shape[1]
    source = lax.broadcasted_iota(jnp.int32, (DH, DH), 0)
    parts = [
        part_ref[...],
        jnp.concatenate([other_ref[rows:], other_ref[:rows]], axis=0),
    ]
    for head in range(cols // DH):
        lanes = slice(head * DH, (head + 1) * DH)

        def spread(part, first):
            pick = (source >= head * 8 + first) & (source < head * 8 + first + 3)
            return jnp.dot(part[:, cols:], pick.astype(F32).astype(BF16), preferred_element_type=F32)

        tops = [spread(part, 0) for part in parts]
        best = functools.reduce(jnp.maximum, tops)
        scales = [spread(part, 3) * jnp.exp(t - best) for part, t in zip(parts, tops)]
        mixed = sum(s * part[:, lanes].astype(F32) for s, part in zip(scales, parts))
        o_ref[:, lanes] = (mixed / sum(scales)).astype(BF16)


def project_kernel(n_head, n_patch, bit, patch, head, *refs):
    o_ref, w_refs, (out_ref, sums) = refs[0], refs[1 : 1 + PLANE], refs[1 + PLANE :]
    slot = head[0] ^ bit ^ (patch[0] // (n_patch // n_head))
    for near in range(PLANE):
        sums[(patch[0] % PLANE) ^ near] = lax.dot_general(
            o_ref[...], w_refs[near][slot], NT, preferred_element_type=F32
        )
    out = jnp.concatenate([sums[c] for c in range(PLANE)], axis=1)
    out_ref[...] = out.astype(out_ref.dtype)


def gate_kernel(n_patch, patch, ids_ref, mod_ref, *refs):
    sum_refs, (own_out, mate_out) = refs[:-2], refs[-2:]
    total = sum(ref[...].astype(F32) for ref in sum_refs)
    rows, width = total.shape
    each = rows // 2 // STEPS
    second = (patch[0] // PLANE) % 2 == 1
    for step in range(STEPS):
        gate = table_row(mod_ref, 2, ids_ref, step)
        gate = jnp.where(second, gate[:, width:], gate[:, :width])
        for mate, ref in enumerate((own_out, mate_out)):
            start = mate * (rows // 2) + step * each
            ref[step] = (gate * total[start : start + each]).astype(BF16)


def in_hbm(values):
    return pltpu.with_memory_space_constraint(values, pltpu.HBM)


def call(kernel, shapes, ins, scratch=(), flops=0, size=0, limit=16):
    return pl.pallas_call(
        kernel,
        out_shape=shapes,
        in_specs=ins,
        out_specs=jax.tree.map(lambda _: VMEM, shapes),
        scratch_shapes=scratch,
        compiler_params=pltpu.CompilerParams(vmem_limit_bytes=limit * MIB),
        cost_estimate=pl.CostEstimate(flops=flops, bytes_accessed=size, transcendentals=0),
    )


def body(n_patch, n_head, inputs, stale_kv, w_qkv, w_out, mod_table, step_ids, slab_order):
    rows, feats = inputs.shape[1:]
    cols = w_qkv.shape[2]
    piece = w_out.shape[1]
    patch = lax.axis_index("patch").astype(jnp.int32)
    head = lax.axis_index("head").astype(jnp.int32)
    shaped = jax.ShapeDtypeStruct

    x_parts = [swap(inputs, "head", n_head, k) for k in range(1, n_head)]
    mod_parts = [swap(mod_table, "head", n_head, k) for k in range(1, n_head)]
    first = (jnp.transpose(w_qkv, (1, 0, 2)), inputs, jnp.transpose(mod_table, (1, 0, 2)), stale_kv)
    w, x_own, mod_own, stale, ids, cos, sin = call(
        load_kernel,
        tuple(pltpu.VMEM(v.shape, v.dtype) for v in first)
        + (shaped((8, DH), jnp.int32), shaped((rows, DH), F32), shaped((rows, DH), F32)),
        [SMEM] * 2 + [ANY] * len(first),
        [pltpu.SemaphoreType.DMA((6,))],
        size=2 * w_qkv.size,
    )(in_hbm(step_ids), slab_order, *map(in_hbm, first))
    x_parts = [x_own] + x_parts
    mod_parts = [mod_own] + [jnp.transpose(part, (1, 0, 2)) for part in mod_parts]

    def across(values, k):
        return swap(values, "patch", n_patch, k)

    def line_of(values):
        return [values] + [across(values, k) for k in range(2 * PLANE, n_patch, 2 * PLANE)]

    def plane_of(values):
        return [values] + [across(values, k) for k in range(1, PLANE)]


    kv_shape = shaped((2, rows, cols), BF16)
    q, kv, kv1 = call(
        functools.partial(qkv_kernel, n_head),
        (kv_shape, shaped((4, rows, cols), BF16), kv_shape),
        [SMEM] + [VMEM] * (2 * n_head + 5),
        flops=2 * STEPS * rows * w_qkv.size,
        size=2 * w_qkv.size,
    )(head[None], ids, *x_parts, *mod_parts, w, cos, sin, stale)

    w_own, kv = lax.optimization_barrier((w_out.T, kv))
    kv_pair = line_of(kv)
    q_mate = across(q, PLANE)
    w_x = across(w_own, 1)
    w_rest = jnp.stack(line_of(w_own)[1:])
    kv_plane = plane_of(jnp.stack(kv_pair))
    w_x, w_rest, q_mate = lax.optimization_barrier((w_x, w_rest, q_mate))
    w_y = across(jnp.stack([w_own, w_x]), 2)
    rest_y = across(w_rest, 2)
    rest_y, *kv_plane[1:] = lax.optimization_barrier((rest_y, *kv_plane[1:]))
    rest_x = across(jnp.stack([w_rest, rest_y]), 1)
    tall = 2 * STEPS * rows
    part = call(
        attend_kernel,
        shaped((tall, cols + DH), BF16),
        [VMEM] * (3 + PLANE),
        flops=4 * STEPS * rows * n_patch * rows * cols,
    )(q, q_mate, kv1, *kv_plane)
    o = call(merge_kernel, shaped((tall, cols), BF16), [VMEM] * 2)(part, across(part, PLANE))
    o, w_y, rest_x = lax.optimization_barrier((o, w_y, rest_x))
    near = [(w_own, w_rest), (w_x, rest_x[0]), (w_y[0], rest_y), (w_y[1], rest_x[1])]
    w_plane = [jnp.concatenate([first[None], others]) for first, others in near]
    wide = PLANE * piece

    def project(bit, dtype):
        return call(
            functools.partial(project_kernel, n_head, n_patch, bit),
            shaped((tall, wide), dtype),
            [SMEM] * 2 + [VMEM] * (1 + PLANE),
            [pltpu.VMEM((PLANE, tall, piece), F32)],
            2 * tall * wide * cols,
            2 * wide * cols,
        )(patch[None], head[None], o, *w_plane)

    sums = [swap(project(k, BF16), "head", n_head, k) for k in range(1, n_head)]
    sums = [project(0, F32)] + sums
    out_half = shaped((STEPS, rows, wide), BF16)
    out_own, out_mate = call(
        functools.partial(gate_kernel, n_patch),
        (out_half, out_half),
        [SMEM] + [VMEM] * (2 + n_head),
    )(patch[None], ids, mod_own, *sums)
    out_back = across(out_mate, PLANE)
    second = (patch // PLANE) % 2 == 1
    return jnp.concatenate(
        [jnp.where(second, out_back, out_own), jnp.where(second, out_own, out_back)], axis=2
    )


def solution(mesh):
    in_specs = (
        P(None, "patch", "head"),
        P(None, "patch", "head"),
        P(None, None, "head"),
        P("head", "patch"),
        P(None, None, "head"),
        P(),
        P("patch"),
    )
    run = functools.partial(body, mesh.shape["patch"], mesh.shape["head"])
    return jax.shard_map(
        run, mesh=mesh, in_specs=in_specs, out_specs=P(None, "patch", "head"), check_vma=False
    )
```

```python
import functools
import math

import jax
import jax.numpy as jnp
from jax import lax
from jax.experimental import pallas as pl
from jax.experimental.pallas import tpu as pltpu
from jax.sharding import PartitionSpec as P

DH = 128
STEPS = 2
PLANE = 4
MIB = 1024 * 1024
VMEM = pl.BlockSpec(memory_space=pltpu.VMEM)
SMEM = pl.BlockSpec(memory_space=pltpu.SMEM)
ANY = pl.BlockSpec(memory_space=pl.ANY)
BF16, F32 = jnp.bfloat16, jnp.float32
NT = (((1,), (1,)), ((), ()))


def swap(values, axis, count, bit):
    return lax.ppermute(values, axis, [(i, i ^ bit) for i in range(count)])


def load_kernel(ids, slab, w_ref, x_ref, mod_ref, stale_ref, w_out, x_out, mod_out, stale_out, *refs):
    ids_out, cos_ref, sin_ref, sems = refs
    copies = [
        pltpu.make_async_copy(w_ref.at[slot], w_out.at[slot], sems.at[slot])
        for slot in range(3)
    ]
    copies.append(pltpu.make_async_copy(x_ref, x_out, sems.at[3]))
    copies.append(pltpu.make_async_copy(mod_ref, mod_out, sems.at[4]))
    copies.append(pltpu.make_async_copy(stale_ref, stale_out, sems.at[5]))
    for copy in copies:
        copy.start()
    row = lax.broadcasted_iota(jnp.int32, ids_out.shape, 0)
    tile = jnp.zeros(ids_out.shape, jnp.int32)
    for step in range(STEPS):
        tile = jnp.where(row == step, ids[step], tile)
    ids_out[...] = tile
    rows, half = cos_ref.shape[0], DH // 2
    lane = lax.broadcasted_iota(jnp.int32, cos_ref.shape, 1)
    spot = slab[0] * rows + lax.broadcasted_iota(jnp.int32, cos_ref.shape, 0)
    power = jnp.where(lane < half, lane, lane - half).astype(F32) * (-2.0 / DH)
    angle = spot.astype(F32) * jnp.exp(power * math.log(10000.0))
    cos_ref[...] = jnp.cos(angle)
    sin = jnp.sin(angle)
    sin_ref[...] = jnp.where(lane < half, -sin, sin)
    for copy in copies:
        copy.wait()


def table_row(mod_ref, kind, ids_ref, step):
    chosen = ids_ref[step : step + 1, :1]
    table = mod_ref[kind]
    return sum(
        jnp.where(chosen == r, table[r : r + 1], 0.0) for r in range(table.shape[0])
    )


def normalized(step, x_refs, mod_refs, ids_ref):
    hidden = [ref[step].astype(F32) for ref in x_refs]
    width = sum(part.shape[1] for part in hidden)
    mean = sum(jnp.sum(part, axis=1, keepdims=True) for part in hidden) / width
    square = sum(jnp.sum(part * part, axis=1, keepdims=True) for part in hidden) / width
    inv = lax.rsqrt(square - mean * mean + 1e-06)
    parts = []
    for part, mod_ref in zip(hidden, mod_refs):
        shift = table_row(mod_ref, 0, ids_ref, step)
        scale = table_row(mod_ref, 1, ids_ref, step)
        parts.append(((part - mean) * inv * (1.0 + scale) + shift).astype(BF16))
    return parts


def projected(parts, w_ref, slot, head):
    feats = parts[0].shape[1]
    total = jnp.zeros((parts[0].shape[0], w_ref.shape[2]), F32)
    for number, part in enumerate(parts):
        start = pl.multiple_of((head[0] ^ number) * feats, feats)
        w = w_ref[slot, pl.ds(start, feats), :]
        total += jnp.dot(part, w, preferred_element_type=F32)
    return total


def rotated(values, cos, sin):
    blocks = []
    for start in range(0, values.shape[1], DH):
        u = values[:, start : start + DH]
        blocks.append(u * cos + pltpu.roll(u, DH // 2, 1) * sin)
    return jnp.concatenate(blocks, axis=1)


def qkv_kernel(n_head, head, ids_ref, *refs):
    x_refs, mod_refs = refs[:n_head], refs[n_head : 2 * n_head]
    w_ref, cos_ref, sin_ref, stale_ref, q_ref, kv_ref, kv1_ref = refs[2 * n_head :]
    rows = x_refs[0].shape[1]
    steps = [normalized(step, x_refs, mod_refs, ids_ref) for step in range(STEPS)]
    parts = [jnp.concatenate(pair, axis=0) for pair in zip(*steps)]
    cos = jnp.concatenate([cos_ref[...]] * STEPS, axis=0)
    sin = jnp.concatenate([sin_ref[...]] * STEPS, axis=0)
    queries = rotated(projected(parts, w_ref, 0, head), cos, sin).astype(BF16)
    keys = rotated(projected(parts, w_ref, 1, head), cos, sin).astype(BF16)
    values = projected(parts, w_ref, 2, head).astype(BF16)
    for step in range(STEPS):
        spot = slice(step * rows, (step + 1) * rows)
        q_ref[step] = queries[spot]
    kv_ref[:2] = stale_ref[...]
    kv_ref[2], kv_ref[3] = keys[:rows], values[:rows]
    kv1_ref[0], kv1_ref[1] = keys[rows:], values[rows:]


def split3(values):
    high = values.astype(BF16).astype(F32)
    middle = (values - high).astype(BF16).astype(F32)
    return [high, middle, values - high - middle]


def attend_kernel(q_ref, mate_ref, kv1_ref, *refs):
    kv_refs, out_ref = refs[:PLANE], refs[PLANE]
    blocks, _, rows, cols = kv_refs[0].shape
    old_rows = PLANE * blocks * rows
    shape = (2 * rows, old_rows + rows)
    mine = lax.broadcasted_iota(jnp.int32, shape, 0) < rows
    stray = jnp.where(mine, 0, PLANE * blocks)
    drop = lax.broadcasted_iota(jnp.int32, shape, 1) // rows == stray
    lane = lax.broadcasted_iota(jnp.int32, (2 * rows, DH), 1)
    for step in range(STEPS):
        fresh = (kv_refs[0].at[0, 2:], kv1_ref)[step]
        stats = jnp.zeros((2 * rows, DH), F32)
        mixed = []
        for head in range(cols // DH):
            lanes = slice(head * DH, (head + 1) * DH)

            def rows_of(kind):
                old = [ref[:, 2 * step + kind, :, lanes].reshape(blocks * rows, DH) for ref in kv_refs]
                return jnp.concatenate([*old, fresh[kind, :, lanes]], axis=0)

            queries = jnp.concatenate([q_ref[step, :, lanes], mate_ref[step, :, lanes]], axis=0)
            scores = lax.dot_general(queries, rows_of(0), NT, preferred_element_type=F32)
            scores = jnp.where(drop, -1e30, scores * (1.0 / math.sqrt(DH)))
            top = jnp.max(scores, axis=1, keepdims=True)
            weights = jnp.exp(scores - top)
            totals = jnp.sum(weights, axis=1, keepdims=True)
            mixed.append(
                jnp.dot(weights.astype(BF16), rows_of(1), preferred_element_type=F32) / totals
            )
            for place, piece in enumerate(split3(top) + split3(totals)):
                stats = jnp.where(lane == head * 8 + place, piece, stats)
        packed = jnp.concatenate([*mixed, stats], axis=1).astype(BF16)
        for mate in range(2):
            start = (mate * STEPS + step) * rows
            out_ref[start : start + rows, :] = packed[mate * rows : (mate + 1) * rows]


def merge_kernel(part_ref, other_ref, o_ref):
    rows = part_ref.shape[0] // 2
    cols = o_ref.shape[1]
    source = lax.broadcasted_iota(jnp.int32, (DH, DH), 0)
    parts = [
        part_ref[...],
        jnp.concatenate([other_ref[rows:], other_ref[:rows]], axis=0),
    ]
    for head in range(cols // DH):
        lanes = slice(head * DH, (head + 1) * DH)

        def spread(part, first):
            pick = (source >= head * 8 + first) & (source < head * 8 + first + 3)
            return jnp.dot(part[:, cols:], pick.astype(F32).astype(BF16), preferred_element_type=F32)

        tops = [spread(part, 0) for part in parts]
        best = functools.reduce(jnp.maximum, tops)
        scales = [spread(part, 3) * jnp.exp(t - best) for part, t in zip(parts, tops)]
        mixed = sum(s * part[:, lanes].astype(F32) for s, part in zip(scales, parts))
        o_ref[:, lanes] = (mixed / sum(scales)).astype(BF16)


def project_kernel(n_head, n_patch, bit, patch, head, *refs):
    o_ref, w_refs, (out_ref, sums) = refs[0], refs[1 : 1 + PLANE], refs[1 + PLANE :]
    slot = head[0] ^ bit ^ (patch[0] // (n_patch // n_head))
    for near in range(PLANE):
        sums[(patch[0] % PLANE) ^ near] = lax.dot_general(
            o_ref[...], w_refs[near][slot], NT, preferred_element_type=F32
        )
    out = jnp.concatenate([sums[c] for c in range(PLANE)], axis=1)
    out_ref[...] = out.astype(out_ref.dtype)


def gate_kernel(n_patch, patch, ids_ref, mod_ref, *refs):
    sum_refs, (own_out, mate_out) = refs[:-2], refs[-2:]
    total = sum(ref[...].astype(F32) for ref in sum_refs)
    rows, width = total.shape
    each = rows // 2 // STEPS
    second = (patch[0] // PLANE) % 2 == 1
    for step in range(STEPS):
        gate = table_row(mod_ref, 2, ids_ref, step)
        gate = jnp.where(second, gate[:, width:], gate[:, :width])
        for mate, ref in enumerate((own_out, mate_out)):
            start = mate * (rows // 2) + step * each
            ref[step] = (gate * total[start : start + each]).astype(BF16)


def in_hbm(values):
    return pltpu.with_memory_space_constraint(values, pltpu.HBM)


def call(kernel, shapes, ins, scratch=(), flops=0, size=0, limit=16):
    return pl.pallas_call(
        kernel,
        out_shape=shapes,
        in_specs=ins,
        out_specs=jax.tree.map(lambda _: VMEM, shapes),
        scratch_shapes=scratch,
        compiler_params=pltpu.CompilerParams(vmem_limit_bytes=limit * MIB),
        cost_estimate=pl.CostEstimate(flops=flops, bytes_accessed=size, transcendentals=0),
    )


def body(n_patch, n_head, inputs, stale_kv, w_qkv, w_out, mod_table, step_ids, slab_order):
    rows, feats = inputs.shape[1:]
    cols = w_qkv.shape[2]
    piece = w_out.shape[1]
    patch = lax.axis_index("patch").astype(jnp.int32)
    head = lax.axis_index("head").astype(jnp.int32)
    shaped = jax.ShapeDtypeStruct

    x_parts = [swap(inputs, "head", n_head, k) for k in range(1, n_head)]
    mod_parts = [swap(mod_table, "head", n_head, k) for k in range(1, n_head)]
    first = (jnp.transpose(w_qkv, (1, 0, 2)), inputs, jnp.transpose(mod_table, (1, 0, 2)), stale_kv)
    w, x_own, mod_own, stale, ids, cos, sin = call(
        load_kernel,
        tuple(pltpu.VMEM(v.shape, v.dtype) for v in first)
        + (shaped((8, DH), jnp.int32), shaped((rows, DH), F32), shaped((rows, DH), F32)),
        [SMEM] * 2 + [ANY] * len(first),
        [pltpu.SemaphoreType.DMA((6,))],
        size=2 * w_qkv.size,
    )(in_hbm(step_ids), slab_order, *map(in_hbm, first))
    x_parts = [x_own] + x_parts
    mod_parts = [mod_own] + [jnp.transpose(part, (1, 0, 2)) for part in mod_parts]

    def across(values, k):
        return swap(values, "patch", n_patch, k)

    def line_of(values):
        return [values] + [across(values, k) for k in range(2 * PLANE, n_patch, 2 * PLANE)]

    def plane_of(values):
        return [values] + [across(values, k) for k in range(1, PLANE)]


    kv_shape = shaped((2, rows, cols), BF16)
    q, kv, kv1 = call(
        functools.partial(qkv_kernel, n_head),
        (kv_shape, shaped((4, rows, cols), BF16), kv_shape),
        [SMEM] + [VMEM] * (2 * n_head + 5),
        flops=2 * STEPS * rows * w_qkv.size,
        size=2 * w_qkv.size,
    )(head[None], ids, *x_parts, *mod_parts, w, cos, sin, stale)

    w_own, w_rest, kv = lax.optimization_barrier((w_out.T, line_of(w_out.T)[1:], kv))
    w_rest = jnp.stack(w_rest)
    kv_pair = line_of(kv)
    q_mate = across(q, PLANE)
    w_x = across(w_own, 1)
    kv_plane = plane_of(jnp.stack(kv_pair))
    w_rest, q_mate = lax.optimization_barrier((w_rest, q_mate))
    rest_y = across(w_rest, 2)
    rest_y, w_x, kv_plane[1] = lax.optimization_barrier((rest_y, w_x, kv_plane[1]))
    w_y = across(jnp.stack([w_own, w_x]), 2)
    rest_x = across(jnp.stack([w_rest, rest_y]), 1)
    tall = 2 * STEPS * rows
    part = call(
        attend_kernel,
        shaped((tall, cols + DH), BF16),
        [VMEM] * (3 + PLANE),
        flops=4 * STEPS * rows * n_patch * rows * cols,
    )(q, q_mate, kv1, *kv_plane)
    o = call(merge_kernel, shaped((tall, cols), BF16), [VMEM] * 2)(part, across(part, PLANE))
    o, w_y, rest_x = lax.optimization_barrier((o, w_y, rest_x))
    near = [(w_own, w_rest), (w_x, rest_x[0]), (w_y[0], rest_y), (w_y[1], rest_x[1])]
    w_plane = [jnp.concatenate([first[None], others]) for first, others in near]
    wide = PLANE * piece

    def project(bit, dtype):
        return call(
            functools.partial(project_kernel, n_head, n_patch, bit),
            shaped((tall, wide), dtype),
            [SMEM] * 2 + [VMEM] * (1 + PLANE),
            [pltpu.VMEM((PLANE, tall, piece), F32)],
            2 * tall * wide * cols,
            2 * wide * cols,
        )(patch[None], head[None], o, *w_plane)

    sums = [swap(project(k, BF16), "head", n_head, k) for k in range(1, n_head)]
    sums = [project(0, F32)] + sums
    out_half = shaped((STEPS, rows, wide), BF16)
    out_own, out_mate = call(
        functools.partial(gate_kernel, n_patch),
        (out_half, out_half),
        [SMEM] + [VMEM] * (2 + n_head),
    )(patch[None], ids, mod_own, *sums)
    out_back = across(out_mate, PLANE)
    second = (patch // PLANE) % 2 == 1
    return jnp.concatenate(
        [jnp.where(second, out_back, out_own), jnp.where(second, out_own, out_back)], axis=2
    )


def solution(mesh):
    in_specs = (
        P(None, "patch", "head"),
        P(None, "patch", "head"),
        P(None, None, "head"),
        P("head", "patch"),
        P(None, None, "head"),
        P(),
        P("patch"),
    )
    run = functools.partial(body, mesh.shape["patch"], mesh.shape["head"])
    return jax.shard_map(
        run, mesh=mesh, in_specs=in_specs, out_specs=P(None, "patch", "head"), check_vma=False
    )
```

```python
import functools
import math

import jax
import jax.numpy as jnp
from jax import lax
from jax.experimental import pallas as pl
from jax.experimental.pallas import tpu as pltpu
from jax.sharding import PartitionSpec as P

DH = 128
STEPS = 2
PLANE = 4
MIB = 1024 * 1024
VMEM = pl.BlockSpec(memory_space=pltpu.VMEM)
SMEM = pl.BlockSpec(memory_space=pltpu.SMEM)
ANY = pl.BlockSpec(memory_space=pl.ANY)
BF16, F32 = jnp.bfloat16, jnp.float32
NT = (((1,), (1,)), ((), ()))


def swap(values, axis, count, bit):
    return lax.ppermute(values, axis, [(i, i ^ bit) for i in range(count)])


def load_kernel(ids, slab, w_ref, x_ref, mod_ref, stale_ref, w_out, x_out, mod_out, stale_out, *refs):
    ids_out, cos_ref, sin_ref, sems = refs
    copies = [
        pltpu.make_async_copy(w_ref.at[slot], w_out.at[slot], sems.at[slot])
        for slot in range(3)
    ]
    copies.append(pltpu.make_async_copy(x_ref, x_out, sems.at[3]))
    copies.append(pltpu.make_async_copy(mod_ref, mod_out, sems.at[4]))
    copies.append(pltpu.make_async_copy(stale_ref, stale_out, sems.at[5]))
    for copy in copies:
        copy.start()
    row = lax.broadcasted_iota(jnp.int32, ids_out.shape, 0)
    tile = jnp.zeros(ids_out.shape, jnp.int32)
    for step in range(STEPS):
        tile = jnp.where(row == step, ids[step], tile)
    ids_out[...] = tile
    rows, half = cos_ref.shape[0], DH // 2
    lane = lax.broadcasted_iota(jnp.int32, cos_ref.shape, 1)
    spot = slab[0] * rows + lax.broadcasted_iota(jnp.int32, cos_ref.shape, 0)
    power = jnp.where(lane < half, lane, lane - half).astype(F32) * (-2.0 / DH)
    angle = spot.astype(F32) * jnp.exp(power * math.log(10000.0))
    cos_ref[...] = jnp.cos(angle)
    sin = jnp.sin(angle)
    sin_ref[...] = jnp.where(lane < half, -sin, sin)
    for copy in copies:
        copy.wait()


def table_row(mod_ref, kind, ids_ref, step):
    chosen = ids_ref[step : step + 1, :1]
    table = mod_ref[kind]
    return sum(
        jnp.where(chosen == r, table[r : r + 1], 0.0) for r in range(table.shape[0])
    )


def normalized(step, x_refs, mod_refs, ids_ref):
    hidden = [ref[step].astype(F32) for ref in x_refs]
    width = sum(part.shape[1] for part in hidden)
    mean = sum(jnp.sum(part, axis=1, keepdims=True) for part in hidden) / width
    square = sum(jnp.sum(part * part, axis=1, keepdims=True) for part in hidden) / width
    inv = lax.rsqrt(square - mean * mean + 1e-06)
    parts = []
    for part, mod_ref in zip(hidden, mod_refs):
        shift = table_row(mod_ref, 0, ids_ref, step)
        scale = table_row(mod_ref, 1, ids_ref, step)
        parts.append(((part - mean) * inv * (1.0 + scale) + shift).astype(BF16))
    return parts


def projected(parts, w_ref, slot, head):
    feats = parts[0].shape[1]
    total = jnp.zeros((parts[0].shape[0], w_ref.shape[2]), F32)
    for number, part in enumerate(parts):
        start = pl.multiple_of((head[0] ^ number) * feats, feats)
        w = w_ref[slot, pl.ds(start, feats), :]
        total += jnp.dot(part, w, preferred_element_type=F32)
    return total


def rotated(values, cos, sin):
    blocks = []
    for start in range(0, values.shape[1], DH):
        u = values[:, start : start + DH]
        blocks.append(u * cos + pltpu.roll(u, DH // 2, 1) * sin)
    return jnp.concatenate(blocks, axis=1)


def qkv_kernel(n_head, head, ids_ref, *refs):
    x_refs, mod_refs = refs[:n_head], refs[n_head : 2 * n_head]
    w_ref, cos_ref, sin_ref, stale_ref, q_ref, kv_ref, kv1_ref = refs[2 * n_head :]
    rows = x_refs[0].shape[1]
    steps = [normalized(step, x_refs, mod_refs, ids_ref) for step in range(STEPS)]
    parts = [jnp.concatenate(pair, axis=0) for pair in zip(*steps)]
    cos = jnp.concatenate([cos_ref[...]] * STEPS, axis=0)
    sin = jnp.concatenate([sin_ref[...]] * STEPS, axis=0)
    queries = rotated(projected(parts, w_ref, 0, head), cos, sin).astype(BF16)
    keys = rotated(projected(parts, w_ref, 1, head), cos, sin).astype(BF16)
    values = projected(parts, w_ref, 2, head).astype(BF16)
    for step in range(STEPS):
        spot = slice(step * rows, (step + 1) * rows)
        q_ref[step] = queries[spot]
    kv_ref[:2] = stale_ref[...]
    kv_ref[2], kv_ref[3] = keys[:rows], values[:rows]
    kv1_ref[0], kv1_ref[1] = keys[rows:], values[rows:]


def split3(values):
    high = values.astype(BF16).astype(F32)
    middle = (values - high).astype(BF16).astype(F32)
    return [high, middle, values - high - middle]


def attend_kernel(q_ref, mate_ref, kv1_ref, *refs):
    own_ref, next_ref, far_ref, out_ref = refs
    kv_refs = [own_ref, next_ref, far_ref.at[0], far_ref.at[1]]
    blocks, _, rows, cols = kv_refs[0].shape
    old_rows = PLANE * blocks * rows
    shape = (2 * rows, old_rows + rows)
    mine = lax.broadcasted_iota(jnp.int32, shape, 0) < rows
    stray = jnp.where(mine, 0, PLANE * blocks)
    drop = lax.broadcasted_iota(jnp.int32, shape, 1) // rows == stray
    lane = lax.broadcasted_iota(jnp.int32, (2 * rows, DH), 1)
    for step in range(STEPS):
        fresh = (kv_refs[0].at[0, 2:], kv1_ref)[step]
        stats = jnp.zeros((2 * rows, DH), F32)
        mixed = []
        for head in range(cols // DH):
            lanes = slice(head * DH, (head + 1) * DH)

            def rows_of(kind):
                old = [ref[:, 2 * step + kind, :, lanes].reshape(blocks * rows, DH) for ref in kv_refs]
                return jnp.concatenate([*old, fresh[kind, :, lanes]], axis=0)

            queries = jnp.concatenate([q_ref[step, :, lanes], mate_ref[step, :, lanes]], axis=0)
            scores = lax.dot_general(queries, rows_of(0), NT, preferred_element_type=F32)
            scores = jnp.where(drop, -1e30, scores * (1.0 / math.sqrt(DH)))
            top = jnp.max(scores, axis=1, keepdims=True)
            weights = jnp.exp(scores - top)
            totals = jnp.sum(weights, axis=1, keepdims=True)
            mixed.append(
                jnp.dot(weights.astype(BF16), rows_of(1), preferred_element_type=F32) / totals
            )
            for place, piece in enumerate(split3(top) + split3(totals)):
                stats = jnp.where(lane == head * 8 + place, piece, stats)
        packed = jnp.concatenate([*mixed, stats], axis=1).astype(BF16)
        for mate in range(2):
            start = (mate * STEPS + step) * rows
            out_ref[start : start + rows, :] = packed[mate * rows : (mate + 1) * rows]


def merge_kernel(part_ref, other_ref, o_ref):
    rows = part_ref.shape[0] // 2
    cols = o_ref.shape[1]
    source = lax.broadcasted_iota(jnp.int32, (DH, DH), 0)
    parts = [
        part_ref[...],
        jnp.concatenate([other_ref[rows:], other_ref[:rows]], axis=0),
    ]
    for head in range(cols // DH):
        lanes = slice(head * DH, (head + 1) * DH)

        def spread(part, first):
            pick = (source >= head * 8 + first) & (source < head * 8 + first + 3)
            return jnp.dot(part[:, cols:], pick.astype(F32).astype(BF16), preferred_element_type=F32)

        tops = [spread(part, 0) for part in parts]
        best = functools.reduce(jnp.maximum, tops)
        scales = [spread(part, 3) * jnp.exp(t - best) for part, t in zip(parts, tops)]
        mixed = sum(s * part[:, lanes].astype(F32) for s, part in zip(scales, parts))
        o_ref[:, lanes] = (mixed / sum(scales)).astype(BF16)


def project_kernel(n_head, n_patch, bit, patch, head, *refs):
    o_ref, own_ref, next_ref, far_ref, out_ref, sums = refs
    slot = head[0] ^ bit ^ (patch[0] // (n_patch // n_head))
    odd = head[0] % 2
    blocks = ((0, own_ref), (1 + odd, next_ref), (2 - odd, far_ref.at[0]), (3, far_ref.at[1]))
    for near, w_ref in blocks:
        sums[(patch[0] % PLANE) ^ near] = lax.dot_general(
            o_ref[...], w_ref[slot], NT, preferred_element_type=F32
        )
    out = jnp.concatenate([sums[c] for c in range(PLANE)], axis=1)
    out_ref[...] = out.astype(out_ref.dtype)


def gate_kernel(n_patch, patch, ids_ref, mod_ref, *refs):
    sum_refs, (own_out, mate_out) = refs[:-2], refs[-2:]
    total = sum(ref[...].astype(F32) for ref in sum_refs)
    rows, width = total.shape
    each = rows // 2 // STEPS
    second = (patch[0] // PLANE) % 2 == 1
    for step in range(STEPS):
        gate = table_row(mod_ref, 2, ids_ref, step)
        gate = jnp.where(second, gate[:, width:], gate[:, :width])
        for mate, ref in enumerate((own_out, mate_out)):
            start = mate * (rows // 2) + step * each
            ref[step] = (gate * total[start : start + each]).astype(BF16)


def in_hbm(values):
    return pltpu.with_memory_space_constraint(values, pltpu.HBM)


def call(kernel, shapes, ins, scratch=(), flops=0, size=0, limit=16):
    return pl.pallas_call(
        kernel,
        out_shape=shapes,
        in_specs=ins,
        out_specs=jax.tree.map(lambda _: VMEM, shapes),
        scratch_shapes=scratch,
        compiler_params=pltpu.CompilerParams(vmem_limit_bytes=limit * MIB),
        cost_estimate=pl.CostEstimate(flops=flops, bytes_accessed=size, transcendentals=0),
    )


def body(n_patch, n_head, inputs, stale_kv, w_qkv, w_out, mod_table, step_ids, slab_order):
    rows, feats = inputs.shape[1:]
    cols = w_qkv.shape[2]
    piece = w_out.shape[1]
    patch = lax.axis_index("patch").astype(jnp.int32)
    head = lax.axis_index("head").astype(jnp.int32)
    shaped = jax.ShapeDtypeStruct

    x_parts = [swap(inputs, "head", n_head, k) for k in range(1, n_head)]
    mod_parts = [swap(mod_table, "head", n_head, k) for k in range(1, n_head)]
    first = (jnp.transpose(w_qkv, (1, 0, 2)), inputs, jnp.transpose(mod_table, (1, 0, 2)), stale_kv)
    w, x_own, mod_own, stale, ids, cos, sin = call(
        load_kernel,
        tuple(pltpu.VMEM(v.shape, v.dtype) for v in first)
        + (shaped((8, DH), jnp.int32), shaped((rows, DH), F32), shaped((rows, DH), F32)),
        [SMEM] * 2 + [ANY] * len(first),
        [pltpu.SemaphoreType.DMA((6,))],
        size=2 * w_qkv.size,
    )(in_hbm(step_ids), slab_order, *map(in_hbm, first))
    x_parts = [x_own] + x_parts
    mod_parts = [mod_own] + [jnp.transpose(part, (1, 0, 2)) for part in mod_parts]

    def across(values, k):
        return swap(values, "patch", n_patch, k)

    def line_of(values):
        return [values] + [across(values, k) for k in range(2 * PLANE, n_patch, 2 * PLANE)]

    def turn(values, first):
        pairs = [
            (p * n_head + h, (p ^ (1 if (h % 2 == 0) == first else 2)) * n_head + h)
            for p in range(n_patch)
            for h in range(n_head)
        ]
        return lax.ppermute(values, ("patch", "head"), pairs)


    kv_shape = shaped((2, rows, cols), BF16)
    q, kv, kv1 = call(
        functools.partial(qkv_kernel, n_head),
        (kv_shape, shaped((4, rows, cols), BF16), kv_shape),
        [SMEM] + [VMEM] * (2 * n_head + 5),
        flops=2 * STEPS * rows * w_qkv.size,
        size=2 * w_qkv.size,
    )(head[None], ids, *x_parts, *mod_parts, w, cos, sin, stale)

    w_pair, kv = lax.optimization_barrier((line_of(w_out.T), kv))
    w_pair = jnp.stack(w_pair)
    kv_pair = jnp.stack(line_of(kv))
    q_mate = across(q, PLANE)
    w_next = turn(w_pair, True)
    kv_next = turn(kv_pair, True)
    kv_far = turn(jnp.stack([kv_pair, kv_next]), False)
    w_far = turn(jnp.stack([w_pair, w_next]), False)
    tall = 2 * STEPS * rows
    part = call(
        attend_kernel,
        shaped((tall, cols + DH), BF16),
        [VMEM] * 6,
        flops=4 * STEPS * rows * n_patch * rows * cols,
    )(q, q_mate, kv1, kv_pair, kv_next, kv_far)
    o = call(merge_kernel, shaped((tall, cols), BF16), [VMEM] * 2)(part, across(part, PLANE))
    wide = PLANE * piece

    def project(bit, dtype):
        return call(
            functools.partial(project_kernel, n_head, n_patch, bit),
            shaped((tall, wide), dtype),
            [SMEM] * 2 + [VMEM] * 4,
            [pltpu.VMEM((PLANE, tall, piece), F32)],
            2 * tall * wide * cols,
            2 * wide * cols,
        )(patch[None], head[None], o, w_pair, w_next, w_far)

    sums = [swap(project(k, BF16), "head", n_head, k) for k in range(1, n_head)]
    sums = [project(0, F32)] + sums
    out_half = shaped((STEPS, rows, wide), BF16)
    out_own, out_mate = call(
        functools.partial(gate_kernel, n_patch),
        (out_half, out_half),
        [SMEM] + [VMEM] * (2 + n_head),
    )(patch[None], ids, mod_own, *sums)
    out_back = across(out_mate, PLANE)
    second = (patch // PLANE) % 2 == 1
    return jnp.concatenate(
        [jnp.where(second, out_back, out_own), jnp.where(second, out_own, out_back)], axis=2
    )


def solution(mesh):
    in_specs = (
        P(None, "patch", "head"),
        P(None, "patch", "head"),
        P(None, None, "head"),
        P("head", "patch"),
        P(None, None, "head"),
        P(),
        P("patch"),
    )
    run = functools.partial(body, mesh.shape["patch"], mesh.shape["head"])
    return jax.shard_map(
        run, mesh=mesh, in_specs=in_specs, out_specs=P(None, "patch", "head"), check_vma=False
    )
```

```python
import functools
import math

import jax
import jax.numpy as jnp
from jax import lax
from jax.experimental import pallas as pl
from jax.experimental.pallas import tpu as pltpu
from jax.sharding import PartitionSpec as P

DH = 128
STEPS = 2
PLANE = 4
MIB = 1024 * 1024
VMEM = pl.BlockSpec(memory_space=pltpu.VMEM)
SMEM = pl.BlockSpec(memory_space=pltpu.SMEM)
ANY = pl.BlockSpec(memory_space=pl.ANY)
BF16, F32 = jnp.bfloat16, jnp.float32
NT = (((1,), (1,)), ((), ()))


def swap(values, axis, count, bit):
    return lax.ppermute(values, axis, [(i, i ^ bit) for i in range(count)])


def load_kernel(ids, slab, w_ref, x_ref, mod_ref, w_out, x_out, mod_out, *refs):
    ids_out, cos_ref, sin_ref, sems = refs
    copies = [
        pltpu.make_async_copy(w_ref.at[slot], w_out.at[slot], sems.at[slot])
        for slot in range(3)
    ]
    copies.append(pltpu.make_async_copy(x_ref, x_out, sems.at[3]))
    copies.append(pltpu.make_async_copy(mod_ref, mod_out, sems.at[4]))
    for copy in copies:
        copy.start()
    row = lax.broadcasted_iota(jnp.int32, ids_out.shape, 0)
    tile = jnp.zeros(ids_out.shape, jnp.int32)
    for step in range(STEPS):
        tile = jnp.where(row == step, ids[step], tile)
    ids_out[...] = tile
    rows, half = cos_ref.shape[0], DH // 2
    lane = lax.broadcasted_iota(jnp.int32, cos_ref.shape, 1)
    spot = slab[0] * rows + lax.broadcasted_iota(jnp.int32, cos_ref.shape, 0)
    power = jnp.where(lane < half, lane, lane - half).astype(F32) * (-2.0 / DH)
    angle = spot.astype(F32) * jnp.exp(power * math.log(10000.0))
    cos_ref[...] = jnp.cos(angle)
    sin = jnp.sin(angle)
    sin_ref[...] = jnp.where(lane < half, -sin, sin)
    for copy in copies:
        copy.wait()


def table_row(mod_ref, kind, ids_ref, step):
    chosen = ids_ref[step : step + 1, :1]
    table = mod_ref[kind]
    return sum(
        jnp.where(chosen == r, table[r : r + 1], 0.0) for r in range(table.shape[0])
    )


def normalized(step, x_refs, mod_refs, ids_ref):
    hidden = [ref[step].astype(F32) for ref in x_refs]
    width = sum(part.shape[1] for part in hidden)
    mean = sum(jnp.sum(part, axis=1, keepdims=True) for part in hidden) / width
    square = sum(jnp.sum(part * part, axis=1, keepdims=True) for part in hidden) / width
    inv = lax.rsqrt(square - mean * mean + 1e-06)
    parts = []
    for part, mod_ref in zip(hidden, mod_refs):
        shift = table_row(mod_ref, 0, ids_ref, step)
        scale = table_row(mod_ref, 1, ids_ref, step)
        parts.append(((part - mean) * inv * (1.0 + scale) + shift).astype(BF16))
    return parts


def projected(parts, w_ref, slot, head):
    feats = parts[0].shape[1]
    total = jnp.zeros((parts[0].shape[0], w_ref.shape[2]), F32)
    for number, part in enumerate(parts):
        start = pl.multiple_of((head[0] ^ number) * feats, feats)
        w = w_ref[slot, pl.ds(start, feats), :]
        total += jnp.dot(part, w, preferred_element_type=F32)
    return total


def rotated(values, cos, sin):
    blocks = []
    for start in range(0, values.shape[1], DH):
        u = values[:, start : start + DH]
        blocks.append(u * cos + pltpu.roll(u, DH // 2, 1) * sin)
    return jnp.concatenate(blocks, axis=1)


def qkv_kernel(n_head, head, ids_ref, *refs):
    x_refs, mod_refs = refs[:n_head], refs[n_head : 2 * n_head]
    w_ref, cos_ref, sin_ref = refs[2 * n_head : 2 * n_head + 3]
    q_ref, kv0_ref, kv1_ref = refs[-3:]
    rows = x_refs[0].shape[1]
    steps = [normalized(step, x_refs, mod_refs, ids_ref) for step in range(STEPS)]
    parts = [jnp.concatenate(pair, axis=0) for pair in zip(*steps)]
    cos = jnp.concatenate([cos_ref[...]] * STEPS, axis=0)
    sin = jnp.concatenate([sin_ref[...]] * STEPS, axis=0)
    queries = rotated(projected(parts, w_ref, 0, head), cos, sin).astype(BF16)
    keys = rotated(projected(parts, w_ref, 1, head), cos, sin).astype(BF16)
    values = projected(parts, w_ref, 2, head).astype(BF16)
    for step in range(STEPS):
        spot = slice(step * rows, (step + 1) * rows)
        q_ref[step] = queries[spot]
    kv0_ref[0], kv0_ref[1] = keys[:rows], values[:rows]
    kv1_ref[0], kv1_ref[1] = keys[rows:], values[rows:]


def split3(values):
    high = values.astype(BF16).astype(F32)
    middle = (values - high).astype(BF16).astype(F32)
    return [high, middle, values - high - middle]


def attend_kernel(q_ref, mate_ref, kv1_ref, *refs):
    own_ref, next_ref, far_ref, out_ref = refs
    kv_refs = [own_ref, next_ref, far_ref.at[0], far_ref.at[1]]
    blocks, _, rows, cols = kv_refs[0].shape
    old_rows = PLANE * blocks * rows
    shape = (2 * rows, old_rows + rows)
    mine = lax.broadcasted_iota(jnp.int32, shape, 0) < rows
    stray = jnp.where(mine, 0, PLANE * blocks)
    drop = lax.broadcasted_iota(jnp.int32, shape, 1) // rows == stray
    lane = lax.broadcasted_iota(jnp.int32, (2 * rows, DH), 1)
    for step in range(STEPS):
        fresh = (kv_refs[0].at[0, 2:], kv1_ref)[step]
        stats = jnp.zeros((2 * rows, DH), F32)
        mixed = []
        for head in range(cols // DH):
            lanes = slice(head * DH, (head + 1) * DH)

            def rows_of(kind):
                old = [ref[:, 2 * step + kind, :, lanes].reshape(blocks * rows, DH) for ref in kv_refs]
                return jnp.concatenate([*old, fresh[kind, :, lanes]], axis=0)

            queries = jnp.concatenate([q_ref[step, :, lanes], mate_ref[step, :, lanes]], axis=0)
            scores = lax.dot_general(queries, rows_of(0), NT, preferred_element_type=F32)
            scores = jnp.where(drop, -1e30, scores * (1.0 / math.sqrt(DH)))
            top = jnp.max(scores, axis=1, keepdims=True)
            weights = jnp.exp(scores - top)
            totals = jnp.sum(weights, axis=1, keepdims=True)
            mixed.append(
                jnp.dot(weights.astype(BF16), rows_of(1), preferred_element_type=F32) / totals
            )
            for place, piece in enumerate(split3(top) + split3(totals)):
                stats = jnp.where(lane == head * 8 + place, piece, stats)
        packed = jnp.concatenate([*mixed, stats], axis=1).astype(BF16)
        for mate in range(2):
            start = (mate * STEPS + step) * rows
            out_ref[start : start + rows, :] = packed[mate * rows : (mate + 1) * rows]


def merge_kernel(part_ref, other_ref, o_ref):
    rows = part_ref.shape[0] // 2
    cols = o_ref.shape[1]
    source = lax.broadcasted_iota(jnp.int32, (DH, DH), 0)
    parts = [
        part_ref[...],
        jnp.concatenate([other_ref[rows:], other_ref[:rows]], axis=0),
    ]
    for head in range(cols // DH):
        lanes = slice(head * DH, (head + 1) * DH)

        def spread(part, first):
            pick = (source >= head * 8 + first) & (source < head * 8 + first + 3)
            return jnp.dot(part[:, cols:], pick.astype(F32).astype(BF16), preferred_element_type=F32)

        tops = [spread(part, 0) for part in parts]
        best = functools.reduce(jnp.maximum, tops)
        scales = [spread(part, 3) * jnp.exp(t - best) for part, t in zip(parts, tops)]
        mixed = sum(s * part[:, lanes].astype(F32) for s, part in zip(scales, parts))
        o_ref[:, lanes] = (mixed / sum(scales)).astype(BF16)


def project_kernel(n_head, n_patch, bit, patch, head, *refs):
    o_ref, own_ref, next_ref, far_ref, out_ref, sums = refs
    slot = head[0] ^ bit ^ (patch[0] // (n_patch // n_head))
    odd = head[0] % 2
    blocks = ((0, own_ref), (1 + odd, next_ref), (2 - odd, far_ref.at[0]), (3, far_ref.at[1]))
    for near, w_ref in blocks:
        sums[(patch[0] % PLANE) ^ near] = lax.dot_general(
            o_ref[...], w_ref[slot], NT, preferred_element_type=F32
        )
    out = jnp.concatenate([sums[c] for c in range(PLANE)], axis=1)
    out_ref[...] = out.astype(out_ref.dtype)


def gate_kernel(n_patch, patch, ids_ref, mod_ref, *refs):
    sum_refs, (own_out, mate_out) = refs[:-2], refs[-2:]
    total = sum(ref[...].astype(F32) for ref in sum_refs)
    rows, width = total.shape
    each = rows // 2 // STEPS
    second = (patch[0] // PLANE) % 2 == 1
    for step in range(STEPS):
        gate = table_row(mod_ref, 2, ids_ref, step)
        gate = jnp.where(second, gate[:, width:], gate[:, :width])
        for mate, ref in enumerate((own_out, mate_out)):
            start = mate * (rows // 2) + step * each
            ref[step] = (gate * total[start : start + each]).astype(BF16)


def in_hbm(values):
    return pltpu.with_memory_space_constraint(values, pltpu.HBM)


def call(kernel, shapes, ins, scratch=(), flops=0, size=0, limit=16):
    return pl.pallas_call(
        kernel,
        out_shape=shapes,
        in_specs=ins,
        out_specs=jax.tree.map(lambda _: VMEM, shapes),
        scratch_shapes=scratch,
        compiler_params=pltpu.CompilerParams(vmem_limit_bytes=limit * MIB),
        cost_estimate=pl.CostEstimate(flops=flops, bytes_accessed=size, transcendentals=0),
    )


def body(n_patch, n_head, inputs, stale_kv, w_qkv, w_out, mod_table, step_ids, slab_order):
    rows, feats = inputs.shape[1:]
    cols = w_qkv.shape[2]
    piece = w_out.shape[1]
    patch = lax.axis_index("patch").astype(jnp.int32)
    head = lax.axis_index("head").astype(jnp.int32)
    shaped = jax.ShapeDtypeStruct

    x_parts = [swap(inputs, "head", n_head, k) for k in range(1, n_head)]
    mod_parts = [swap(mod_table, "head", n_head, k) for k in range(1, n_head)]
    first = (jnp.transpose(w_qkv, (1, 0, 2)), inputs, jnp.transpose(mod_table, (1, 0, 2)))
    w, x_own, mod_own, ids, cos, sin = call(
        load_kernel,
        tuple(pltpu.VMEM(v.shape, v.dtype) for v in first)
        + (shaped((8, DH), jnp.int32), shaped((rows, DH), F32), shaped((rows, DH), F32)),
        [SMEM] * 2 + [ANY] * len(first),
        [pltpu.SemaphoreType.DMA((5,))],
        size=2 * w_qkv.size,
    )(in_hbm(step_ids), slab_order, *map(in_hbm, first))
    x_parts = [x_own] + x_parts
    mod_parts = [mod_own] + [jnp.transpose(part, (1, 0, 2)) for part in mod_parts]

    def across(values, k):
        return swap(values, "patch", n_patch, k)

    def line_of(values):
        return [values] + [across(values, k) for k in range(2 * PLANE, n_patch, 2 * PLANE)]

    def turn(values, first):
        pairs = [
            (p * n_head + h, (p ^ (1 if (h % 2 == 0) == first else 2)) * n_head + h)
            for p in range(n_patch)
            for h in range(n_head)
        ]
        return lax.ppermute(values, ("patch", "head"), pairs)


    stale_pair = line_of(stale_kv)
    kv_shape = shaped((2, rows, cols), BF16)
    q, kv, kv1 = call(
        functools.partial(qkv_kernel, n_head),
        (kv_shape,) * 3,
        [SMEM] + [VMEM] * (2 * n_head + 4),
        flops=2 * STEPS * rows * w_qkv.size,
        size=2 * w_qkv.size,
    )(head[None], ids, *x_parts, *mod_parts, w, cos, sin)

    w_pair, kv = lax.optimization_barrier((line_of(w_out.T), kv))
    w_pair = jnp.stack(w_pair)
    stale_pair, kv_line = lax.optimization_barrier((stale_pair, line_of(kv)))
    kv_pair = jnp.stack([jnp.concatenate(pair) for pair in zip(stale_pair, kv_line)])
    q_mate = across(q, PLANE)
    w_next = turn(w_pair, True)
    kv_next = turn(kv_pair, True)
    kv_next, w_next, q_mate = lax.optimization_barrier((kv_next, w_next, q_mate))
    kv_far = turn(jnp.stack([kv_pair, kv_next]), False)
    w_next, kv_far = lax.optimization_barrier((w_next, kv_far))
    w_far = turn(jnp.stack([w_pair, w_next]), False)
    tall = 2 * STEPS * rows
    part = call(
        attend_kernel,
        shaped((tall, cols + DH), BF16),
        [VMEM] * 6,
        flops=4 * STEPS * rows * n_patch * rows * cols,
    )(q, q_mate, kv1, kv_pair, kv_next, kv_far)
    o = call(merge_kernel, shaped((tall, cols), BF16), [VMEM] * 2)(part, across(part, PLANE))
    wide = PLANE * piece

    def project(bit, dtype):
        return call(
            functools.partial(project_kernel, n_head, n_patch, bit),
            shaped((tall, wide), dtype),
            [SMEM] * 2 + [VMEM] * 4,
            [pltpu.VMEM((PLANE, tall, piece), F32)],
            2 * tall * wide * cols,
            2 * wide * cols,
        )(patch[None], head[None], o, w_pair, w_next, w_far)

    sums = [swap(project(k, BF16), "head", n_head, k) for k in range(1, n_head)]
    sums = [project(0, F32)] + sums
    out_half = shaped((STEPS, rows, wide), BF16)
    out_own, out_mate = call(
        functools.partial(gate_kernel, n_patch),
        (out_half, out_half),
        [SMEM] + [VMEM] * (2 + n_head),
    )(patch[None], ids, mod_own, *sums)
    out_back = across(out_mate, PLANE)
    second = (patch // PLANE) % 2 == 1
    return jnp.concatenate(
        [jnp.where(second, out_back, out_own), jnp.where(second, out_own, out_back)], axis=2
    )


def solution(mesh):
    in_specs = (
        P(None, "patch", "head"),
        P(None, "patch", "head"),
        P(None, None, "head"),
        P("head", "patch"),
        P(None, None, "head"),
        P(),
        P("patch"),
    )
    run = functools.partial(body, mesh.shape["patch"], mesh.shape["head"])
    return jax.shard_map(
        run, mesh=mesh, in_specs=in_specs, out_specs=P(None, "patch", "head"), check_vma=False
    )
```

```python
import functools
import math

import jax
import jax.numpy as jnp
from jax import lax
from jax.experimental import pallas as pl
from jax.experimental.pallas import tpu as pltpu
from jax.sharding import PartitionSpec as P

DH = 128
STEPS = 2
PLANE = 4
MIB = 1024 * 1024
VMEM = pl.BlockSpec(memory_space=pltpu.VMEM)
SMEM = pl.BlockSpec(memory_space=pltpu.SMEM)
ANY = pl.BlockSpec(memory_space=pl.ANY)
BF16, F32 = jnp.bfloat16, jnp.float32
NT = (((1,), (1,)), ((), ()))


def swap(values, axis, count, bit):
    return lax.ppermute(values, axis, [(i, i ^ bit) for i in range(count)])


def load_kernel(ids, slab, w_ref, x_ref, mod_ref, w_out, x_out, mod_out, *refs):
    ids_out, cos_ref, sin_ref, sems = refs
    copies = [
        pltpu.make_async_copy(w_ref.at[slot], w_out.at[slot], sems.at[slot])
        for slot in range(3)
    ]
    copies.append(pltpu.make_async_copy(x_ref, x_out, sems.at[3]))
    copies.append(pltpu.make_async_copy(mod_ref, mod_out, sems.at[4]))
    for copy in copies:
        copy.start()
    row = lax.broadcasted_iota(jnp.int32, ids_out.shape, 0)
    tile = jnp.zeros(ids_out.shape, jnp.int32)
    for step in range(STEPS):
        tile = jnp.where(row == step, ids[step], tile)
    ids_out[...] = tile
    rows, half = cos_ref.shape[0], DH // 2
    lane = lax.broadcasted_iota(jnp.int32, cos_ref.shape, 1)
    spot = slab[0] * rows + lax.broadcasted_iota(jnp.int32, cos_ref.shape, 0)
    power = jnp.where(lane < half, lane, lane - half).astype(F32) * (-2.0 / DH)
    angle = spot.astype(F32) * jnp.exp(power * math.log(10000.0))
    cos_ref[...] = jnp.cos(angle)
    sin = jnp.sin(angle)
    sin_ref[...] = jnp.where(lane < half, -sin, sin)
    for copy in copies:
        copy.wait()


def table_row(mod_ref, kind, ids_ref, step):
    chosen = ids_ref[step : step + 1, :1]
    table = mod_ref[kind]
    return sum(
        jnp.where(chosen == r, table[r : r + 1], 0.0) for r in range(table.shape[0])
    )


def normalized(step, x_refs, mod_refs, ids_ref):
    hidden = [ref[step].astype(F32) for ref in x_refs]
    width = sum(part.shape[1] for part in hidden)
    mean = sum(jnp.sum(part, axis=1, keepdims=True) for part in hidden) / width
    square = sum(jnp.sum(part * part, axis=1, keepdims=True) for part in hidden) / width
    inv = lax.rsqrt(square - mean * mean + 1e-06)
    parts = []
    for part, mod_ref in zip(hidden, mod_refs):
        shift = table_row(mod_ref, 0, ids_ref, step)
        scale = table_row(mod_ref, 1, ids_ref, step)
        parts.append(((part - mean) * inv * (1.0 + scale) + shift).astype(BF16))
    return parts


def projected(parts, w_ref, slot, head):
    feats = parts[0].shape[1]
    total = jnp.zeros((parts[0].shape[0], w_ref.shape[2]), F32)
    for number, part in enumerate(parts):
        start = pl.multiple_of((head[0] ^ number) * feats, feats)
        w = w_ref[slot, pl.ds(start, feats), :]
        total += jnp.dot(part, w, preferred_element_type=F32)
    return total


def rotated(values, cos, sin):
    blocks = []
    for start in range(0, values.shape[1], DH):
        u = values[:, start : start + DH]
        blocks.append(u * cos + pltpu.roll(u, DH // 2, 1) * sin)
    return jnp.concatenate(blocks, axis=1)


def qkv_kernel(n_head, head, ids_ref, *refs):
    x_refs, mod_refs = refs[:n_head], refs[n_head : 2 * n_head]
    w_ref, cos_ref, sin_ref = refs[2 * n_head : 2 * n_head + 3]
    q_ref, kv0_ref, kv1_ref = refs[-3:]
    rows = x_refs[0].shape[1]
    steps = [normalized(step, x_refs, mod_refs, ids_ref) for step in range(STEPS)]
    parts = [jnp.concatenate(pair, axis=0) for pair in zip(*steps)]
    cos = jnp.concatenate([cos_ref[...]] * STEPS, axis=0)
    sin = jnp.concatenate([sin_ref[...]] * STEPS, axis=0)
    queries = rotated(projected(parts, w_ref, 0, head), cos, sin).astype(BF16)
    keys = rotated(projected(parts, w_ref, 1, head), cos, sin).astype(BF16)
    values = projected(parts, w_ref, 2, head).astype(BF16)
    for step in range(STEPS):
        spot = slice(step * rows, (step + 1) * rows)
        q_ref[step] = queries[spot]
    kv0_ref[0], kv0_ref[1] = keys[:rows], values[:rows]
    kv1_ref[0], kv1_ref[1] = keys[rows:], values[rows:]


def split3(values):
    high = values.astype(BF16).astype(F32)
    middle = (values - high).astype(BF16).astype(F32)
    return [high, middle, values - high - middle]


def attend_kernel(q_ref, mate_ref, kv1_ref, *refs):
    kv_refs, out_ref = refs[:PLANE], refs[PLANE]
    blocks, _, rows, cols = kv_refs[0].shape
    old_rows = PLANE * blocks * rows
    shape = (2 * rows, old_rows + rows)
    mine = lax.broadcasted_iota(jnp.int32, shape, 0) < rows
    stray = jnp.where(mine, 0, PLANE * blocks)
    drop = lax.broadcasted_iota(jnp.int32, shape, 1) // rows == stray
    lane = lax.broadcasted_iota(jnp.int32, (2 * rows, DH), 1)
    for step in range(STEPS):
        fresh = (kv_refs[0].at[0, 2:], kv1_ref)[step]
        stats = jnp.zeros((2 * rows, DH), F32)
        mixed = []
        for head in range(cols // DH):
            lanes = slice(head * DH, (head + 1) * DH)

            def rows_of(kind):
                old = [ref[:, 2 * step + kind, :, lanes].reshape(blocks * rows, DH) for ref in kv_refs]
                return jnp.concatenate([*old, fresh[kind, :, lanes]], axis=0)

            queries = jnp.concatenate([q_ref[step, :, lanes], mate_ref[step, :, lanes]], axis=0)
            scores = lax.dot_general(queries, rows_of(0), NT, preferred_element_type=F32)
            scores = jnp.where(drop, -1e30, scores * (1.0 / math.sqrt(DH)))
            top = jnp.max(scores, axis=1, keepdims=True)
            weights = jnp.exp(scores - top)
            totals = jnp.sum(weights, axis=1, keepdims=True)
            mixed.append(
                jnp.dot(weights.astype(BF16), rows_of(1), preferred_element_type=F32) / totals
            )
            for place, piece in enumerate(split3(top) + split3(totals)):
                stats = jnp.where(lane == head * 8 + place, piece, stats)
        packed = jnp.concatenate([*mixed, stats], axis=1).astype(BF16)
        for mate in range(2):
            start = (mate * STEPS + step) * rows
            out_ref[start : start + rows, :] = packed[mate * rows : (mate + 1) * rows]


def merge_kernel(part_ref, other_ref, o_ref):
    rows = part_ref.shape[0] // 2
    cols = o_ref.shape[1]
    source = lax.broadcasted_iota(jnp.int32, (DH, DH), 0)
    parts = [
        part_ref[...],
        jnp.concatenate([other_ref[rows:], other_ref[:rows]], axis=0),
    ]
    for head in range(cols // DH):
        lanes = slice(head * DH, (head + 1) * DH)

        def spread(part, first):
            pick = (source >= head * 8 + first) & (source < head * 8 + first + 3)
            return jnp.dot(part[:, cols:], pick.astype(F32).astype(BF16), preferred_element_type=F32)

        tops = [spread(part, 0) for part in parts]
        best = functools.reduce(jnp.maximum, tops)
        scales = [spread(part, 3) * jnp.exp(t - best) for part, t in zip(parts, tops)]
        mixed = sum(s * part[:, lanes].astype(F32) for s, part in zip(scales, parts))
        o_ref[:, lanes] = (mixed / sum(scales)).astype(BF16)


def project_kernel(n_head, n_patch, bit, patch, head, *refs):
    o_ref, low_ref, high_ref, out_ref, sums = refs
    slot = head[0] ^ bit ^ (patch[0] // (n_patch // n_head))
    for core, w_ref in enumerate((low_ref, high_ref)):

        @pl.when(head[0] % 2 == core)
        def _():
            for near in range(PLANE):
                sums[(patch[0] % PLANE) ^ near] = lax.dot_general(
                    o_ref[...], w_ref[near, slot], NT, preferred_element_type=F32
                )

    out = jnp.concatenate([sums[c] for c in range(PLANE)], axis=1)
    out_ref[...] = out.astype(out_ref.dtype)


def gate_kernel(n_patch, patch, ids_ref, mod_ref, *refs):
    sum_refs, (own_out, mate_out) = refs[:-2], refs[-2:]
    total = sum(ref[...].astype(F32) for ref in sum_refs)
    rows, width = total.shape
    each = rows // 2 // STEPS
    second = (patch[0] // PLANE) % 2 == 1
    for step in range(STEPS):
        gate = table_row(mod_ref, 2, ids_ref, step)
        gate = jnp.where(second, gate[:, width:], gate[:, :width])
        for mate, ref in enumerate((own_out, mate_out)):
            start = mate * (rows // 2) + step * each
            ref[step] = (gate * total[start : start + each]).astype(BF16)


def in_hbm(values):
    return pltpu.with_memory_space_constraint(values, pltpu.HBM)


def call(kernel, shapes, ins, scratch=(), flops=0, size=0, limit=16):
    return pl.pallas_call(
        kernel,
        out_shape=shapes,
        in_specs=ins,
        out_specs=jax.tree.map(lambda _: VMEM, shapes),
        scratch_shapes=scratch,
        compiler_params=pltpu.CompilerParams(vmem_limit_bytes=limit * MIB),
        cost_estimate=pl.CostEstimate(flops=flops, bytes_accessed=size, transcendentals=0),
    )


def body(n_patch, n_head, inputs, stale_kv, w_qkv, w_out, mod_table, step_ids, slab_order):
    rows, feats = inputs.shape[1:]
    cols = w_qkv.shape[2]
    piece = w_out.shape[1]
    patch = lax.axis_index("patch").astype(jnp.int32)
    head = lax.axis_index("head").astype(jnp.int32)
    shaped = jax.ShapeDtypeStruct

    x_parts = [swap(inputs, "head", n_head, k) for k in range(1, n_head)]
    mod_parts = [swap(mod_table, "head", n_head, k) for k in range(1, n_head)]
    first = (jnp.transpose(w_qkv, (1, 0, 2)), inputs, jnp.transpose(mod_table, (1, 0, 2)))
    w, x_own, mod_own, ids, cos, sin = call(
        load_kernel,
        tuple(pltpu.VMEM(v.shape, v.dtype) for v in first)
        + (shaped((8, DH), jnp.int32), shaped((rows, DH), F32), shaped((rows, DH), F32)),
        [SMEM] * 2 + [ANY] * len(first),
        [pltpu.SemaphoreType.DMA((5,))],
        size=2 * w_qkv.size,
    )(in_hbm(step_ids), slab_order, *map(in_hbm, first))
    x_parts = [x_own] + x_parts
    mod_parts = [mod_own] + [jnp.transpose(part, (1, 0, 2)) for part in mod_parts]

    def across(values, k):
        return swap(values, "patch", n_patch, k)

    def line_of(values):
        return [values] + [across(values, k) for k in range(2 * PLANE, n_patch, 2 * PLANE)]

    def pairs_of(moves):
        return [
            (p * n_head + h, q * n_head + g)
            for p in range(n_patch)
            for h in range(n_head)
            for q, g in moves(p, h)
        ]

    def lone(values, k):
        pairs = pairs_of(lambda p, h: [(p ^ k, h)] if h % 2 else [])
        return lax.ppermute(values, ("patch", "head"), pairs)

    def lift(values):
        pairs = pairs_of(lambda p, h: [] if h % 2 else [(p, h + 1)])
        return lax.ppermute(values, ("patch", "head"), pairs)

    def lower(values):
        pairs = pairs_of(lambda p, h: [(p, h - 1)] if h % 2 else [])
        return lax.ppermute(values, ("patch", "head"), pairs)

    def plane_of(values):
        return [values] + [across(values, k) for k in range(1, PLANE)]

    stale_pair = line_of(stale_kv)
    w_own, *w_rest = line_of(w_out.T)
    w_even = lift(w_own)
    kv_shape = shaped((2, rows, cols), BF16)
    q, kv, kv1 = call(
        functools.partial(qkv_kernel, n_head),
        (kv_shape,) * 3,
        [SMEM] + [VMEM] * (2 * n_head + 4),
        flops=2 * STEPS * rows * w_qkv.size,
        size=2 * w_qkv.size,
    )(head[None], ids, *x_parts, *mod_parts, w, cos, sin)

    w_own, w_even, w_rest, kv = lax.optimization_barrier((w_own, w_even, w_rest, kv))
    w_rest = jnp.stack(w_rest)
    w_both = jnp.stack([w_even, w_own])
    rest_both = jnp.stack([lift(w_rest), w_rest], axis=1)
    stale_pair, kv_line = lax.optimization_barrier((stale_pair, line_of(kv)))
    kv_pair = jnp.stack([jnp.concatenate(pair) for pair in zip(stale_pair, kv_line)])
    q_mate = across(q, PLANE)
    kv_plane = plane_of(kv_pair)
    w_x = lone(w_both, 1)
    rest_y = lone(rest_both, 2)
    w_x, rest_y, q_mate, kv_plane[1] = lax.optimization_barrier(
        (w_x, rest_y, q_mate, kv_plane[1])
    )
    w_y = lone(jnp.stack([w_both, w_x]), 2)
    rest_x = lone(jnp.stack([rest_both, rest_y]), 1)
    tall = 2 * STEPS * rows
    part = call(
        attend_kernel,
        shaped((tall, cols + DH), BF16),
        [VMEM] * (3 + PLANE),
        flops=4 * STEPS * rows * n_patch * rows * cols,
    )(q, q_mate, kv1, *kv_plane)
    o = call(merge_kernel, shaped((tall, cols), BF16), [VMEM] * 2)(part, across(part, PLANE))
    o, w_y, rest_x = lax.optimization_barrier((o, w_y, rest_x))
    near = [(w_both, rest_both), (w_x, rest_x[0]), (w_y[0], rest_y), (w_y[1], rest_x[1])]
    w_all = [
        jnp.stack([jnp.concatenate([first[None, k], others[:, k]]) for first, others in near])
        for k in range(2)
    ]
    w_low, w_high = lower(w_all[0]), w_all[1]
    wide = PLANE * piece

    def project(bit, dtype):
        return call(
            functools.partial(project_kernel, n_head, n_patch, bit),
            shaped((tall, wide), dtype),
            [SMEM] * 2 + [VMEM] * 3,
            [pltpu.VMEM((PLANE, tall, piece), F32)],
            2 * tall * wide * cols,
            2 * wide * cols,
        )(patch[None], head[None], o, w_low, w_high)

    sums = [swap(project(k, BF16), "head", n_head, k) for k in range(1, n_head)]
    sums = [project(0, F32)] + sums
    out_half = shaped((STEPS, rows, wide), BF16)
    out_own, out_mate = call(
        functools.partial(gate_kernel, n_patch),
        (out_half, out_half),
        [SMEM] + [VMEM] * (2 + n_head),
    )(patch[None], ids, mod_own, *sums)
    out_back = across(out_mate, PLANE)
    second = (patch // PLANE) % 2 == 1
    return jnp.concatenate(
        [jnp.where(second, out_back, out_own), jnp.where(second, out_own, out_back)], axis=2
    )


def solution(mesh):
    in_specs = (
        P(None, "patch", "head"),
        P(None, "patch", "head"),
        P(None, None, "head"),
        P("head", "patch"),
        P(None, None, "head"),
        P(),
        P("patch"),
    )
    run = functools.partial(body, mesh.shape["patch"], mesh.shape["head"])
    return jax.shard_map(
        run, mesh=mesh, in_specs=in_specs, out_specs=P(None, "patch", "head"), check_vma=False
    )
```

```python
import functools
import math

import jax
import jax.numpy as jnp
from jax import lax
from jax.experimental import pallas as pl
from jax.experimental.pallas import tpu as pltpu
from jax.sharding import PartitionSpec as P

DH = 128
STEPS = 2
PLANE = 4
MIB = 1024 * 1024
VMEM = pl.BlockSpec(memory_space=pltpu.VMEM)
SMEM = pl.BlockSpec(memory_space=pltpu.SMEM)
ANY = pl.BlockSpec(memory_space=pl.ANY)
BF16, F32 = jnp.bfloat16, jnp.float32
NT = (((1,), (1,)), ((), ()))


def swap(values, axis, count, bit):
    return lax.ppermute(values, axis, [(i, i ^ bit) for i in range(count)])


def load_kernel(ids, slab, w_ref, x_ref, mod_ref, stale_ref, w_out, x_out, mod_out, stale_out, *refs):
    ids_out, cos_ref, sin_ref, sems = refs
    copies = [
        pltpu.make_async_copy(w_ref.at[slot + 1], w_out.at[slot], sems.at[slot])
        for slot in range(2)
    ]
    copies.append(pltpu.make_async_copy(x_ref, x_out, sems.at[2]))
    copies.append(pltpu.make_async_copy(mod_ref, mod_out, sems.at[3]))
    copies.append(pltpu.make_async_copy(stale_ref, stale_out, sems.at[4]))
    for copy in copies:
        copy.start()
    row = lax.broadcasted_iota(jnp.int32, ids_out.shape, 0)
    tile = jnp.zeros(ids_out.shape, jnp.int32)
    for step in range(STEPS):
        tile = jnp.where(row == step, ids[step], tile)
    ids_out[...] = tile
    rows, half = cos_ref.shape[0], DH // 2
    lane = lax.broadcasted_iota(jnp.int32, cos_ref.shape, 1)
    spot = slab[0] * rows + lax.broadcasted_iota(jnp.int32, cos_ref.shape, 0)
    power = jnp.where(lane < half, lane, lane - half).astype(F32) * (-2.0 / DH)
    angle = spot.astype(F32) * jnp.exp(power * math.log(10000.0))
    cos_ref[...] = jnp.cos(angle)
    sin = jnp.sin(angle)
    sin_ref[...] = jnp.where(lane < half, -sin, sin)
    for copy in copies:
        copy.wait()


def table_row(mod_ref, kind, ids_ref, step):
    chosen = ids_ref[step : step + 1, :1]
    table = mod_ref[kind]
    return sum(
        jnp.where(chosen == r, table[r : r + 1], 0.0) for r in range(table.shape[0])
    )


def normalized(step, x_refs, mod_refs, ids_ref):
    hidden = [ref[step].astype(F32) for ref in x_refs]
    width = sum(part.shape[1] for part in hidden)
    mean = sum(jnp.sum(part, axis=1, keepdims=True) for part in hidden) / width
    square = sum(jnp.sum(part * part, axis=1, keepdims=True) for part in hidden) / width
    inv = lax.rsqrt(square - mean * mean + 1e-06)
    parts = []
    for part, mod_ref in zip(hidden, mod_refs):
        shift = table_row(mod_ref, 0, ids_ref, step)
        scale = table_row(mod_ref, 1, ids_ref, step)
        parts.append(((part - mean) * inv * (1.0 + scale) + shift).astype(BF16))
    return parts


def projected(parts, w_ref, slot, head):
    feats = parts[0].shape[1]
    total = jnp.zeros((parts[0].shape[0], w_ref.shape[2]), F32)
    for number, part in enumerate(parts):
        start = pl.multiple_of((head[0] ^ number) * feats, feats)
        w = w_ref[slot, pl.ds(start, feats), :]
        total += jnp.dot(part, w, preferred_element_type=F32)
    return total


def rotated(values, cos, sin):
    blocks = []
    for start in range(0, values.shape[1], DH):
        u = values[:, start : start + DH]
        blocks.append(u * cos + pltpu.roll(u, DH // 2, 1) * sin)
    return jnp.concatenate(blocks, axis=1)


def fresh_kernel(n_head, head, ids_ref, *refs):
    x_refs, mod_refs = refs[:n_head], refs[n_head : 2 * n_head]
    w_ref, cos_ref, sin_ref = refs[2 * n_head : 2 * n_head + 3]
    stale_ref, a_ref, kv_ref = refs[2 * n_head + 3 :]
    kv_ref[:2] = stale_ref[...]
    parts = normalized(0, x_refs, mod_refs, ids_ref)
    for number, part in enumerate(parts):
        a_ref[number] = part
    keys = rotated(projected(parts, w_ref, 0, head), cos_ref[...], sin_ref[...])
    kv_ref[2] = keys.astype(BF16)
    kv_ref[3] = projected(parts, w_ref, 1, head).astype(BF16)


def rest_kernel(n_head, head, ids_ref, *refs):
    x_refs, mod_refs = refs[:n_head], refs[n_head : 2 * n_head]
    w_ref, cos_ref, sin_ref, a_ref, w_far, q_ref, kv1_ref, wq_ref, sem = refs[2 * n_head :]
    copy = pltpu.make_async_copy(w_far.at[0], wq_ref.at[0], sem)
    copy.start()
    rows = a_ref.shape[1]
    parts = normalized(1, x_refs, mod_refs, ids_ref)
    cos, sin = cos_ref[...], sin_ref[...]
    both = [jnp.concatenate([a_ref[k], part], axis=0) for k, part in enumerate(parts)]
    kv1_ref[0] = rotated(projected(parts, w_ref, 0, head), cos, sin).astype(BF16)
    kv1_ref[1] = projected(parts, w_ref, 1, head).astype(BF16)
    copy.wait()
    queries = projected(both, wq_ref, 0, head)
    for step in range(STEPS):
        spot = slice(step * rows, (step + 1) * rows)
        q_ref[step] = rotated(queries[spot], cos, sin).astype(BF16)


def split3(values):
    high = values.astype(BF16).astype(F32)
    middle = (values - high).astype(BF16).astype(F32)
    return [high, middle, values - high - middle]


def attend_kernel(q_ref, mate_ref, kv1_ref, *refs):
    kv_refs, out_ref = refs[:PLANE], refs[PLANE]
    blocks, _, rows, cols = kv_refs[0].shape
    old_rows = PLANE * blocks * rows
    shape = (2 * rows, old_rows + rows)
    mine = lax.broadcasted_iota(jnp.int32, shape, 0) < rows
    stray = jnp.where(mine, 0, PLANE * blocks)
    drop = lax.broadcasted_iota(jnp.int32, shape, 1) // rows == stray
    lane = lax.broadcasted_iota(jnp.int32, (2 * rows, DH), 1)
    for step in range(STEPS):
        fresh = (kv_refs[0].at[0, 2:], kv1_ref)[step]
        stats = jnp.zeros((2 * rows, DH), F32)
        mixed = []
        for head in range(cols // DH):
            lanes = slice(head * DH, (head + 1) * DH)

            def rows_of(kind):
                old = [ref[:, 2 * step + kind, :, lanes].reshape(blocks * rows, DH) for ref in kv_refs]
                return jnp.concatenate([*old, fresh[kind, :, lanes]], axis=0)

            queries = jnp.concatenate([q_ref[step, :, lanes], mate_ref[step, :, lanes]], axis=0)
            scores = lax.dot_general(queries, rows_of(0), NT, preferred_element_type=F32)
            scores = jnp.where(drop, -1e30, scores * (1.0 / math.sqrt(DH)))
            top = jnp.max(scores, axis=1, keepdims=True)
            weights = jnp.exp(scores - top)
            totals = jnp.sum(weights, axis=1, keepdims=True)
            mixed.append(
                jnp.dot(weights.astype(BF16), rows_of(1), preferred_element_type=F32) / totals
            )
            for place, piece in enumerate(split3(top) + split3(totals)):
                stats = jnp.where(lane == head * 8 + place, piece, stats)
        packed = jnp.concatenate([*mixed, stats], axis=1).astype(BF16)
        for mate in range(2):
            start = (mate * STEPS + step) * rows
            out_ref[start : start + rows, :] = packed[mate * rows : (mate + 1) * rows]


def merge_kernel(part_ref, other_ref, o_ref):
    rows = part_ref.shape[0] // 2
    cols = o_ref.shape[1]
    source = lax.broadcasted_iota(jnp.int32, (DH, DH), 0)
    parts = [
        part_ref[...],
        jnp.concatenate([other_ref[rows:], other_ref[:rows]], axis=0),
    ]
    for head in range(cols // DH):
        lanes = slice(head * DH, (head + 1) * DH)

        def spread(part, first):
            pick = (source >= head * 8 + first) & (source < head * 8 + first + 3)
            return jnp.dot(part[:, cols:], pick.astype(F32).astype(BF16), preferred_element_type=F32)

        tops = [spread(part, 0) for part in parts]
        best = functools.reduce(jnp.maximum, tops)
        scales = [spread(part, 3) * jnp.exp(t - best) for part, t in zip(parts, tops)]
        mixed = sum(s * part[:, lanes].astype(F32) for s, part in zip(scales, parts))
        o_ref[:, lanes] = (mixed / sum(scales)).astype(BF16)


def project_kernel(n_head, n_patch, bit, patch, head, *refs):
    o_ref, own_ref, next_ref, far_ref, out_ref, sums = refs
    slot = head[0] ^ bit ^ (patch[0] // (n_patch // n_head))
    odd = head[0] % 2
    blocks = ((0, own_ref), (1 + odd, next_ref), (2 - odd, far_ref.at[0]), (3, far_ref.at[1]))
    for near, w_ref in blocks:
        sums[(patch[0] % PLANE) ^ near] = lax.dot_general(
            o_ref[...], w_ref[slot], NT, preferred_element_type=F32
        )
    out = jnp.concatenate([sums[c] for c in range(PLANE)], axis=1)
    out_ref[...] = out.astype(out_ref.dtype)


def gate_kernel(n_patch, patch, ids_ref, mod_ref, *refs):
    sum_refs, (own_out, mate_out) = refs[:-2], refs[-2:]
    total = sum(ref[...].astype(F32) for ref in sum_refs)
    rows, width = total.shape
    each = rows // 2 // STEPS
    second = (patch[0] // PLANE) % 2 == 1
    for step in range(STEPS):
        gate = table_row(mod_ref, 2, ids_ref, step)
        gate = jnp.where(second, gate[:, width:], gate[:, :width])
        for mate, ref in enumerate((own_out, mate_out)):
            start = mate * (rows // 2) + step * each
            ref[step] = (gate * total[start : start + each]).astype(BF16)


def in_hbm(values):
    return pltpu.with_memory_space_constraint(values, pltpu.HBM)


def call(kernel, shapes, ins, scratch=(), flops=0, size=0, limit=16):
    return pl.pallas_call(
        kernel,
        out_shape=shapes,
        in_specs=ins,
        out_specs=jax.tree.map(lambda _: VMEM, shapes),
        scratch_shapes=scratch,
        compiler_params=pltpu.CompilerParams(vmem_limit_bytes=limit * MIB),
        cost_estimate=pl.CostEstimate(flops=flops, bytes_accessed=size, transcendentals=0),
    )


def body(n_patch, n_head, inputs, stale_kv, w_qkv, w_out, mod_table, step_ids, slab_order):
    rows, feats = inputs.shape[1:]
    cols = w_qkv.shape[2]
    piece = w_out.shape[1]
    patch = lax.axis_index("patch").astype(jnp.int32)
    head = lax.axis_index("head").astype(jnp.int32)
    shaped = jax.ShapeDtypeStruct

    x_parts = [swap(inputs, "head", n_head, k) for k in range(1, n_head)]
    mod_parts = [swap(mod_table, "head", n_head, k) for k in range(1, n_head)]
    first = (jnp.transpose(w_qkv, (1, 0, 2)), inputs, jnp.transpose(mod_table, (1, 0, 2)), stale_kv)
    w, x_own, mod_own, stale, ids, cos, sin = call(
        load_kernel,
        (pltpu.VMEM((2, *first[0].shape[1:]), BF16),)
        + tuple(pltpu.VMEM(v.shape, v.dtype) for v in first[1:])
        + (shaped((8, DH), jnp.int32), shaped((rows, DH), F32), shaped((rows, DH), F32)),
        [SMEM] * 2 + [ANY] * len(first),
        [pltpu.SemaphoreType.DMA((5,))],
        size=2 * w_qkv.size,
    )(in_hbm(step_ids), slab_order, *map(in_hbm, first))
    x_parts = [x_own] + x_parts
    mod_parts = [mod_own] + [jnp.transpose(part, (1, 0, 2)) for part in mod_parts]

    def across(values, k):
        return swap(values, "patch", n_patch, k)

    def line_of(values):
        return [values] + [across(values, k) for k in range(2 * PLANE, n_patch, 2 * PLANE)]

    def plane_of(values):
        return [values] + [across(values, k) for k in range(1, PLANE)]

    def turn(values, first):
        pairs = [
            (p * n_head + h, (p ^ (1 if (h % 2 == 0) == first else 2)) * n_head + h)
            for p in range(n_patch)
            for h in range(n_head)
        ]
        return lax.ppermute(values, ("patch", "head"), pairs)

    w_pair = line_of(w_out.T)

    kv_shape = shaped((2, rows, cols), BF16)
    common = (head[None], ids, *x_parts, *mod_parts, w, cos, sin)
    specs = [SMEM] + [VMEM] * (2 * n_head + 4)
    a, kv = call(
        functools.partial(fresh_kernel, n_head),
        (shaped((n_head, rows, feats), BF16), shaped((4, rows, cols), BF16)),
        specs + [VMEM],
        flops=4 * rows * w_qkv.size // 3,
        size=2 * w_qkv.size,
    )(*common, stale)
    q, kv1 = call(
        functools.partial(rest_kernel, n_head),
        (kv_shape, kv_shape),
        specs + [VMEM, ANY],
        [pltpu.VMEM((1, *first[0].shape[1:]), BF16), pltpu.SemaphoreType.DMA],
        8 * rows * w_qkv.size // 3,
        2 * w_qkv.size,
    )(*common, a, in_hbm(first[0]))

    kv_pair = line_of(kv)
    q_mate = across(q, PLANE)
    kv_pair, w_pair, kv1 = lax.optimization_barrier((kv_pair, w_pair, kv1))
    w_pair = jnp.stack(w_pair)
    w_next = turn(w_pair, True)
    kv_plane = plane_of(jnp.stack(kv_pair))
    w_next, q_mate, kv_plane = lax.optimization_barrier((w_next, q_mate, kv_plane))
    w_far = turn(jnp.stack([w_pair, w_next]), False)
    tall = 2 * STEPS * rows
    part = call(
        attend_kernel,
        shaped((tall, cols + DH), BF16),
        [VMEM] * (3 + PLANE),
        flops=4 * STEPS * rows * n_patch * rows * cols,
    )(q, q_mate, kv1, *kv_plane)
    o = call(merge_kernel, shaped((tall, cols), BF16), [VMEM] * 2)(part, across(part, PLANE))
    wide = PLANE * piece

    def project(bit, dtype):
        return call(
            functools.partial(project_kernel, n_head, n_patch, bit),
            shaped((tall, wide), dtype),
            [SMEM] * 2 + [VMEM] * 4,
            [pltpu.VMEM((PLANE, tall, piece), F32)],
            2 * tall * wide * cols,
            2 * wide * cols,
        )(patch[None], head[None], o, w_pair, w_next, w_far)

    sums = [swap(project(k, BF16), "head", n_head, k) for k in range(1, n_head)]
    sums = [project(0, F32)] + sums
    out_half = shaped((STEPS, rows, wide), BF16)
    out_own, out_mate = call(
        functools.partial(gate_kernel, n_patch),
        (out_half, out_half),
        [SMEM] + [VMEM] * (2 + n_head),
    )(patch[None], ids, mod_own, *sums)
    out_back = across(out_mate, PLANE)
    second = (patch // PLANE) % 2 == 1
    return jnp.concatenate(
        [jnp.where(second, out_back, out_own), jnp.where(second, out_own, out_back)], axis=2
    )


def solution(mesh):
    in_specs = (
        P(None, "patch", "head"),
        P(None, "patch", "head"),
        P(None, None, "head"),
        P("head", "patch"),
        P(None, None, "head"),
        P(),
        P("patch"),
    )
    run = functools.partial(body, mesh.shape["patch"], mesh.shape["head"])
    return jax.shard_map(
        run, mesh=mesh, in_specs=in_specs, out_specs=P(None, "patch", "head"), check_vma=False
    )
```

```python
import functools
import math

import jax
import jax.numpy as jnp
from jax import lax
from jax.experimental import pallas as pl
from jax.experimental.pallas import tpu as pltpu
from jax.sharding import PartitionSpec as P

DH = 128
STEPS = 2
PLANE = 4
MIB = 1024 * 1024
VMEM = pl.BlockSpec(memory_space=pltpu.VMEM)
SMEM = pl.BlockSpec(memory_space=pltpu.SMEM)
ANY = pl.BlockSpec(memory_space=pl.ANY)
BF16, F32 = jnp.bfloat16, jnp.float32
NT = (((1,), (1,)), ((), ()))


def swap(values, axis, count, bit):
    return lax.ppermute(values, axis, [(i, i ^ bit) for i in range(count)])


def load_kernel(ids, slab, w_ref, x_ref, mod_ref, stale_ref, w_out, x_out, mod_out, stale_out, *refs):
    ids_out, cos_ref, sin_ref, sems = refs
    copies = [
        pltpu.make_async_copy(w_ref.at[slot], w_out.at[slot], sems.at[slot])
        for slot in range(3)
    ]
    copies.append(pltpu.make_async_copy(x_ref, x_out, sems.at[3]))
    copies.append(pltpu.make_async_copy(mod_ref, mod_out, sems.at[4]))
    copies.append(pltpu.make_async_copy(stale_ref, stale_out, sems.at[5]))
    for copy in copies:
        copy.start()
    row = lax.broadcasted_iota(jnp.int32, ids_out.shape, 0)
    tile = jnp.zeros(ids_out.shape, jnp.int32)
    for step in range(STEPS):
        tile = jnp.where(row == step, ids[step], tile)
    ids_out[...] = tile
    rows, half = cos_ref.shape[0], DH // 2
    lane = lax.broadcasted_iota(jnp.int32, cos_ref.shape, 1)
    spot = slab[0] * rows + lax.broadcasted_iota(jnp.int32, cos_ref.shape, 0)
    power = jnp.where(lane < half, lane, lane - half).astype(F32) * (-2.0 / DH)
    angle = spot.astype(F32) * jnp.exp(power * math.log(10000.0))
    cos_ref[...] = jnp.cos(angle)
    sin = jnp.sin(angle)
    sin_ref[...] = jnp.where(lane < half, -sin, sin)
    for copy in copies:
        copy.wait()


def table_row(mod_ref, kind, ids_ref, step):
    chosen = ids_ref[step : step + 1, :1]
    table = mod_ref[kind]
    return sum(
        jnp.where(chosen == r, table[r : r + 1], 0.0) for r in range(table.shape[0])
    )


def normalized(step, x_refs, mod_refs, ids_ref):
    hidden = [ref[step].astype(F32) for ref in x_refs]
    width = sum(part.shape[1] for part in hidden)
    mean = sum(jnp.sum(part, axis=1, keepdims=True) for part in hidden) / width
    square = sum(jnp.sum(part * part, axis=1, keepdims=True) for part in hidden) / width
    inv = lax.rsqrt(square - mean * mean + 1e-06)
    parts = []
    for part, mod_ref in zip(hidden, mod_refs):
        shift = table_row(mod_ref, 0, ids_ref, step)
        scale = table_row(mod_ref, 1, ids_ref, step)
        parts.append(((part - mean) * inv * (1.0 + scale) + shift).astype(BF16))
    return parts


def projected(parts, w_ref, slot, head):
    feats = parts[0].shape[1]
    total = jnp.zeros((parts[0].shape[0], w_ref.shape[2]), F32)
    for number, part in enumerate(parts):
        start = pl.multiple_of((head[0] ^ number) * feats, feats)
        w = w_ref[slot, pl.ds(start, feats), :]
        total += jnp.dot(part, w, preferred_element_type=F32)
    return total


def rotated(values, cos, sin):
    blocks = []
    for start in range(0, values.shape[1], DH):
        u = values[:, start : start + DH]
        blocks.append(u * cos + pltpu.roll(u, DH // 2, 1) * sin)
    return jnp.concatenate(blocks, axis=1)


def qkv_kernel(n_head, head, ids_ref, *refs):
    x_refs, mod_refs = refs[:n_head], refs[n_head : 2 * n_head]
    w_ref, cos_ref, sin_ref, stale_ref, q_ref, kv_ref, kv1_ref = refs[2 * n_head :]
    rows = x_refs[0].shape[1]
    steps = [normalized(step, x_refs, mod_refs, ids_ref) for step in range(STEPS)]
    parts = [jnp.concatenate(pair, axis=0) for pair in zip(*steps)]
    cos = jnp.concatenate([cos_ref[...]] * STEPS, axis=0)
    sin = jnp.concatenate([sin_ref[...]] * STEPS, axis=0)
    queries = rotated(projected(parts, w_ref, 0, head), cos, sin).astype(BF16)
    keys = rotated(projected(parts, w_ref, 1, head), cos, sin).astype(BF16)
    values = projected(parts, w_ref, 2, head).astype(BF16)
    for step in range(STEPS):
        spot = slice(step * rows, (step + 1) * rows)
        q_ref[step] = queries[spot]
    kv_ref[:2] = stale_ref[...]
    kv_ref[2], kv_ref[3] = keys[:rows], values[:rows]
    kv1_ref[0], kv1_ref[1] = keys[rows:], values[rows:]


def split3(values):
    high = values.astype(BF16).astype(F32)
    middle = (values - high).astype(BF16).astype(F32)
    return [high, middle, values - high - middle]


def attend_kernel(q_ref, mate_ref, kv1_ref, *refs):
    kv_refs, out_ref = refs[:PLANE], refs[PLANE]
    blocks, _, rows, cols = kv_refs[0].shape
    old_rows = PLANE * blocks * rows
    shape = (2 * rows, old_rows + rows)
    mine = lax.broadcasted_iota(jnp.int32, shape, 0) < rows
    stray = jnp.where(mine, 0, PLANE * blocks)
    drop = lax.broadcasted_iota(jnp.int32, shape, 1) // rows == stray
    lane = lax.broadcasted_iota(jnp.int32, (2 * rows, DH), 1)
    for step in range(STEPS):
        fresh = (kv_refs[0].at[0, 2:], kv1_ref)[step]
        stats = jnp.zeros((2 * rows, DH), F32)
        mixed = []
        for head in range(cols // DH):
            lanes = slice(head * DH, (head + 1) * DH)

            def rows_of(kind):
                old = [ref[:, 2 * step + kind, :, lanes].reshape(blocks * rows, DH) for ref in kv_refs]
                return jnp.concatenate([*old, fresh[kind, :, lanes]], axis=0)

            queries = jnp.concatenate([q_ref[step, :, lanes], mate_ref[step, :, lanes]], axis=0)
            scores = lax.dot_general(queries, rows_of(0), NT, preferred_element_type=F32)
            scores = jnp.where(drop, -1e30, scores * (1.0 / math.sqrt(DH)))
            top = jnp.max(scores, axis=1, keepdims=True)
            weights = jnp.exp(scores - top)
            totals = jnp.sum(weights, axis=1, keepdims=True)
            mixed.append(
                jnp.dot(weights.astype(BF16), rows_of(1), preferred_element_type=F32) / totals
            )
            for place, piece in enumerate(split3(top) + split3(totals)):
                stats = jnp.where(lane == head * 8 + place, piece, stats)
        packed = jnp.concatenate([*mixed, stats], axis=1).astype(BF16)
        for mate in range(2):
            start = (mate * STEPS + step) * rows
            out_ref[start : start + rows, :] = packed[mate * rows : (mate + 1) * rows]


def merge_kernel(part_ref, other_ref, o_ref):
    rows = part_ref.shape[0] // 2
    cols = o_ref.shape[1]
    source = lax.broadcasted_iota(jnp.int32, (DH, DH), 0)
    parts = [
        part_ref[...],
        jnp.concatenate([other_ref[rows:], other_ref[:rows]], axis=0),
    ]
    for head in range(cols // DH):
        lanes = slice(head * DH, (head + 1) * DH)

        def spread(part, first):
            pick = (source >= head * 8 + first) & (source < head * 8 + first + 3)
            return jnp.dot(part[:, cols:], pick.astype(F32).astype(BF16), preferred_element_type=F32)

        tops = [spread(part, 0) for part in parts]
        best = functools.reduce(jnp.maximum, tops)
        scales = [spread(part, 3) * jnp.exp(t - best) for part, t in zip(parts, tops)]
        mixed = sum(s * part[:, lanes].astype(F32) for s, part in zip(scales, parts))
        o_ref[:, lanes] = (mixed / sum(scales)).astype(BF16)


def project_kernel(n_head, n_patch, bit, patch, head, *refs):
    o_ref, own_ref, next_ref, far_ref, out_ref, sums = refs
    slot = head[0] ^ bit ^ (patch[0] // (n_patch // n_head))
    odd = head[0] % 2
    blocks = ((0, own_ref), (1 + odd, next_ref), (2 - odd, far_ref.at[0]), (3, far_ref.at[1]))
    for near, w_ref in blocks:
        sums[(patch[0] % PLANE) ^ near] = lax.dot_general(
            o_ref[...], w_ref[slot], NT, preferred_element_type=F32
        )
    out = jnp.concatenate([sums[c] for c in range(PLANE)], axis=1)
    out_ref[...] = out.astype(out_ref.dtype)


def gate_kernel(n_patch, patch, ids_ref, mod_ref, *refs):
    sum_refs, (own_out, mate_out) = refs[:-2], refs[-2:]
    total = sum(ref[...].astype(F32) for ref in sum_refs)
    rows, width = total.shape
    each = rows // 2 // STEPS
    second = (patch[0] // PLANE) % 2 == 1
    for step in range(STEPS):
        gate = table_row(mod_ref, 2, ids_ref, step)
        gate = jnp.where(second, gate[:, width:], gate[:, :width])
        for mate, ref in enumerate((own_out, mate_out)):
            start = mate * (rows // 2) + step * each
            ref[step] = (gate * total[start : start + each]).astype(BF16)


def in_hbm(values):
    return pltpu.with_memory_space_constraint(values, pltpu.HBM)


def call(kernel, shapes, ins, scratch=(), flops=0, size=0, limit=16):
    return pl.pallas_call(
        kernel,
        out_shape=shapes,
        in_specs=ins,
        out_specs=jax.tree.map(lambda _: VMEM, shapes),
        scratch_shapes=scratch,
        compiler_params=pltpu.CompilerParams(vmem_limit_bytes=limit * MIB),
        cost_estimate=pl.CostEstimate(flops=flops, bytes_accessed=size, transcendentals=0),
    )


def body(n_patch, n_head, inputs, stale_kv, w_qkv, w_out, mod_table, step_ids, slab_order):
    rows, feats = inputs.shape[1:]
    cols = w_qkv.shape[2]
    piece = w_out.shape[1]
    patch = lax.axis_index("patch").astype(jnp.int32)
    head = lax.axis_index("head").astype(jnp.int32)
    shaped = jax.ShapeDtypeStruct

    x_parts = [swap(inputs, "head", n_head, k) for k in range(1, n_head)]
    mod_parts = [swap(mod_table, "head", n_head, k) for k in range(1, n_head)]
    first = (jnp.transpose(w_qkv, (1, 0, 2)), inputs, jnp.transpose(mod_table, (1, 0, 2)), stale_kv)
    w, x_own, mod_own, stale, ids, cos, sin = call(
        load_kernel,
        tuple(pltpu.VMEM(v.shape, v.dtype) for v in first)
        + (shaped((8, DH), jnp.int32), shaped((rows, DH), F32), shaped((rows, DH), F32)),
        [SMEM] * 2 + [ANY] * len(first),
        [pltpu.SemaphoreType.DMA((6,))],
        size=2 * w_qkv.size,
    )(in_hbm(step_ids), slab_order, *map(in_hbm, first))
    x_parts = [x_own] + x_parts
    mod_parts = [mod_own] + [jnp.transpose(part, (1, 0, 2)) for part in mod_parts]

    def across(values, k):
        return swap(values, "patch", n_patch, k)

    def line_of(values):
        return [values] + [across(values, k) for k in range(2 * PLANE, n_patch, 2 * PLANE)]

    def plane_of(values):
        return [values] + [across(values, k) for k in range(1, PLANE)]

    def turn(values, first):
        pairs = [
            (p * n_head + h, (p ^ (1 if (h % 2 == 0) == first else 2)) * n_head + h)
            for p in range(n_patch)
            for h in range(n_head)
        ]
        return lax.ppermute(values, ("patch", "head"), pairs)

    w_pair = line_of(w_out.T)

    kv_shape = shaped((2, rows, cols), BF16)
    q, kv, kv1 = call(
        functools.partial(qkv_kernel, n_head),
        (kv_shape, shaped((4, rows, cols), BF16), kv_shape),
        [SMEM] + [VMEM] * (2 * n_head + 5),
        flops=2 * STEPS * rows * w_qkv.size,
        size=2 * w_qkv.size,
    )(head[None], ids, *x_parts, *mod_parts, w, cos, sin, stale)

    kv_pair = line_of(kv)
    q_mate = across(q, PLANE)
    w_pair, q = lax.optimization_barrier((w_pair, q))
    w_pair = jnp.stack(w_pair)
    w_next = turn(w_pair, True)
    kv_pair, q_mate = lax.optimization_barrier((kv_pair, q_mate))
    kv_plane = plane_of(jnp.stack(kv_pair))
    w_next, kv_plane = lax.optimization_barrier((w_next, kv_plane))
    w_far = turn(jnp.stack([w_pair, w_next]), False)
    tall = 2 * STEPS * rows
    part = call(
        attend_kernel,
        shaped((tall, cols + DH), BF16),
        [VMEM] * (3 + PLANE),
        flops=4 * STEPS * rows * n_patch * rows * cols,
    )(q, q_mate, kv1, *kv_plane)
    o = call(merge_kernel, shaped((tall, cols), BF16), [VMEM] * 2)(part, across(part, PLANE))
    wide = PLANE * piece

    def project(bit, dtype):
        return call(
            functools.partial(project_kernel, n_head, n_patch, bit),
            shaped((tall, wide), dtype),
            [SMEM] * 2 + [VMEM] * 4,
            [pltpu.VMEM((PLANE, tall, piece), F32)],
            2 * tall * wide * cols,
            2 * wide * cols,
        )(patch[None], head[None], o, w_pair, w_next, w_far)

    sums = [swap(project(k, BF16), "head", n_head, k) for k in range(1, n_head)]
    sums = [project(0, F32)] + sums
    out_half = shaped((STEPS, rows, wide), BF16)
    out_own, out_mate = call(
        functools.partial(gate_kernel, n_patch),
        (out_half, out_half),
        [SMEM] + [VMEM] * (2 + n_head),
    )(patch[None], ids, mod_own, *sums)
    out_back = across(out_mate, PLANE)
    second = (patch // PLANE) % 2 == 1
    return jnp.concatenate(
        [jnp.where(second, out_back, out_own), jnp.where(second, out_own, out_back)], axis=2
    )


def solution(mesh):
    in_specs = (
        P(None, "patch", "head"),
        P(None, "patch", "head"),
        P(None, None, "head"),
        P("head", "patch"),
        P(None, None, "head"),
        P(),
        P("patch"),
    )
    run = functools.partial(body, mesh.shape["patch"], mesh.shape["head"])
    return jax.shard_map(
        run, mesh=mesh, in_specs=in_specs, out_specs=P(None, "patch", "head"), check_vma=False
    )
```

```python
import functools
import math

import jax
import jax.numpy as jnp
from jax import lax
from jax.experimental import pallas as pl
from jax.experimental.pallas import tpu as pltpu
from jax.sharding import PartitionSpec as P

DH = 128
STEPS = 2
PLANE = 4
MIB = 1024 * 1024
VMEM = pl.BlockSpec(memory_space=pltpu.VMEM)
SMEM = pl.BlockSpec(memory_space=pltpu.SMEM)
ANY = pl.BlockSpec(memory_space=pl.ANY)
BF16, F32 = jnp.bfloat16, jnp.float32
NT = (((1,), (1,)), ((), ()))


def swap(values, axis, count, bit):
    return lax.ppermute(values, axis, [(i, i ^ bit) for i in range(count)])


def load_kernel(ids, slab, w_ref, x_ref, mod_ref, w_out, x_out, mod_out, *refs):
    ids_out, cos_ref, sin_ref, sems = refs
    copies = [
        pltpu.make_async_copy(w_ref.at[slot], w_out.at[slot], sems.at[slot])
        for slot in range(3)
    ]
    copies.append(pltpu.make_async_copy(x_ref, x_out, sems.at[3]))
    copies.append(pltpu.make_async_copy(mod_ref, mod_out, sems.at[4]))
    for copy in copies:
        copy.start()
    row = lax.broadcasted_iota(jnp.int32, ids_out.shape, 0)
    tile = jnp.zeros(ids_out.shape, jnp.int32)
    for step in range(STEPS):
        tile = jnp.where(row == step, ids[step], tile)
    ids_out[...] = tile
    rows, half = cos_ref.shape[0], DH // 2
    lane = lax.broadcasted_iota(jnp.int32, cos_ref.shape, 1)
    spot = slab[0] * rows + lax.broadcasted_iota(jnp.int32, cos_ref.shape, 0)
    power = jnp.where(lane < half, lane, lane - half).astype(F32) * (-2.0 / DH)
    angle = spot.astype(F32) * jnp.exp(power * math.log(10000.0))
    cos_ref[...] = jnp.cos(angle)
    sin = jnp.sin(angle)
    sin_ref[...] = jnp.where(lane < half, -sin, sin)
    for copy in copies:
        copy.wait()


def table_row(mod_ref, kind, ids_ref, step):
    chosen = ids_ref[step : step + 1, :1]
    table = mod_ref[kind]
    return sum(
        jnp.where(chosen == r, table[r : r + 1], 0.0) for r in range(table.shape[0])
    )


def normalized(step, x_refs, mod_refs, ids_ref):
    hidden = [ref[step].astype(F32) for ref in x_refs]
    width = sum(part.shape[1] for part in hidden)
    mean = sum(jnp.sum(part, axis=1, keepdims=True) for part in hidden) / width
    square = sum(jnp.sum(part * part, axis=1, keepdims=True) for part in hidden) / width
    inv = lax.rsqrt(square - mean * mean + 1e-06)
    parts = []
    for part, mod_ref in zip(hidden, mod_refs):
        shift = table_row(mod_ref, 0, ids_ref, step)
        scale = table_row(mod_ref, 1, ids_ref, step)
        parts.append(((part - mean) * inv * (1.0 + scale) + shift).astype(BF16))
    return parts


def projected(parts, w_ref, slot, head):
    feats = parts[0].shape[1]
    total = jnp.zeros((parts[0].shape[0], w_ref.shape[2]), F32)
    for number, part in enumerate(parts):
        start = pl.multiple_of((head[0] ^ number) * feats, feats)
        w = w_ref[slot, pl.ds(start, feats), :]
        total += jnp.dot(part, w, preferred_element_type=F32)
    return total


def rotated(values, cos, sin):
    blocks = []
    for start in range(0, values.shape[1], DH):
        u = values[:, start : start + DH]
        blocks.append(u * cos + pltpu.roll(u, DH // 2, 1) * sin)
    return jnp.concatenate(blocks, axis=1)


def qkv_kernel(n_head, head, ids_ref, *refs):
    x_refs, mod_refs = refs[:n_head], refs[n_head : 2 * n_head]
    w_ref, cos_ref, sin_ref = refs[2 * n_head : 2 * n_head + 3]
    q_ref, kv0_ref, kv1_ref = refs[-3:]
    rows = x_refs[0].shape[1]
    steps = [normalized(step, x_refs, mod_refs, ids_ref) for step in range(STEPS)]
    parts = [jnp.concatenate(pair, axis=0) for pair in zip(*steps)]
    cos = jnp.concatenate([cos_ref[...]] * STEPS, axis=0)
    sin = jnp.concatenate([sin_ref[...]] * STEPS, axis=0)
    queries = rotated(projected(parts, w_ref, 0, head), cos, sin).astype(BF16)
    keys = rotated(projected(parts, w_ref, 1, head), cos, sin).astype(BF16)
    values = projected(parts, w_ref, 2, head).astype(BF16)
    for step in range(STEPS):
        spot = slice(step * rows, (step + 1) * rows)
        q_ref[step] = queries[spot]
    kv0_ref[0], kv0_ref[1] = keys[:rows], values[:rows]
    kv1_ref[0], kv1_ref[1] = keys[rows:], values[rows:]


def split3(values):
    high = values.astype(BF16).astype(F32)
    middle = (values - high).astype(BF16).astype(F32)
    return [high, middle, values - high - middle]


def attend_kernel(q_ref, mate_ref, kv1_ref, *refs):
    own_ref, next_ref, far_ref = refs[:3]
    cargo_refs = [own_ref, next_ref, far_ref.at[0], far_ref.at[1]]
    kv_refs, out_ref = refs[3 : 3 + PLANE], refs[3 + PLANE]
    blocks, _, rows, cols = kv_refs[0].shape
    skip = own_ref.shape[1] - 2 * rows
    old_rows = PLANE * blocks * rows
    shape = (2 * rows, old_rows + rows)
    mine = lax.broadcasted_iota(jnp.int32, shape, 0) < rows
    stray = jnp.where(mine, 0, PLANE * blocks)
    drop = lax.broadcasted_iota(jnp.int32, shape, 1) // rows == stray
    lane = lax.broadcasted_iota(jnp.int32, (2 * rows, DH), 1)
    for step in range(STEPS):
        fresh = (kv_refs[0].at[0], kv1_ref)[step]
        stats = jnp.zeros((2 * rows, DH), F32)
        mixed = []
        for head in range(cols // DH):
            lanes = slice(head * DH, (head + 1) * DH)

            def rows_of(kind):
                if step:
                    old = [ref[:, kind, :, lanes] for ref in kv_refs]
                else:
                    spot = slice(skip + kind * rows, skip + (kind + 1) * rows)
                    old = [ref[:, spot, lanes] for ref in cargo_refs]
                old = [piece.reshape(blocks * rows, DH) for piece in old]
                return jnp.concatenate([*old, fresh[kind, :, lanes]], axis=0)

            queries = jnp.concatenate([q_ref[step, :, lanes], mate_ref[step, :, lanes]], axis=0)
            scores = lax.dot_general(queries, rows_of(0), NT, preferred_element_type=F32)
            scores = jnp.where(drop, -1e30, scores * (1.0 / math.sqrt(DH)))
            top = jnp.max(scores, axis=1, keepdims=True)
            weights = jnp.exp(scores - top)
            totals = jnp.sum(weights, axis=1, keepdims=True)
            mixed.append(
                jnp.dot(weights.astype(BF16), rows_of(1), preferred_element_type=F32) / totals
            )
            for place, piece in enumerate(split3(top) + split3(totals)):
                stats = jnp.where(lane == head * 8 + place, piece, stats)
        packed = jnp.concatenate([*mixed, stats], axis=1).astype(BF16)
        for mate in range(2):
            start = (mate * STEPS + step) * rows
            out_ref[start : start + rows, :] = packed[mate * rows : (mate + 1) * rows]


def merge_kernel(part_ref, other_ref, o_ref):
    rows = part_ref.shape[0] // 2
    cols = o_ref.shape[1]
    source = lax.broadcasted_iota(jnp.int32, (DH, DH), 0)
    parts = [
        part_ref[...],
        jnp.concatenate([other_ref[rows:], other_ref[:rows]], axis=0),
    ]
    for head in range(cols // DH):
        lanes = slice(head * DH, (head + 1) * DH)

        def spread(part, first):
            pick = (source >= head * 8 + first) & (source < head * 8 + first + 3)
            return jnp.dot(part[:, cols:], pick.astype(F32).astype(BF16), preferred_element_type=F32)

        tops = [spread(part, 0) for part in parts]
        best = functools.reduce(jnp.maximum, tops)
        scales = [spread(part, 3) * jnp.exp(t - best) for part, t in zip(parts, tops)]
        mixed = sum(s * part[:, lanes].astype(F32) for s, part in zip(scales, parts))
        o_ref[:, lanes] = (mixed / sum(scales)).astype(BF16)


def project_kernel(n_head, n_patch, bit, patch, head, *refs):
    o_ref, own_ref, next_ref, far_ref, out_ref, sums = refs
    slot = head[0] ^ bit ^ (patch[0] // (n_patch // n_head))
    odd = head[0] % 2
    blocks = ((0, own_ref), (1 + odd, next_ref), (2 - odd, far_ref.at[0]), (3, far_ref.at[1]))
    for near, w_ref in blocks:
        sums[(patch[0] % PLANE) ^ near] = lax.dot_general(
            o_ref[...], w_ref[slot, : sums.shape[2], :], NT, preferred_element_type=F32
        )
    out = jnp.concatenate([sums[c] for c in range(PLANE)], axis=1)
    out_ref[...] = out.astype(out_ref.dtype)


def gate_kernel(n_patch, patch, ids_ref, mod_ref, *refs):
    sum_refs, (own_out, mate_out) = refs[:-2], refs[-2:]
    total = sum(ref[...].astype(F32) for ref in sum_refs)
    rows, width = total.shape
    each = rows // 2 // STEPS
    second = (patch[0] // PLANE) % 2 == 1
    for step in range(STEPS):
        gate = table_row(mod_ref, 2, ids_ref, step)
        gate = jnp.where(second, gate[:, width:], gate[:, :width])
        for mate, ref in enumerate((own_out, mate_out)):
            start = mate * (rows // 2) + step * each
            ref[step] = (gate * total[start : start + each]).astype(BF16)


def in_hbm(values):
    return pltpu.with_memory_space_constraint(values, pltpu.HBM)


def call(kernel, shapes, ins, scratch=(), flops=0, size=0, limit=16):
    return pl.pallas_call(
        kernel,
        out_shape=shapes,
        in_specs=ins,
        out_specs=jax.tree.map(lambda _: VMEM, shapes),
        scratch_shapes=scratch,
        compiler_params=pltpu.CompilerParams(vmem_limit_bytes=limit * MIB),
        cost_estimate=pl.CostEstimate(flops=flops, bytes_accessed=size, transcendentals=0),
    )


def body(n_patch, n_head, inputs, stale_kv, w_qkv, w_out, mod_table, step_ids, slab_order):
    rows, feats = inputs.shape[1:]
    cols = w_qkv.shape[2]
    piece = w_out.shape[1]
    patch = lax.axis_index("patch").astype(jnp.int32)
    head = lax.axis_index("head").astype(jnp.int32)
    shaped = jax.ShapeDtypeStruct

    x_parts = [swap(inputs, "head", n_head, k) for k in range(1, n_head)]
    mod_parts = [swap(mod_table, "head", n_head, k) for k in range(1, n_head)]
    first = (jnp.transpose(w_qkv, (1, 0, 2)), inputs, jnp.transpose(mod_table, (1, 0, 2)))
    w, x_own, mod_own, ids, cos, sin = call(
        load_kernel,
        tuple(pltpu.VMEM(v.shape, v.dtype) for v in first)
        + (shaped((8, DH), jnp.int32), shaped((rows, DH), F32), shaped((rows, DH), F32)),
        [SMEM] * 2 + [ANY] * len(first),
        [pltpu.SemaphoreType.DMA((5,))],
        size=2 * w_qkv.size,
    )(in_hbm(step_ids), slab_order, *map(in_hbm, first))
    x_parts = [x_own] + x_parts
    mod_parts = [mod_own] + [jnp.transpose(part, (1, 0, 2)) for part in mod_parts]

    def across(values, k):
        return swap(values, "patch", n_patch, k)

    def line_of(values):
        return [values] + [across(values, k) for k in range(2 * PLANE, n_patch, 2 * PLANE)]

    def plane_of(values):
        return [values] + [across(values, k) for k in range(1, PLANE)]

    def turn(values, first):
        pairs = [
            (p * n_head + h, (p ^ (1 if (h % 2 == 0) == first else 2)) * n_head + h)
            for p in range(n_patch)
            for h in range(n_head)
        ]
        return lax.ppermute(values, ("patch", "head"), pairs)

    w_pair = line_of(w_out.T)

    stale_pair = line_of(stale_kv)
    kv_shape = shaped((2, rows, cols), BF16)
    q, kv, kv1 = call(
        functools.partial(qkv_kernel, n_head),
        (kv_shape,) * 3,
        [SMEM] + [VMEM] * (2 * n_head + 4),
        flops=2 * STEPS * rows * w_qkv.size,
        size=2 * w_qkv.size,
    )(head[None], ids, *x_parts, *mod_parts, w, cos, sin)

    kv_pair = line_of(kv)
    q_mate = across(q, PLANE)
    w_pair, stale_pair, q = lax.optimization_barrier((w_pair, stale_pair, q))
    cargo = jnp.stack(
        [
            jnp.concatenate([w_block, kv_block.reshape(2 * rows, cols)])
            for w_block, kv_block in zip(w_pair, stale_pair)
        ]
    )
    next_cargo = turn(cargo, True)
    kv_pair, q_mate = lax.optimization_barrier((kv_pair, q_mate))
    kv_plane = plane_of(jnp.stack(kv_pair))
    next_cargo, kv_pair = lax.optimization_barrier((next_cargo, kv_pair))
    far_cargo = turn(jnp.stack([cargo, next_cargo]), False)
    tall = 2 * STEPS * rows
    part = call(
        attend_kernel,
        shaped((tall, cols + DH), BF16),
        [VMEM] * (6 + PLANE),
        flops=4 * STEPS * rows * n_patch * rows * cols,
    )(q, q_mate, kv1, cargo, next_cargo, far_cargo, *kv_plane)
    o = call(merge_kernel, shaped((tall, cols), BF16), [VMEM] * 2)(part, across(part, PLANE))
    wide = PLANE * piece

    def project(bit, dtype):
        return call(
            functools.partial(project_kernel, n_head, n_patch, bit),
            shaped((tall, wide), dtype),
            [SMEM] * 2 + [VMEM] * 4,
            [pltpu.VMEM((PLANE, tall, piece), F32)],
            2 * tall * wide * cols,
            2 * wide * cols,
        )(patch[None], head[None], o, cargo, next_cargo, far_cargo)

    sums = [swap(project(k, BF16), "head", n_head, k) for k in range(1, n_head)]
    sums = [project(0, F32)] + sums
    out_half = shaped((STEPS, rows, wide), BF16)
    out_own, out_mate = call(
        functools.partial(gate_kernel, n_patch),
        (out_half, out_half),
        [SMEM] + [VMEM] * (2 + n_head),
    )(patch[None], ids, mod_own, *sums)
    out_back = across(out_mate, PLANE)
    second = (patch // PLANE) % 2 == 1
    return jnp.concatenate(
        [jnp.where(second, out_back, out_own), jnp.where(second, out_own, out_back)], axis=2
    )


def solution(mesh):
    in_specs = (
        P(None, "patch", "head"),
        P(None, "patch", "head"),
        P(None, None, "head"),
        P("head", "patch"),
        P(None, None, "head"),
        P(),
        P("patch"),
    )
    run = functools.partial(body, mesh.shape["patch"], mesh.shape["head"])
    return jax.shard_map(
        run, mesh=mesh, in_specs=in_specs, out_specs=P(None, "patch", "head"), check_vma=False
    )
```

```python
import functools
import math

import jax
import jax.numpy as jnp
from jax import lax
from jax.experimental import pallas as pl
from jax.experimental.pallas import tpu as pltpu
from jax.sharding import PartitionSpec as P

DH = 128
STEPS = 2
PLANE = 4
MIB = 1024 * 1024
VMEM = pl.BlockSpec(memory_space=pltpu.VMEM)
SMEM = pl.BlockSpec(memory_space=pltpu.SMEM)
ANY = pl.BlockSpec(memory_space=pl.ANY)
BF16, F32 = jnp.bfloat16, jnp.float32
NT = (((1,), (1,)), ((), ()))


def swap(values, axis, count, bit):
    return lax.ppermute(values, axis, [(i, i ^ bit) for i in range(count)])


def load_kernel(ids, slab, w_ref, x_ref, mod_ref, stale_ref, w_out, x_out, mod_out, stale_out, *refs):
    ids_out, cos_ref, sin_ref, sems = refs
    copies = [
        pltpu.make_async_copy(w_ref.at[slot], w_out.at[slot], sems.at[slot])
        for slot in range(3)
    ]
    copies.append(pltpu.make_async_copy(x_ref, x_out, sems.at[3]))
    copies.append(pltpu.make_async_copy(mod_ref, mod_out, sems.at[4]))
    copies.append(pltpu.make_async_copy(stale_ref, stale_out, sems.at[5]))
    for copy in copies:
        copy.start()
    row = lax.broadcasted_iota(jnp.int32, ids_out.shape, 0)
    tile = jnp.zeros(ids_out.shape, jnp.int32)
    for step in range(STEPS):
        tile = jnp.where(row == step, ids[step], tile)
    ids_out[...] = tile
    rows, half = cos_ref.shape[0], DH // 2
    lane = lax.broadcasted_iota(jnp.int32, cos_ref.shape, 1)
    spot = slab[0] * rows + lax.broadcasted_iota(jnp.int32, cos_ref.shape, 0)
    power = jnp.where(lane < half, lane, lane - half).astype(F32) * (-2.0 / DH)
    angle = spot.astype(F32) * jnp.exp(power * math.log(10000.0))
    cos_ref[...] = jnp.cos(angle)
    sin = jnp.sin(angle)
    sin_ref[...] = jnp.where(lane < half, -sin, sin)
    for copy in copies:
        copy.wait()


def table_row(mod_ref, kind, ids_ref, step):
    chosen = ids_ref[step : step + 1, :1]
    table = mod_ref[kind]
    return sum(
        jnp.where(chosen == r, table[r : r + 1], 0.0) for r in range(table.shape[0])
    )


def normalized(step, x_refs, mod_refs, ids_ref):
    hidden = [ref[step].astype(F32) for ref in x_refs]
    width = sum(part.shape[1] for part in hidden)
    mean = sum(jnp.sum(part, axis=1, keepdims=True) for part in hidden) / width
    square = sum(jnp.sum(part * part, axis=1, keepdims=True) for part in hidden) / width
    inv = lax.rsqrt(square - mean * mean + 1e-06)
    parts = []
    for part, mod_ref in zip(hidden, mod_refs):
        shift = table_row(mod_ref, 0, ids_ref, step)
        scale = table_row(mod_ref, 1, ids_ref, step)
        parts.append(((part - mean) * inv * (1.0 + scale) + shift).astype(BF16))
    return parts


def projected(parts, w_ref, slot, head):
    feats = parts[0].shape[1]
    total = jnp.zeros((parts[0].shape[0], w_ref.shape[2]), F32)
    for number, part in enumerate(parts):
        start = pl.multiple_of((head[0] ^ number) * feats, feats)
        w = w_ref[slot, pl.ds(start, feats), :]
        total += jnp.dot(part, w, preferred_element_type=F32)
    return total


def rotated(values, cos, sin):
    blocks = []
    for start in range(0, values.shape[1], DH):
        u = values[:, start : start + DH]
        blocks.append(u * cos + pltpu.roll(u, DH // 2, 1) * sin)
    return jnp.concatenate(blocks, axis=1)


def qkv_kernel(n_head, head, ids_ref, *refs):
    x_refs, mod_refs = refs[:n_head], refs[n_head : 2 * n_head]
    w_ref, cos_ref, sin_ref, stale_ref, q_ref, kv_ref, kv1_ref = refs[2 * n_head :]
    rows = x_refs[0].shape[1]
    steps = [normalized(step, x_refs, mod_refs, ids_ref) for step in range(STEPS)]
    parts = [jnp.concatenate(pair, axis=0) for pair in zip(*steps)]
    cos = jnp.concatenate([cos_ref[...]] * STEPS, axis=0)
    sin = jnp.concatenate([sin_ref[...]] * STEPS, axis=0)
    queries = rotated(projected(parts, w_ref, 0, head), cos, sin).astype(BF16)
    keys = rotated(projected(parts, w_ref, 1, head), cos, sin).astype(BF16)
    values = projected(parts, w_ref, 2, head).astype(BF16)
    for step in range(STEPS):
        spot = slice(step * rows, (step + 1) * rows)
        q_ref[step] = queries[spot]
    kv_ref[:2] = stale_ref[...]
    kv_ref[2], kv_ref[3] = keys[:rows], values[:rows]
    kv1_ref[0], kv1_ref[1] = keys[rows:], values[rows:]


def split3(values):
    high = values.astype(BF16).astype(F32)
    middle = (values - high).astype(BF16).astype(F32)
    return [high, middle, values - high - middle]


def attend_kernel(q_ref, mate_ref, kv1_ref, *refs):
    kv_refs, out_ref = refs[:PLANE], refs[PLANE]
    blocks, _, rows, cols = kv_refs[0].shape
    old_rows = PLANE * blocks * rows
    shape = (2 * rows, old_rows + rows)
    mine = lax.broadcasted_iota(jnp.int32, shape, 0) < rows
    stray = jnp.where(mine, 0, PLANE * blocks)
    drop = lax.broadcasted_iota(jnp.int32, shape, 1) // rows == stray
    lane = lax.broadcasted_iota(jnp.int32, (2 * rows, DH), 1)
    for step in range(STEPS):
        fresh = (kv_refs[0].at[0, 2:], kv1_ref)[step]
        stats = jnp.zeros((2 * rows, DH), F32)
        mixed = []
        for head in range(cols // DH):
            lanes = slice(head * DH, (head + 1) * DH)

            def rows_of(kind):
                old = [ref[:, 2 * step + kind, :, lanes].reshape(blocks * rows, DH) for ref in kv_refs]
                return jnp.concatenate([*old, fresh[kind, :, lanes]], axis=0)

            queries = jnp.concatenate([q_ref[step, :, lanes], mate_ref[step, :, lanes]], axis=0)
            scores = lax.dot_general(queries, rows_of(0), NT, preferred_element_type=F32)
            scores = jnp.where(drop, -1e30, scores * (1.0 / math.sqrt(DH)))
            top = jnp.max(scores, axis=1, keepdims=True)
            weights = jnp.exp(scores - top)
            totals = jnp.sum(weights, axis=1, keepdims=True)
            mixed.append(
                jnp.dot(weights.astype(BF16), rows_of(1), preferred_element_type=F32) / totals
            )
            for place, piece in enumerate(split3(top) + split3(totals)):
                stats = jnp.where(lane == head * 8 + place, piece, stats)
        packed = jnp.concatenate([*mixed, stats], axis=1).astype(BF16)
        for mate in range(2):
            start = (mate * STEPS + step) * rows
            out_ref[start : start + rows, :] = packed[mate * rows : (mate + 1) * rows]


def merge_kernel(part_ref, other_ref, o_ref):
    rows = part_ref.shape[0] // 2
    cols = o_ref.shape[1]
    source = lax.broadcasted_iota(jnp.int32, (DH, DH), 0)
    parts = [
        part_ref[...],
        jnp.concatenate([other_ref[rows:], other_ref[:rows]], axis=0),
    ]
    for head in range(cols // DH):
        lanes = slice(head * DH, (head + 1) * DH)

        def spread(part, first):
            pick = (source >= head * 8 + first) & (source < head * 8 + first + 3)
            return jnp.dot(part[:, cols:], pick.astype(F32).astype(BF16), preferred_element_type=F32)

        tops = [spread(part, 0) for part in parts]
        best = functools.reduce(jnp.maximum, tops)
        scales = [spread(part, 3) * jnp.exp(t - best) for part, t in zip(parts, tops)]
        mixed = sum(s * part[:, lanes].astype(F32) for s, part in zip(scales, parts))
        o_ref[:, lanes] = (mixed / sum(scales)).astype(BF16)


def project_kernel(n_head, n_patch, bit, patch, head, *refs):
    o_ref, w_refs, (out_ref, sums) = refs[0], refs[1 : 1 + PLANE], refs[1 + PLANE :]
    slot = head[0] ^ bit ^ (patch[0] // (n_patch // n_head))
    for near in range(PLANE):
        sums[(patch[0] % PLANE) ^ near] = lax.dot_general(
            o_ref[...], w_refs[near][slot], NT, preferred_element_type=F32
        )
    out = jnp.concatenate([sums[c] for c in range(PLANE)], axis=1)
    out_ref[...] = out.astype(out_ref.dtype)


def gate_kernel(n_patch, patch, ids_ref, mod_ref, *refs):
    sum_refs, (own_out, mate_out) = refs[:-2], refs[-2:]
    total = sum(ref[...].astype(F32) for ref in sum_refs)
    rows, width = total.shape
    each = rows // 2 // STEPS
    second = (patch[0] // PLANE) % 2 == 1
    for step in range(STEPS):
        gate = table_row(mod_ref, 2, ids_ref, step)
        gate = jnp.where(second, gate[:, width:], gate[:, :width])
        for mate, ref in enumerate((own_out, mate_out)):
            start = mate * (rows // 2) + step * each
            ref[step] = (gate * total[start : start + each]).astype(BF16)


def in_hbm(values):
    return pltpu.with_memory_space_constraint(values, pltpu.HBM)


def call(kernel, shapes, ins, scratch=(), flops=0, size=0, limit=16):
    return pl.pallas_call(
        kernel,
        out_shape=shapes,
        in_specs=ins,
        out_specs=jax.tree.map(lambda _: VMEM, shapes),
        scratch_shapes=scratch,
        compiler_params=pltpu.CompilerParams(vmem_limit_bytes=limit * MIB),
        cost_estimate=pl.CostEstimate(flops=flops, bytes_accessed=size, transcendentals=0),
    )


def body(n_patch, n_head, inputs, stale_kv, w_qkv, w_out, mod_table, step_ids, slab_order):
    rows, feats = inputs.shape[1:]
    cols = w_qkv.shape[2]
    piece = w_out.shape[1]
    patch = lax.axis_index("patch").astype(jnp.int32)
    head = lax.axis_index("head").astype(jnp.int32)
    shaped = jax.ShapeDtypeStruct

    x_parts = [swap(inputs, "head", n_head, k) for k in range(1, n_head)]
    mod_parts = [swap(mod_table, "head", n_head, k) for k in range(1, n_head)]
    first = (jnp.transpose(w_qkv, (1, 0, 2)), inputs, jnp.transpose(mod_table, (1, 0, 2)), stale_kv)
    w, x_own, mod_own, stale, ids, cos, sin = call(
        load_kernel,
        tuple(pltpu.VMEM(v.shape, v.dtype) for v in first)
        + (shaped((8, DH), jnp.int32), shaped((rows, DH), F32), shaped((rows, DH), F32)),
        [SMEM] * 2 + [ANY] * len(first),
        [pltpu.SemaphoreType.DMA((6,))],
        size=2 * w_qkv.size,
    )(in_hbm(step_ids), slab_order, *map(in_hbm, first))
    x_parts = [x_own] + x_parts
    mod_parts = [mod_own] + [jnp.transpose(part, (1, 0, 2)) for part in mod_parts]

    def across(values, k):
        return swap(values, "patch", n_patch, k)

    def line_of(values):
        return [values] + [across(values, k) for k in range(2 * PLANE, n_patch, 2 * PLANE)]

    def plane_of(values):
        return [values] + [across(values, k) for k in range(1, PLANE)]


    kv_shape = shaped((2, rows, cols), BF16)
    q, kv, kv1 = call(
        functools.partial(qkv_kernel, n_head),
        (kv_shape, shaped((4, rows, cols), BF16), kv_shape),
        [SMEM] + [VMEM] * (2 * n_head + 5),
        flops=2 * STEPS * rows * w_qkv.size,
        size=2 * w_qkv.size,
    )(head[None], ids, *x_parts, *mod_parts, w, cos, sin, stale)

    w_own, kv = lax.optimization_barrier((w_out.T, kv))
    kv_pair = line_of(kv)
    q_mate = across(q, PLANE)
    w_x = across(w_own, 1)
    w_late, q_mate = lax.optimization_barrier((w_own, q_mate))
    w_rest = jnp.stack(line_of(w_late)[1:])
    kv_plane = plane_of(jnp.stack(kv_pair))
    w_rest, q_mate = lax.optimization_barrier((w_rest, q_mate))
    w_y = across(jnp.stack([w_own, w_x]), 2)
    rest_y = across(w_rest, 2)
    rest_y, *kv_plane[1:] = lax.optimization_barrier((rest_y, *kv_plane[1:]))
    rest_x = across(jnp.stack([w_rest, rest_y]), 1)
    tall = 2 * STEPS * rows
    part = call(
        attend_kernel,
        shaped((tall, cols + DH), BF16),
        [VMEM] * (3 + PLANE),
        flops=4 * STEPS * rows * n_patch * rows * cols,
    )(q, q_mate, kv1, *kv_plane)
    o = call(merge_kernel, shaped((tall, cols), BF16), [VMEM] * 2)(part, across(part, PLANE))
    o, w_y, rest_x = lax.optimization_barrier((o, w_y, rest_x))
    near = [(w_own, w_rest), (w_x, rest_x[0]), (w_y[0], rest_y), (w_y[1], rest_x[1])]
    w_plane = [jnp.concatenate([first[None], others]) for first, others in near]
    wide = PLANE * piece

    def project(bit, dtype):
        return call(
            functools.partial(project_kernel, n_head, n_patch, bit),
            shaped((tall, wide), dtype),
            [SMEM] * 2 + [VMEM] * (1 + PLANE),
            [pltpu.VMEM((PLANE, tall, piece), F32)],
            2 * tall * wide * cols,
            2 * wide * cols,
        )(patch[None], head[None], o, *w_plane)

    sums = [swap(project(k, BF16), "head", n_head, k) for k in range(1, n_head)]
    sums = [project(0, F32)] + sums
    out_half = shaped((STEPS, rows, wide), BF16)
    out_own, out_mate = call(
        functools.partial(gate_kernel, n_patch),
        (out_half, out_half),
        [SMEM] + [VMEM] * (2 + n_head),
    )(patch[None], ids, mod_own, *sums)
    out_back = across(out_mate, PLANE)
    second = (patch // PLANE) % 2 == 1
    return jnp.concatenate(
        [jnp.where(second, out_back, out_own), jnp.where(second, out_own, out_back)], axis=2
    )


def solution(mesh):
    in_specs = (
        P(None, "patch", "head"),
        P(None, "patch", "head"),
        P(None, None, "head"),
        P("head", "patch"),
        P(None, None, "head"),
        P(),
        P("patch"),
    )
    run = functools.partial(body, mesh.shape["patch"], mesh.shape["head"])
    return jax.shard_map(
        run, mesh=mesh, in_specs=in_specs, out_specs=P(None, "patch", "head"), check_vma=False
    )
```

```python
import functools
import math

import jax
import jax.numpy as jnp
from jax import lax
from jax.experimental import pallas as pl
from jax.experimental.pallas import tpu as pltpu
from jax.sharding import PartitionSpec as P

DH = 128
STEPS = 2
PLANE = 4
MIB = 1024 * 1024
VMEM = pl.BlockSpec(memory_space=pltpu.VMEM)
SMEM = pl.BlockSpec(memory_space=pltpu.SMEM)
ANY = pl.BlockSpec(memory_space=pl.ANY)
BF16, F32 = jnp.bfloat16, jnp.float32
NT = (((1,), (1,)), ((), ()))


def swap(values, axis, count, bit):
    return lax.ppermute(values, axis, [(i, i ^ bit) for i in range(count)])


def load_kernel(ids, slab, w_ref, x_ref, mod_ref, stale_ref, w_out, x_out, mod_out, stale_out, *refs):
    ids_out, cos_ref, sin_ref, sems = refs
    copies = [
        pltpu.make_async_copy(w_ref.at[slot], w_out.at[slot], sems.at[slot])
        for slot in range(3)
    ]
    copies.append(pltpu.make_async_copy(x_ref, x_out, sems.at[3]))
    copies.append(pltpu.make_async_copy(mod_ref, mod_out, sems.at[4]))
    copies.append(pltpu.make_async_copy(stale_ref, stale_out, sems.at[5]))
    for copy in copies:
        copy.start()
    row = lax.broadcasted_iota(jnp.int32, ids_out.shape, 0)
    tile = jnp.zeros(ids_out.shape, jnp.int32)
    for step in range(STEPS):
        tile = jnp.where(row == step, ids[step], tile)
    ids_out[...] = tile
    rows, half = cos_ref.shape[0], DH // 2
    lane = lax.broadcasted_iota(jnp.int32, cos_ref.shape, 1)
    spot = slab[0] * rows + lax.broadcasted_iota(jnp.int32, cos_ref.shape, 0)
    power = jnp.where(lane < half, lane, lane - half).astype(F32) * (-2.0 / DH)
    angle = spot.astype(F32) * jnp.exp(power * math.log(10000.0))
    cos_ref[...] = jnp.cos(angle)
    sin = jnp.sin(angle)
    sin_ref[...] = jnp.where(lane < half, -sin, sin)
    for copy in copies:
        copy.wait()


def table_row(mod_ref, kind, ids_ref, step):
    chosen = ids_ref[step : step + 1, :1]
    table = mod_ref[kind]
    return sum(
        jnp.where(chosen == r, table[r : r + 1], 0.0) for r in range(table.shape[0])
    )


def normalized(step, x_refs, mod_refs, ids_ref):
    hidden = [ref[step].astype(F32) for ref in x_refs]
    width = sum(part.shape[1] for part in hidden)
    mean = sum(jnp.sum(part, axis=1, keepdims=True) for part in hidden) / width
    square = sum(jnp.sum(part * part, axis=1, keepdims=True) for part in hidden) / width
    inv = lax.rsqrt(square - mean * mean + 1e-06)
    parts = []
    for part, mod_ref in zip(hidden, mod_refs):
        shift = table_row(mod_ref, 0, ids_ref, step)
        scale = table_row(mod_ref, 1, ids_ref, step)
        parts.append(((part - mean) * inv * (1.0 + scale) + shift).astype(BF16))
    return parts


def projected(parts, w_ref, slot, head):
    feats = parts[0].shape[1]
    total = jnp.zeros((parts[0].shape[0], w_ref.shape[2]), F32)
    for number, part in enumerate(parts):
        start = pl.multiple_of((head[0] ^ number) * feats, feats)
        w = w_ref[slot, pl.ds(start, feats), :]
        total += jnp.dot(part, w, preferred_element_type=F32)
    return total


def rotated(values, cos, sin):
    blocks = []
    for start in range(0, values.shape[1], DH):
        u = values[:, start : start + DH]
        blocks.append(u * cos + pltpu.roll(u, DH // 2, 1) * sin)
    return jnp.concatenate(blocks, axis=1)


def qkv_kernel(n_head, head, ids_ref, *refs):
    x_refs, mod_refs = refs[:n_head], refs[n_head : 2 * n_head]
    w_ref, cos_ref, sin_ref, stale_ref, q_ref, kv_ref, kv1_ref = refs[2 * n_head :]
    rows = x_refs[0].shape[1]
    steps = [normalized(step, x_refs, mod_refs, ids_ref) for step in range(STEPS)]
    parts = [jnp.concatenate(pair, axis=0) for pair in zip(*steps)]
    cos = jnp.concatenate([cos_ref[...]] * STEPS, axis=0)
    sin = jnp.concatenate([sin_ref[...]] * STEPS, axis=0)
    queries = rotated(projected(parts, w_ref, 0, head), cos, sin).astype(BF16)
    keys = rotated(projected(parts, w_ref, 1, head), cos, sin).astype(BF16)
    values = projected(parts, w_ref, 2, head).astype(BF16)
    for step in range(STEPS):
        spot = slice(step * rows, (step + 1) * rows)
        q_ref[step] = queries[spot]
    kv_ref[:2] = stale_ref[...]
    kv_ref[2], kv_ref[3] = keys[:rows], values[:rows]
    kv1_ref[0], kv1_ref[1] = keys[rows:], values[rows:]


def split3(values):
    high = values.astype(BF16).astype(F32)
    middle = (values - high).astype(BF16).astype(F32)
    return [high, middle, values - high - middle]


def attend_kernel(q_ref, mate_ref, kv1_ref, *refs):
    kv_refs, out_ref = refs[:PLANE], refs[PLANE]
    blocks, _, rows, cols = kv_refs[0].shape
    old_rows = PLANE * blocks * rows
    shape = (2 * rows, old_rows + rows)
    mine = lax.broadcasted_iota(jnp.int32, shape, 0) < rows
    stray = jnp.where(mine, 0, PLANE * blocks)
    drop = lax.broadcasted_iota(jnp.int32, shape, 1) // rows == stray
    lane = lax.broadcasted_iota(jnp.int32, (2 * rows, DH), 1)
    for step in range(STEPS):
        fresh = (kv_refs[0].at[0, 2:], kv1_ref)[step]
        stats = jnp.zeros((2 * rows, DH), F32)
        mixed = []
        for head in range(cols // DH):
            lanes = slice(head * DH, (head + 1) * DH)

            def rows_of(kind):
                old = [ref[:, 2 * step + kind, :, lanes].reshape(blocks * rows, DH) for ref in kv_refs]
                return jnp.concatenate([*old, fresh[kind, :, lanes]], axis=0)

            queries = jnp.concatenate([q_ref[step, :, lanes], mate_ref[step, :, lanes]], axis=0)
            scores = lax.dot_general(queries, rows_of(0), NT, preferred_element_type=F32)
            scores = jnp.where(drop, -1e30, scores * (1.0 / math.sqrt(DH)))
            top = jnp.max(scores, axis=1, keepdims=True)
            weights = jnp.exp(scores - top)
            totals = jnp.sum(weights, axis=1, keepdims=True)
            mixed.append(
                jnp.dot(weights.astype(BF16), rows_of(1), preferred_element_type=F32) / totals
            )
            for place, piece in enumerate(split3(top) + split3(totals)):
                stats = jnp.where(lane == head * 8 + place, piece, stats)
        packed = jnp.concatenate([*mixed, stats], axis=1).astype(BF16)
        for mate in range(2):
            start = (mate * STEPS + step) * rows
            out_ref[start : start + rows, :] = packed[mate * rows : (mate + 1) * rows]


def merge_kernel(part_ref, other_ref, o_ref):
    rows = part_ref.shape[0] // 2
    cols = o_ref.shape[1]
    source = lax.broadcasted_iota(jnp.int32, (DH, DH), 0)
    parts = [
        part_ref[...],
        jnp.concatenate([other_ref[rows:], other_ref[:rows]], axis=0),
    ]
    for head in range(cols // DH):
        lanes = slice(head * DH, (head + 1) * DH)

        def spread(part, first):
            pick = (source >= head * 8 + first) & (source < head * 8 + first + 3)
            return jnp.dot(part[:, cols:], pick.astype(F32).astype(BF16), preferred_element_type=F32)

        tops = [spread(part, 0) for part in parts]
        best = functools.reduce(jnp.maximum, tops)
        scales = [spread(part, 3) * jnp.exp(t - best) for part, t in zip(parts, tops)]
        mixed = sum(s * part[:, lanes].astype(F32) for s, part in zip(scales, parts))
        o_ref[:, lanes] = (mixed / sum(scales)).astype(BF16)


def project_kernel(n_head, n_patch, bit, mate, patch, head, o_ref, *refs):
    w_refs, (out_ref, sums) = refs[:PLANE], refs[PLANE:]
    rows = out_ref.shape[0]
    slot = head[0] ^ bit ^ (patch[0] // (n_patch // n_head))
    for near in range(PLANE):
        sums[(patch[0] % PLANE) ^ near] = lax.dot_general(
            o_ref[mate * rows : (mate + 1) * rows, :],
            w_refs[near][slot],
            NT,
            preferred_element_type=F32,
        )
    out = jnp.concatenate([sums[c] for c in range(PLANE)], axis=1)
    out_ref[...] = out.astype(out_ref.dtype)


def gate_kernel(n_patch, patch, ids_ref, mod_ref, *refs):
    sum_refs, out_ref = refs[:-1], refs[-1]
    total = sum(ref[...].astype(F32) for ref in sum_refs)
    rows, width = total.shape
    each = rows // STEPS
    second = (patch[0] // PLANE) % 2 == 1
    for step in range(STEPS):
        gate = table_row(mod_ref, 2, ids_ref, step)
        gate = jnp.where(second, gate[:, width:], gate[:, :width])
        out_ref[step] = (gate * total[step * each : (step + 1) * each]).astype(BF16)


def in_hbm(values):
    return pltpu.with_memory_space_constraint(values, pltpu.HBM)


def call(kernel, shapes, ins, scratch=(), flops=0, size=0, limit=16):
    return pl.pallas_call(
        kernel,
        out_shape=shapes,
        in_specs=ins,
        out_specs=jax.tree.map(lambda _: VMEM, shapes),
        scratch_shapes=scratch,
        compiler_params=pltpu.CompilerParams(vmem_limit_bytes=limit * MIB),
        cost_estimate=pl.CostEstimate(flops=flops, bytes_accessed=size, transcendentals=0),
    )


def body(n_patch, n_head, inputs, stale_kv, w_qkv, w_out, mod_table, step_ids, slab_order):
    rows, feats = inputs.shape[1:]
    cols = w_qkv.shape[2]
    piece = w_out.shape[1]
    patch = lax.axis_index("patch").astype(jnp.int32)
    head = lax.axis_index("head").astype(jnp.int32)
    shaped = jax.ShapeDtypeStruct

    x_parts = [swap(inputs, "head", n_head, k) for k in range(1, n_head)]
    mod_parts = [swap(mod_table, "head", n_head, k) for k in range(1, n_head)]
    first = (jnp.transpose(w_qkv, (1, 0, 2)), inputs, jnp.transpose(mod_table, (1, 0, 2)), stale_kv)
    w, x_own, mod_own, stale, ids, cos, sin = call(
        load_kernel,
        tuple(pltpu.VMEM(v.shape, v.dtype) for v in first)
        + (shaped((8, DH), jnp.int32), shaped((rows, DH), F32), shaped((rows, DH), F32)),
        [SMEM] * 2 + [ANY] * len(first),
        [pltpu.SemaphoreType.DMA((6,))],
        size=2 * w_qkv.size,
    )(in_hbm(step_ids), slab_order, *map(in_hbm, first))
    x_parts = [x_own] + x_parts
    mod_parts = [mod_own] + [jnp.transpose(part, (1, 0, 2)) for part in mod_parts]

    def across(values, k):
        return swap(values, "patch", n_patch, k)

    def line_of(values):
        return [values] + [across(values, k) for k in range(2 * PLANE, n_patch, 2 * PLANE)]

    def plane_of(values):
        return [values] + [across(values, k) for k in range(1, PLANE)]


    kv_shape = shaped((2, rows, cols), BF16)
    q, kv, kv1 = call(
        functools.partial(qkv_kernel, n_head),
        (kv_shape, shaped((4, rows, cols), BF16), kv_shape),
        [SMEM] + [VMEM] * (2 * n_head + 5),
        flops=2 * STEPS * rows * w_qkv.size,
        size=2 * w_qkv.size,
    )(head[None], ids, *x_parts, *mod_parts, w, cos, sin, stale)

    w_own, kv = lax.optimization_barrier((w_out.T, kv))
    kv_pair = line_of(kv)
    q_mate = across(q, PLANE)
    w_x = across(w_own, 1)
    w_late, q_mate = lax.optimization_barrier((w_own, q_mate))
    w_rest = jnp.stack(line_of(w_late)[1:])
    kv_plane = plane_of(jnp.stack(kv_pair))
    w_rest, q_mate = lax.optimization_barrier((w_rest, q_mate))
    w_y = across(jnp.stack([w_own, w_x]), 2)
    rest_y = across(w_rest, 2)
    tall = 2 * STEPS * rows
    part = call(
        attend_kernel,
        shaped((tall, cols + DH), BF16),
        [VMEM] * (3 + PLANE),
        flops=4 * STEPS * rows * n_patch * rows * cols,
    )(q, q_mate, kv1, *kv_plane)
    rest_y, part = lax.optimization_barrier((rest_y, part))
    rest_x = across(jnp.stack([w_rest, rest_y]), 1)
    o = call(merge_kernel, shaped((tall, cols), BF16), [VMEM] * 2)(part, across(part, PLANE))
    o, w_y, rest_x = lax.optimization_barrier((o, w_y, rest_x))
    near = [(w_own, w_rest), (w_x, rest_x[0]), (w_y[0], rest_y), (w_y[1], rest_x[1])]
    w_plane = [jnp.concatenate([first[None], others]) for first, others in near]
    wide = PLANE * piece

    half = tall // 2

    def project(mate, bit, dtype):
        return call(
            functools.partial(project_kernel, n_head, n_patch, bit, mate),
            shaped((half, wide), dtype),
            [SMEM] * 2 + [VMEM] * (1 + PLANE),
            [pltpu.VMEM((PLANE, half, piece), F32)],
            2 * half * wide * cols,
            2 * wide * cols,
        )(patch[None], head[None], o, *w_plane)

    def gated(mate):
        sent = [swap(project(mate, k, BF16), "head", n_head, k) for k in range(1, n_head)]
        return call(
            functools.partial(gate_kernel, n_patch),
            shaped((STEPS, rows, wide), BF16),
            [SMEM] + [VMEM] * (2 + n_head),
        )(patch[None], ids, mod_own, project(mate, 0, F32), *sent)

    out_back = across(gated(1), PLANE)
    out_own = gated(0)
    second = (patch // PLANE) % 2 == 1
    return jnp.concatenate(
        [jnp.where(second, out_back, out_own), jnp.where(second, out_own, out_back)], axis=2
    )


def solution(mesh):
    in_specs = (
        P(None, "patch", "head"),
        P(None, "patch", "head"),
        P(None, None, "head"),
        P("head", "patch"),
        P(None, None, "head"),
        P(),
        P("patch"),
    )
    run = functools.partial(body, mesh.shape["patch"], mesh.shape["head"])
    return jax.shard_map(
        run, mesh=mesh, in_specs=in_specs, out_specs=P(None, "patch", "head"), check_vma=False
    )
```

```python
import functools
import math

import jax
import jax.numpy as jnp
from jax import lax
from jax.experimental import pallas as pl
from jax.experimental.pallas import tpu as pltpu
from jax.sharding import PartitionSpec as P

DH = 128
STEPS = 2
PLANE = 4
MIB = 1024 * 1024
VMEM = pl.BlockSpec(memory_space=pltpu.VMEM)
SMEM = pl.BlockSpec(memory_space=pltpu.SMEM)
ANY = pl.BlockSpec(memory_space=pl.ANY)
BF16, F32 = jnp.bfloat16, jnp.float32
NT = (((1,), (1,)), ((), ()))


def swap(values, axis, count, bit):
    return lax.ppermute(values, axis, [(i, i ^ bit) for i in range(count)])


def load_kernel(ids, slab, w_ref, x_ref, mod_ref, stale_ref, w_out, x_out, mod_out, stale_out, *refs):
    ids_out, cos_ref, sin_ref, sems = refs
    copies = [
        pltpu.make_async_copy(w_ref.at[slot], w_out.at[slot], sems.at[slot])
        for slot in range(3)
    ]
    copies.append(pltpu.make_async_copy(x_ref, x_out, sems.at[3]))
    copies.append(pltpu.make_async_copy(mod_ref, mod_out, sems.at[4]))
    copies.append(pltpu.make_async_copy(stale_ref, stale_out, sems.at[5]))
    for copy in copies:
        copy.start()
    row = lax.broadcasted_iota(jnp.int32, ids_out.shape, 0)
    tile = jnp.zeros(ids_out.shape, jnp.int32)
    for step in range(STEPS):
        tile = jnp.where(row == step, ids[step], tile)
    ids_out[...] = tile
    rows, half = cos_ref.shape[0], DH // 2
    lane = lax.broadcasted_iota(jnp.int32, cos_ref.shape, 1)
    spot = slab[0] * rows + lax.broadcasted_iota(jnp.int32, cos_ref.shape, 0)
    power = jnp.where(lane < half, lane, lane - half).astype(F32) * (-2.0 / DH)
    angle = spot.astype(F32) * jnp.exp(power * math.log(10000.0))
    cos_ref[...] = jnp.cos(angle)
    sin = jnp.sin(angle)
    sin_ref[...] = jnp.where(lane < half, -sin, sin)
    for copy in copies:
        copy.wait()


def table_row(mod_ref, kind, ids_ref, step):
    chosen = ids_ref[step : step + 1, :1]
    table = mod_ref[kind]
    return sum(
        jnp.where(chosen == r, table[r : r + 1], 0.0) for r in range(table.shape[0])
    )


def normalized(step, x_refs, mod_refs, ids_ref):
    hidden = [ref[step].astype(F32) for ref in x_refs]
    width = sum(part.shape[1] for part in hidden)
    mean = sum(jnp.sum(part, axis=1, keepdims=True) for part in hidden) / width
    square = sum(jnp.sum(part * part, axis=1, keepdims=True) for part in hidden) / width
    inv = lax.rsqrt(square - mean * mean + 1e-06)
    parts = []
    for part, mod_ref in zip(hidden, mod_refs):
        shift = table_row(mod_ref, 0, ids_ref, step)
        scale = table_row(mod_ref, 1, ids_ref, step)
        parts.append(((part - mean) * inv * (1.0 + scale) + shift).astype(BF16))
    return parts


def projected(parts, w_ref, slot, head):
    feats = parts[0].shape[1]
    total = jnp.zeros((parts[0].shape[0], w_ref.shape[2]), F32)
    for number, part in enumerate(parts):
        start = pl.multiple_of((head[0] ^ number) * feats, feats)
        w = w_ref[slot, pl.ds(start, feats), :]
        total += jnp.dot(part, w, preferred_element_type=F32)
    return total


def rotated(values, cos, sin):
    blocks = []
    for start in range(0, values.shape[1], DH):
        u = values[:, start : start + DH]
        blocks.append(u * cos + pltpu.roll(u, DH // 2, 1) * sin)
    return jnp.concatenate(blocks, axis=1)


def qkv_kernel(n_head, head, ids_ref, *refs):
    x_refs, mod_refs = refs[:n_head], refs[n_head : 2 * n_head]
    w_ref, cos_ref, sin_ref, stale_ref, q_ref, kv_ref, kv1_ref = refs[2 * n_head :]
    rows = x_refs[0].shape[1]
    steps = [normalized(step, x_refs, mod_refs, ids_ref) for step in range(STEPS)]
    parts = [jnp.concatenate(pair, axis=0) for pair in zip(*steps)]
    cos = jnp.concatenate([cos_ref[...]] * STEPS, axis=0)
    sin = jnp.concatenate([sin_ref[...]] * STEPS, axis=0)
    queries = rotated(projected(parts, w_ref, 0, head), cos, sin).astype(BF16)
    keys = rotated(projected(parts, w_ref, 1, head), cos, sin).astype(BF16)
    values = projected(parts, w_ref, 2, head).astype(BF16)
    for step in range(STEPS):
        spot = slice(step * rows, (step + 1) * rows)
        q_ref[step] = queries[spot]
    kv_ref[:2] = stale_ref[...]
    kv_ref[2], kv_ref[3] = keys[:rows], values[:rows]
    kv1_ref[0], kv1_ref[1] = keys[rows:], values[rows:]


def split3(values):
    high = values.astype(BF16).astype(F32)
    middle = (values - high).astype(BF16).astype(F32)
    return [high, middle, values - high - middle]


def attend_kernel(q_ref, mate_ref, kv1_ref, *refs):
    kv_refs, out_ref = refs[:PLANE], refs[PLANE]
    blocks, _, rows, cols = kv_refs[0].shape
    old_rows = PLANE * blocks * rows
    shape = (2 * rows, old_rows + rows)
    mine = lax.broadcasted_iota(jnp.int32, shape, 0) < rows
    stray = jnp.where(mine, 0, PLANE * blocks)
    drop = lax.broadcasted_iota(jnp.int32, shape, 1) // rows == stray
    lane = lax.broadcasted_iota(jnp.int32, (2 * rows, DH), 1)
    for step in range(STEPS):
        fresh = (kv_refs[0].at[0, 2:], kv1_ref)[step]
        stats = jnp.zeros((2 * rows, DH), F32)
        mixed = []
        for head in range(cols // DH):
            lanes = slice(head * DH, (head + 1) * DH)

            def rows_of(kind):
                old = [ref[:, 2 * step + kind, :, lanes].reshape(blocks * rows, DH) for ref in kv_refs]
                return jnp.concatenate([*old, fresh[kind, :, lanes]], axis=0)

            queries = jnp.concatenate([q_ref[step, :, lanes], mate_ref[step, :, lanes]], axis=0)
            scores = lax.dot_general(queries, rows_of(0), NT, preferred_element_type=F32)
            scores = jnp.where(drop, -1e30, scores * (1.0 / math.sqrt(DH)))
            top = jnp.max(scores, axis=1, keepdims=True)
            weights = jnp.exp(scores - top)
            totals = jnp.sum(weights, axis=1, keepdims=True)
            mixed.append(
                jnp.dot(weights.astype(BF16), rows_of(1), preferred_element_type=F32) / totals
            )
            for place, piece in enumerate(split3(top) + split3(totals)):
                stats = jnp.where(lane == head * 8 + place, piece, stats)
        packed = jnp.concatenate([*mixed, stats], axis=1).astype(BF16)
        for mate in range(2):
            start = (mate * STEPS + step) * rows
            out_ref[start : start + rows, :] = packed[mate * rows : (mate + 1) * rows]


def merge_kernel(part_ref, other_ref, o_ref):
    rows = part_ref.shape[0] // 2
    cols = o_ref.shape[1]
    source = lax.broadcasted_iota(jnp.int32, (DH, DH), 0)
    parts = [
        part_ref[...],
        jnp.concatenate([other_ref[rows:], other_ref[:rows]], axis=0),
    ]
    for head in range(cols // DH):
        lanes = slice(head * DH, (head + 1) * DH)

        def spread(part, first):
            pick = (source >= head * 8 + first) & (source < head * 8 + first + 3)
            return jnp.dot(part[:, cols:], pick.astype(F32).astype(BF16), preferred_element_type=F32)

        tops = [spread(part, 0) for part in parts]
        best = functools.reduce(jnp.maximum, tops)
        scales = [spread(part, 3) * jnp.exp(t - best) for part, t in zip(parts, tops)]
        mixed = sum(s * part[:, lanes].astype(F32) for s, part in zip(scales, parts))
        o_ref[:, lanes] = (mixed / sum(scales)).astype(BF16)


def project_kernel(n_head, n_patch, bit, mate, patch, head, o_ref, *refs):
    w_refs, (out_ref, sums) = refs[:PLANE], refs[PLANE:]
    rows = out_ref.shape[0]
    slot = head[0] ^ bit ^ (patch[0] // (n_patch // n_head))
    for near in range(PLANE):
        sums[(patch[0] % PLANE) ^ near] = lax.dot_general(
            o_ref[mate * rows : (mate + 1) * rows, :],
            w_refs[near][slot],
            NT,
            preferred_element_type=F32,
        )
    out = jnp.concatenate([sums[c] for c in range(PLANE)], axis=1)
    out_ref[...] = out.astype(out_ref.dtype)


def gate_kernel(n_patch, patch, ids_ref, mod_ref, *refs):
    sum_refs, out_ref = refs[:-1], refs[-1]
    total = sum(ref[...].astype(F32) for ref in sum_refs)
    rows, width = total.shape
    each = rows // STEPS
    second = (patch[0] // PLANE) % 2 == 1
    for step in range(STEPS):
        gate = table_row(mod_ref, 2, ids_ref, step)
        gate = jnp.where(second, gate[:, width:], gate[:, :width])
        out_ref[step] = (gate * total[step * each : (step + 1) * each]).astype(BF16)


def in_hbm(values):
    return pltpu.with_memory_space_constraint(values, pltpu.HBM)


def call(kernel, shapes, ins, scratch=(), flops=0, size=0, limit=16):
    return pl.pallas_call(
        kernel,
        out_shape=shapes,
        in_specs=ins,
        out_specs=jax.tree.map(lambda _: VMEM, shapes),
        scratch_shapes=scratch,
        compiler_params=pltpu.CompilerParams(vmem_limit_bytes=limit * MIB),
        cost_estimate=pl.CostEstimate(flops=flops, bytes_accessed=size, transcendentals=0),
    )


def body(n_patch, n_head, inputs, stale_kv, w_qkv, w_out, mod_table, step_ids, slab_order):
    rows, feats = inputs.shape[1:]
    cols = w_qkv.shape[2]
    piece = w_out.shape[1]
    patch = lax.axis_index("patch").astype(jnp.int32)
    head = lax.axis_index("head").astype(jnp.int32)
    shaped = jax.ShapeDtypeStruct

    x_parts = [swap(inputs, "head", n_head, k) for k in range(1, n_head)]
    mod_parts = [swap(mod_table, "head", n_head, k) for k in range(1, n_head)]
    first = (jnp.transpose(w_qkv, (1, 0, 2)), inputs, jnp.transpose(mod_table, (1, 0, 2)), stale_kv)
    w, x_own, mod_own, stale, ids, cos, sin = call(
        load_kernel,
        tuple(pltpu.VMEM(v.shape, v.dtype) for v in first)
        + (shaped((8, DH), jnp.int32), shaped((rows, DH), F32), shaped((rows, DH), F32)),
        [SMEM] * 2 + [ANY] * len(first),
        [pltpu.SemaphoreType.DMA((6,))],
        size=2 * w_qkv.size,
    )(in_hbm(step_ids), slab_order, *map(in_hbm, first))
    x_parts = [x_own] + x_parts
    mod_parts = [mod_own] + [jnp.transpose(part, (1, 0, 2)) for part in mod_parts]

    def across(values, k):
        return swap(values, "patch", n_patch, k)

    def line_of(values):
        return [values] + [across(values, k) for k in range(2 * PLANE, n_patch, 2 * PLANE)]

    def plane_of(values):
        return [values] + [across(values, k) for k in range(1, PLANE)]


    kv_shape = shaped((2, rows, cols), BF16)
    q, kv, kv1 = call(
        functools.partial(qkv_kernel, n_head),
        (kv_shape, shaped((4, rows, cols), BF16), kv_shape),
        [SMEM] + [VMEM] * (2 * n_head + 5),
        flops=2 * STEPS * rows * w_qkv.size,
        size=2 * w_qkv.size,
    )(head[None], ids, *x_parts, *mod_parts, w, cos, sin, stale)

    w_own, kv = lax.optimization_barrier((w_out.T, kv))
    kv_pair = line_of(kv)
    q_mate = across(q, PLANE)
    w_x = across(w_own, 1)
    w_late, q_mate = lax.optimization_barrier((w_own, q_mate))
    w_rest = jnp.stack(line_of(w_late)[1:])
    kv_plane = plane_of(jnp.stack(kv_pair))
    w_rest, q_mate = lax.optimization_barrier((w_rest, q_mate))
    w_y = across(jnp.stack([w_own, w_x]), 2)
    rest_plane = plane_of(w_rest)
    rest_plane[1], rest_plane[2], kv_plane[3] = lax.optimization_barrier(
        (rest_plane[1], rest_plane[2], kv_plane[3])
    )
    tall = 2 * STEPS * rows
    part = call(
        attend_kernel,
        shaped((tall, cols + DH), BF16),
        [VMEM] * (3 + PLANE),
        flops=4 * STEPS * rows * n_patch * rows * cols,
    )(q, q_mate, kv1, *kv_plane)
    o = call(merge_kernel, shaped((tall, cols), BF16), [VMEM] * 2)(part, across(part, PLANE))
    o, w_y, rest_plane = lax.optimization_barrier((o, w_y, rest_plane))
    near = zip((w_own, w_x, w_y[0], w_y[1]), rest_plane)
    w_plane = [jnp.concatenate([first[None], others]) for first, others in near]
    wide = PLANE * piece

    half = tall // 2

    def project(mate, bit, dtype):
        return call(
            functools.partial(project_kernel, n_head, n_patch, bit, mate),
            shaped((half, wide), dtype),
            [SMEM] * 2 + [VMEM] * (1 + PLANE),
            [pltpu.VMEM((PLANE, half, piece), F32)],
            2 * half * wide * cols,
            2 * wide * cols,
        )(patch[None], head[None], o, *w_plane)

    def gated(mate):
        sent = [swap(project(mate, k, BF16), "head", n_head, k) for k in range(1, n_head)]
        return call(
            functools.partial(gate_kernel, n_patch),
            shaped((STEPS, rows, wide), BF16),
            [SMEM] + [VMEM] * (2 + n_head),
        )(patch[None], ids, mod_own, project(mate, 0, F32), *sent)

    out_back = across(gated(1), PLANE)
    out_own = gated(0)
    second = (patch // PLANE) % 2 == 1
    return jnp.concatenate(
        [jnp.where(second, out_back, out_own), jnp.where(second, out_own, out_back)], axis=2
    )


def solution(mesh):
    in_specs = (
        P(None, "patch", "head"),
        P(None, "patch", "head"),
        P(None, None, "head"),
        P("head", "patch"),
        P(None, None, "head"),
        P(),
        P("patch"),
    )
    run = functools.partial(body, mesh.shape["patch"], mesh.shape["head"])
    return jax.shard_map(
        run, mesh=mesh, in_specs=in_specs, out_specs=P(None, "patch", "head"), check_vma=False
    )
```

```python
import functools
import math

import jax
import jax.numpy as jnp
from jax import lax
from jax.experimental import pallas as pl
from jax.experimental.pallas import tpu as pltpu
from jax.sharding import PartitionSpec as P

DH = 128
STEPS = 2
PLANE = 4
MIB = 1024 * 1024
VMEM = pl.BlockSpec(memory_space=pltpu.VMEM)
SMEM = pl.BlockSpec(memory_space=pltpu.SMEM)
ANY = pl.BlockSpec(memory_space=pl.ANY)
BF16, F32 = jnp.bfloat16, jnp.float32
NT = (((1,), (1,)), ((), ()))


def swap(values, axis, count, bit):
    return lax.ppermute(values, axis, [(i, i ^ bit) for i in range(count)])


def load_kernel(ids, slab, w_ref, x_ref, mod_ref, stale_ref, w_out, x_out, mod_out, stale_out, *refs):
    ids_out, cos_ref, sin_ref, sems = refs
    copies = [
        pltpu.make_async_copy(w_ref.at[slot], w_out.at[slot], sems.at[slot])
        for slot in range(3)
    ]
    copies.append(pltpu.make_async_copy(x_ref, x_out, sems.at[3]))
    copies.append(pltpu.make_async_copy(mod_ref, mod_out, sems.at[4]))
    copies.append(pltpu.make_async_copy(stale_ref, stale_out, sems.at[5]))
    for copy in copies:
        copy.start()
    row = lax.broadcasted_iota(jnp.int32, ids_out.shape, 0)
    tile = jnp.zeros(ids_out.shape, jnp.int32)
    for step in range(STEPS):
        tile = jnp.where(row == step, ids[step], tile)
    ids_out[...] = tile
    rows, half = cos_ref.shape[0], DH // 2
    lane = lax.broadcasted_iota(jnp.int32, cos_ref.shape, 1)
    spot = slab[0] * rows + lax.broadcasted_iota(jnp.int32, cos_ref.shape, 0)
    power = jnp.where(lane < half, lane, lane - half).astype(F32) * (-2.0 / DH)
    angle = spot.astype(F32) * jnp.exp(power * math.log(10000.0))
    cos_ref[...] = jnp.cos(angle)
    sin = jnp.sin(angle)
    sin_ref[...] = jnp.where(lane < half, -sin, sin)
    for copy in copies:
        copy.wait()


def table_row(mod_ref, kind, ids_ref, step):
    chosen = ids_ref[step : step + 1, :1]
    table = mod_ref[kind]
    return sum(
        jnp.where(chosen == r, table[r : r + 1], 0.0) for r in range(table.shape[0])
    )


def normalized(step, x_refs, mod_refs, ids_ref):
    hidden = [ref[step].astype(F32) for ref in x_refs]
    width = sum(part.shape[1] for part in hidden)
    mean = sum(jnp.sum(part, axis=1, keepdims=True) for part in hidden) / width
    square = sum(jnp.sum(part * part, axis=1, keepdims=True) for part in hidden) / width
    inv = lax.rsqrt(square - mean * mean + 1e-06)
    parts = []
    for part, mod_ref in zip(hidden, mod_refs):
        shift = table_row(mod_ref, 0, ids_ref, step)
        scale = table_row(mod_ref, 1, ids_ref, step)
        parts.append(((part - mean) * inv * (1.0 + scale) + shift).astype(BF16))
    return parts


def projected(parts, w_ref, slot, head):
    feats = parts[0].shape[1]
    total = jnp.zeros((parts[0].shape[0], w_ref.shape[2]), F32)
    for number, part in enumerate(parts):
        start = pl.multiple_of((head[0] ^ number) * feats, feats)
        w = w_ref[slot, pl.ds(start, feats), :]
        total += jnp.dot(part, w, preferred_element_type=F32)
    return total


def rotated(values, cos, sin):
    blocks = []
    for start in range(0, values.shape[1], DH):
        u = values[:, start : start + DH]
        blocks.append(u * cos + pltpu.roll(u, DH // 2, 1) * sin)
    return jnp.concatenate(blocks, axis=1)


def fresh_kernel(n_head, head, ids_ref, *refs):
    x_refs, mod_refs = refs[:n_head], refs[n_head : 2 * n_head]
    w_ref, cos_ref, sin_ref, stale_ref, a_ref, kv_ref = refs[2 * n_head :]
    parts = normalized(0, x_refs, mod_refs, ids_ref)
    for number, part in enumerate(parts):
        a_ref[number] = part
    keys = rotated(projected(parts, w_ref, 1, head), cos_ref[...], sin_ref[...])
    kv_ref[:2] = stale_ref[...]
    kv_ref[2] = keys.astype(BF16)
    kv_ref[3] = projected(parts, w_ref, 2, head).astype(BF16)


def rest_kernel(n_head, head, ids_ref, *refs):
    x_refs, mod_refs = refs[:n_head], refs[n_head : 2 * n_head]
    w_ref, cos_ref, sin_ref, a_ref, q_ref, kv1_ref = refs[2 * n_head :]
    rows = a_ref.shape[1]
    parts = normalized(1, x_refs, mod_refs, ids_ref)
    cos, sin = cos_ref[...], sin_ref[...]
    both = [jnp.concatenate([a_ref[k], part], axis=0) for k, part in enumerate(parts)]
    queries = projected(both, w_ref, 0, head)
    for step in range(STEPS):
        spot = slice(step * rows, (step + 1) * rows)
        q_ref[step] = rotated(queries[spot], cos, sin).astype(BF16)
    kv1_ref[0] = rotated(projected(parts, w_ref, 1, head), cos, sin).astype(BF16)
    kv1_ref[1] = projected(parts, w_ref, 2, head).astype(BF16)


def split3(values):
    high = values.astype(BF16).astype(F32)
    middle = (values - high).astype(BF16).astype(F32)
    return [high, middle, values - high - middle]


def attend_kernel(q_ref, mate_ref, kv1_ref, *refs):
    kv_refs, out_ref = refs[:PLANE], refs[PLANE]
    blocks, _, rows, cols = kv_refs[0].shape
    old_rows = PLANE * blocks * rows
    shape = (2 * rows, old_rows + rows)
    mine = lax.broadcasted_iota(jnp.int32, shape, 0) < rows
    stray = jnp.where(mine, 0, PLANE * blocks)
    drop = lax.broadcasted_iota(jnp.int32, shape, 1) // rows == stray
    lane = lax.broadcasted_iota(jnp.int32, (2 * rows, DH), 1)
    for step in range(STEPS):
        fresh = (kv_refs[0].at[0, 2:], kv1_ref)[step]
        stats = jnp.zeros((2 * rows, DH), F32)
        mixed = []
        for head in range(cols // DH):
            lanes = slice(head * DH, (head + 1) * DH)

            def rows_of(kind):
                old = [ref[:, 2 * step + kind, :, lanes].reshape(blocks * rows, DH) for ref in kv_refs]
                return jnp.concatenate([*old, fresh[kind, :, lanes]], axis=0)

            queries = jnp.concatenate([q_ref[step, :, lanes], mate_ref[step, :, lanes]], axis=0)
            scores = lax.dot_general(queries, rows_of(0), NT, preferred_element_type=F32)
            scores = jnp.where(drop, -1e30, scores * (1.0 / math.sqrt(DH)))
            top = jnp.max(scores, axis=1, keepdims=True)
            weights = jnp.exp(scores - top)
            totals = jnp.sum(weights, axis=1, keepdims=True)
            mixed.append(
                jnp.dot(weights.astype(BF16), rows_of(1), preferred_element_type=F32) / totals
            )
            for place, piece in enumerate(split3(top) + split3(totals)):
                stats = jnp.where(lane == head * 8 + place, piece, stats)
        packed = jnp.concatenate([*mixed, stats], axis=1).astype(BF16)
        for mate in range(2):
            start = (mate * STEPS + step) * rows
            out_ref[start : start + rows, :] = packed[mate * rows : (mate + 1) * rows]


def merge_kernel(part_ref, other_ref, o_ref):
    rows = part_ref.shape[0] // 2
    cols = o_ref.shape[1]
    source = lax.broadcasted_iota(jnp.int32, (DH, DH), 0)
    parts = [
        part_ref[...],
        jnp.concatenate([other_ref[rows:], other_ref[:rows]], axis=0),
    ]
    for head in range(cols // DH):
        lanes = slice(head * DH, (head + 1) * DH)

        def spread(part, first):
            pick = (source >= head * 8 + first) & (source < head * 8 + first + 3)
            return jnp.dot(part[:, cols:], pick.astype(F32).astype(BF16), preferred_element_type=F32)

        tops = [spread(part, 0) for part in parts]
        best = functools.reduce(jnp.maximum, tops)
        scales = [spread(part, 3) * jnp.exp(t - best) for part, t in zip(parts, tops)]
        mixed = sum(s * part[:, lanes].astype(F32) for s, part in zip(scales, parts))
        o_ref[:, lanes] = (mixed / sum(scales)).astype(BF16)


def project_kernel(n_head, n_patch, bit, mate, patch, head, o_ref, *refs):
    w_refs, (out_ref, sums) = refs[:PLANE], refs[PLANE:]
    rows = out_ref.shape[0]
    slot = head[0] ^ bit ^ (patch[0] // (n_patch // n_head))
    for near in range(PLANE):
        sums[(patch[0] % PLANE) ^ near] = lax.dot_general(
            o_ref[mate * rows : (mate + 1) * rows, :],
            w_refs[near][slot],
            NT,
            preferred_element_type=F32,
        )
    out = jnp.concatenate([sums[c] for c in range(PLANE)], axis=1)
    out_ref[...] = out.astype(out_ref.dtype)


def gate_kernel(n_patch, patch, ids_ref, mod_ref, *refs):
    sum_refs, out_ref = refs[:-1], refs[-1]
    total = sum(ref[...].astype(F32) for ref in sum_refs)
    rows, width = total.shape
    each = rows // STEPS
    second = (patch[0] // PLANE) % 2 == 1
    for step in range(STEPS):
        gate = table_row(mod_ref, 2, ids_ref, step)
        gate = jnp.where(second, gate[:, width:], gate[:, :width])
        out_ref[step] = (gate * total[step * each : (step + 1) * each]).astype(BF16)


def in_hbm(values):
    return pltpu.with_memory_space_constraint(values, pltpu.HBM)


def call(kernel, shapes, ins, scratch=(), flops=0, size=0, limit=16):
    return pl.pallas_call(
        kernel,
        out_shape=shapes,
        in_specs=ins,
        out_specs=jax.tree.map(lambda _: VMEM, shapes),
        scratch_shapes=scratch,
        compiler_params=pltpu.CompilerParams(vmem_limit_bytes=limit * MIB),
        cost_estimate=pl.CostEstimate(flops=flops, bytes_accessed=size, transcendentals=0),
    )


def body(n_patch, n_head, inputs, stale_kv, w_qkv, w_out, mod_table, step_ids, slab_order):
    rows, feats = inputs.shape[1:]
    cols = w_qkv.shape[2]
    piece = w_out.shape[1]
    patch = lax.axis_index("patch").astype(jnp.int32)
    head = lax.axis_index("head").astype(jnp.int32)
    shaped = jax.ShapeDtypeStruct

    x_parts = [swap(inputs, "head", n_head, k) for k in range(1, n_head)]
    mod_parts = [swap(mod_table, "head", n_head, k) for k in range(1, n_head)]
    first = (jnp.transpose(w_qkv, (1, 0, 2)), inputs, jnp.transpose(mod_table, (1, 0, 2)), stale_kv)
    w, x_own, mod_own, stale, ids, cos, sin = call(
        load_kernel,
        tuple(pltpu.VMEM(v.shape, v.dtype) for v in first)
        + (shaped((8, DH), jnp.int32), shaped((rows, DH), F32), shaped((rows, DH), F32)),
        [SMEM] * 2 + [ANY] * len(first),
        [pltpu.SemaphoreType.DMA((6,))],
        size=2 * w_qkv.size,
    )(in_hbm(step_ids), slab_order, *map(in_hbm, first))
    x_parts = [x_own] + x_parts
    mod_parts = [mod_own] + [jnp.transpose(part, (1, 0, 2)) for part in mod_parts]

    def across(values, k):
        return swap(values, "patch", n_patch, k)

    def line_of(values):
        return [values] + [across(values, k) for k in range(2 * PLANE, n_patch, 2 * PLANE)]

    def plane_of(values):
        return [values] + [across(values, k) for k in range(1, PLANE)]


    kv_shape = shaped((2, rows, cols), BF16)
    common = (head[None], ids, *x_parts, *mod_parts, w, cos, sin)
    specs = [SMEM] + [VMEM] * (2 * n_head + 5)
    a, kv = call(
        functools.partial(fresh_kernel, n_head),
        (shaped((n_head, rows, feats), BF16), shaped((4, rows, cols), BF16)),
        specs,
        flops=4 * rows * w_qkv.size // 3,
        size=2 * w_qkv.size,
    )(*common, stale)
    q, kv1 = call(
        functools.partial(rest_kernel, n_head),
        (kv_shape, kv_shape),
        specs,
        flops=8 * rows * w_qkv.size // 3,
        size=2 * w_qkv.size,
    )(*common, a)

    w_own, kv1 = lax.optimization_barrier((w_out.T, kv1))
    kv_pair = line_of(kv)
    q_mate = across(q, PLANE)
    w_x = across(w_own, 1)
    w_rest = jnp.stack(line_of(w_own)[1:])
    kv_plane = plane_of(jnp.stack(kv_pair))
    w_rest, q_mate = lax.optimization_barrier((w_rest, q_mate))
    w_y = across(jnp.stack([w_own, w_x]), 2)
    rest_y = across(w_rest, 2)
    tall = 2 * STEPS * rows
    part = call(
        attend_kernel,
        shaped((tall, cols + DH), BF16),
        [VMEM] * (3 + PLANE),
        flops=4 * STEPS * rows * n_patch * rows * cols,
    )(q, q_mate, kv1, *kv_plane)
    rest_y, part = lax.optimization_barrier((rest_y, part))
    rest_x = across(jnp.stack([w_rest, rest_y]), 1)
    o = call(merge_kernel, shaped((tall, cols), BF16), [VMEM] * 2)(part, across(part, PLANE))
    o, w_y, rest_x = lax.optimization_barrier((o, w_y, rest_x))
    near = [(w_own, w_rest), (w_x, rest_x[0]), (w_y[0], rest_y), (w_y[1], rest_x[1])]
    w_plane = [jnp.concatenate([first[None], others]) for first, others in near]
    wide = PLANE * piece

    half = tall // 2

    def project(mate, bit, dtype):
        return call(
            functools.partial(project_kernel, n_head, n_patch, bit, mate),
            shaped((half, wide), dtype),
            [SMEM] * 2 + [VMEM] * (1 + PLANE),
            [pltpu.VMEM((PLANE, half, piece), F32)],
            2 * half * wide * cols,
            2 * wide * cols,
        )(patch[None], head[None], o, *w_plane)

    def gated(mate):
        sent = [swap(project(mate, k, BF16), "head", n_head, k) for k in range(1, n_head)]
        return call(
            functools.partial(gate_kernel, n_patch),
            shaped((STEPS, rows, wide), BF16),
            [SMEM] + [VMEM] * (2 + n_head),
        )(patch[None], ids, mod_own, project(mate, 0, F32), *sent)

    out_back = across(gated(1), PLANE)
    out_own = gated(0)
    second = (patch // PLANE) % 2 == 1
    return jnp.concatenate(
        [jnp.where(second, out_back, out_own), jnp.where(second, out_own, out_back)], axis=2
    )


def solution(mesh):
    in_specs = (
        P(None, "patch", "head"),
        P(None, "patch", "head"),
        P(None, None, "head"),
        P("head", "patch"),
        P(None, None, "head"),
        P(),
        P("patch"),
    )
    run = functools.partial(body, mesh.shape["patch"], mesh.shape["head"])
    return jax.shard_map(
        run, mesh=mesh, in_specs=in_specs, out_specs=P(None, "patch", "head"), check_vma=False
    )
```

```python
import functools
import math

import jax
import jax.numpy as jnp
from jax import lax
from jax.experimental import pallas as pl
from jax.experimental.pallas import tpu as pltpu
from jax.sharding import PartitionSpec as P

DH = 128
STEPS = 2
PLANE = 4
MIB = 1024 * 1024
VMEM = pl.BlockSpec(memory_space=pltpu.VMEM)
SMEM = pl.BlockSpec(memory_space=pltpu.SMEM)
ANY = pl.BlockSpec(memory_space=pl.ANY)
BF16, F32 = jnp.bfloat16, jnp.float32
NT = (((1,), (1,)), ((), ()))


def swap(values, axis, count, bit):
    return lax.ppermute(values, axis, [(i, i ^ bit) for i in range(count)])


def load_kernel(ids, slab, w_ref, x_ref, mod_ref, stale_ref, w_out, x_out, mod_out, stale_out, *refs):
    ids_out, cos_ref, sin_ref, sems = refs
    copies = [
        pltpu.make_async_copy(w_ref.at[slot], w_out.at[slot], sems.at[slot])
        for slot in range(3)
    ]
    copies.append(pltpu.make_async_copy(x_ref, x_out, sems.at[3]))
    copies.append(pltpu.make_async_copy(mod_ref, mod_out, sems.at[4]))
    copies.append(pltpu.make_async_copy(stale_ref, stale_out, sems.at[5]))
    for copy in copies:
        copy.start()
    row = lax.broadcasted_iota(jnp.int32, ids_out.shape, 0)
    tile = jnp.zeros(ids_out.shape, jnp.int32)
    for step in range(STEPS):
        tile = jnp.where(row == step, ids[step], tile)
    ids_out[...] = tile
    rows, half = cos_ref.shape[0], DH // 2
    lane = lax.broadcasted_iota(jnp.int32, cos_ref.shape, 1)
    spot = slab[0] * rows + lax.broadcasted_iota(jnp.int32, cos_ref.shape, 0)
    power = jnp.where(lane < half, lane, lane - half).astype(F32) * (-2.0 / DH)
    angle = spot.astype(F32) * jnp.exp(power * math.log(10000.0))
    cos_ref[...] = jnp.cos(angle)
    sin = jnp.sin(angle)
    sin_ref[...] = jnp.where(lane < half, -sin, sin)
    for copy in copies:
        copy.wait()


def table_row(mod_ref, kind, ids_ref, step):
    chosen = ids_ref[step : step + 1, :1]
    table = mod_ref[kind]
    return sum(
        jnp.where(chosen == r, table[r : r + 1], 0.0) for r in range(table.shape[0])
    )


def normalized(step, x_refs, mod_refs, ids_ref):
    hidden = [ref[step].astype(F32) for ref in x_refs]
    width = sum(part.shape[1] for part in hidden)
    mean = sum(jnp.sum(part, axis=1, keepdims=True) for part in hidden) / width
    square = sum(jnp.sum(part * part, axis=1, keepdims=True) for part in hidden) / width
    inv = lax.rsqrt(square - mean * mean + 1e-06)
    parts = []
    for part, mod_ref in zip(hidden, mod_refs):
        shift = table_row(mod_ref, 0, ids_ref, step)
        scale = table_row(mod_ref, 1, ids_ref, step)
        parts.append(((part - mean) * inv * (1.0 + scale) + shift).astype(BF16))
    return parts


def projected(parts, w_ref, slot, head):
    feats = parts[0].shape[1]
    total = jnp.zeros((parts[0].shape[0], w_ref.shape[2]), F32)
    for number, part in enumerate(parts):
        start = pl.multiple_of((head[0] ^ number) * feats, feats)
        w = w_ref[slot, pl.ds(start, feats), :]
        total += jnp.dot(part, w, preferred_element_type=F32)
    return total


def rotated(values, cos, sin):
    blocks = []
    for start in range(0, values.shape[1], DH):
        u = values[:, start : start + DH]
        blocks.append(u * cos + pltpu.roll(u, DH // 2, 1) * sin)
    return jnp.concatenate(blocks, axis=1)


def qkv_kernel(n_head, head, ids_ref, *refs):
    x_refs, mod_refs = refs[:n_head], refs[n_head : 2 * n_head]
    w_ref, cos_ref, sin_ref, stale_ref, q_ref, kv_ref, kv1_ref = refs[2 * n_head :]
    rows = x_refs[0].shape[1]
    steps = [normalized(step, x_refs, mod_refs, ids_ref) for step in range(STEPS)]
    parts = [jnp.concatenate(pair, axis=0) for pair in zip(*steps)]
    cos = jnp.concatenate([cos_ref[...]] * STEPS, axis=0)
    sin = jnp.concatenate([sin_ref[...]] * STEPS, axis=0)
    queries = rotated(projected(parts, w_ref, 0, head), cos, sin).astype(BF16)
    keys = rotated(projected(parts, w_ref, 1, head), cos, sin).astype(BF16)
    values = projected(parts, w_ref, 2, head).astype(BF16)
    for step in range(STEPS):
        spot = slice(step * rows, (step + 1) * rows)
        q_ref[step] = queries[spot]
    kv_ref[:2] = stale_ref[...]
    kv_ref[2], kv_ref[3] = keys[:rows], values[:rows]
    kv1_ref[0], kv1_ref[1] = keys[rows:], values[rows:]


def split3(values):
    high = values.astype(BF16).astype(F32)
    middle = (values - high).astype(BF16).astype(F32)
    return [high, middle, values - high - middle]


def attend_kernel(q_ref, mate_ref, kv1_ref, *refs):
    kv_refs, out_ref = refs[:PLANE], refs[PLANE]
    blocks, _, rows, cols = kv_refs[0].shape
    old_rows = PLANE * blocks * rows
    shape = (2 * rows, old_rows + rows)
    mine = lax.broadcasted_iota(jnp.int32, shape, 0) < rows
    stray = jnp.where(mine, 0, PLANE * blocks)
    drop = lax.broadcasted_iota(jnp.int32, shape, 1) // rows == stray
    lane = lax.broadcasted_iota(jnp.int32, (2 * rows, DH), 1)
    for step in range(STEPS):
        fresh = (kv_refs[0].at[0, 2:], kv1_ref)[step]
        stats = jnp.zeros((2 * rows, DH), F32)
        mixed = []
        for head in range(cols // DH):
            lanes = slice(head * DH, (head + 1) * DH)

            def rows_of(kind):
                old = [ref[:, 2 * step + kind, :, lanes].reshape(blocks * rows, DH) for ref in kv_refs]
                return jnp.concatenate([*old, fresh[kind, :, lanes]], axis=0)

            queries = jnp.concatenate([q_ref[step, :, lanes], mate_ref[step, :, lanes]], axis=0)
            scores = lax.dot_general(queries, rows_of(0), NT, preferred_element_type=F32)
            scores = jnp.where(drop, -1e30, scores * (1.0 / math.sqrt(DH)))
            top = jnp.max(scores, axis=1, keepdims=True)
            weights = jnp.exp(scores - top)
            totals = jnp.sum(weights, axis=1, keepdims=True)
            mixed.append(
                jnp.dot(weights.astype(BF16), rows_of(1), preferred_element_type=F32) / totals
            )
            for place, piece in enumerate(split3(top) + split3(totals)):
                stats = jnp.where(lane == head * 8 + place, piece, stats)
        packed = jnp.concatenate([*mixed, stats], axis=1).astype(BF16)
        for mate in range(2):
            start = (mate * STEPS + step) * rows
            out_ref[start : start + rows, :] = packed[mate * rows : (mate + 1) * rows]


def merge_kernel(part_ref, other_ref, o_ref):
    rows = part_ref.shape[0] // 2
    cols = o_ref.shape[1]
    source = lax.broadcasted_iota(jnp.int32, (DH, DH), 0)
    parts = [
        part_ref[...],
        jnp.concatenate([other_ref[rows:], other_ref[:rows]], axis=0),
    ]
    for head in range(cols // DH):
        lanes = slice(head * DH, (head + 1) * DH)

        def spread(part, first):
            pick = (source >= head * 8 + first) & (source < head * 8 + first + 3)
            return jnp.dot(part[:, cols:], pick.astype(F32).astype(BF16), preferred_element_type=F32)

        tops = [spread(part, 0) for part in parts]
        best = functools.reduce(jnp.maximum, tops)
        scales = [spread(part, 3) * jnp.exp(t - best) for part, t in zip(parts, tops)]
        mixed = sum(s * part[:, lanes].astype(F32) for s, part in zip(scales, parts))
        o_ref[:, lanes] = (mixed / sum(scales)).astype(BF16)


def project_kernel(n_head, n_patch, bit, mate, patch, head, o_ref, *refs):
    w_refs, (out_ref, sums) = refs[:PLANE], refs[PLANE:]
    rows = out_ref.shape[0]
    slot = head[0] ^ bit ^ (patch[0] // (n_patch // n_head))
    for near in range(PLANE):
        sums[(patch[0] % PLANE) ^ near] = lax.dot_general(
            o_ref[mate * rows : (mate + 1) * rows, :],
            w_refs[near][slot],
            NT,
            preferred_element_type=F32,
        )
    out = jnp.concatenate([sums[c] for c in range(PLANE)], axis=1)
    out_ref[...] = out.astype(out_ref.dtype)


def gate_kernel(n_patch, patch, ids_ref, mod_ref, *refs):
    sum_refs, out_ref = refs[:-1], refs[-1]
    total = sum(ref[...].astype(F32) for ref in sum_refs)
    rows, width = total.shape
    each = rows // STEPS
    second = (patch[0] // PLANE) % 2 == 1
    for step in range(STEPS):
        gate = table_row(mod_ref, 2, ids_ref, step)
        gate = jnp.where(second, gate[:, width:], gate[:, :width])
        out_ref[step] = (gate * total[step * each : (step + 1) * each]).astype(BF16)


def in_hbm(values):
    return pltpu.with_memory_space_constraint(values, pltpu.HBM)


def call(kernel, shapes, ins, scratch=(), flops=0, size=0, limit=16):
    return pl.pallas_call(
        kernel,
        out_shape=shapes,
        in_specs=ins,
        out_specs=jax.tree.map(lambda _: VMEM, shapes),
        scratch_shapes=scratch,
        compiler_params=pltpu.CompilerParams(vmem_limit_bytes=limit * MIB),
        cost_estimate=pl.CostEstimate(flops=flops, bytes_accessed=size, transcendentals=0),
    )


def body(n_patch, n_head, inputs, stale_kv, w_qkv, w_out, mod_table, step_ids, slab_order):
    rows, feats = inputs.shape[1:]
    cols = w_qkv.shape[2]
    piece = w_out.shape[1]
    patch = lax.axis_index("patch").astype(jnp.int32)
    head = lax.axis_index("head").astype(jnp.int32)
    shaped = jax.ShapeDtypeStruct

    x_parts = [swap(inputs, "head", n_head, k) for k in range(1, n_head)]
    mod_parts = [swap(mod_table, "head", n_head, k) for k in range(1, n_head)]
    first = (jnp.transpose(w_qkv, (1, 0, 2)), inputs, jnp.transpose(mod_table, (1, 0, 2)), stale_kv)
    w, x_own, mod_own, stale, ids, cos, sin = call(
        load_kernel,
        tuple(pltpu.VMEM(v.shape, v.dtype) for v in first)
        + (shaped((8, DH), jnp.int32), shaped((rows, DH), F32), shaped((rows, DH), F32)),
        [SMEM] * 2 + [ANY] * len(first),
        [pltpu.SemaphoreType.DMA((6,))],
        size=2 * w_qkv.size,
    )(in_hbm(step_ids), slab_order, *map(in_hbm, first))
    x_parts = [x_own] + x_parts
    mod_parts = [mod_own] + [jnp.transpose(part, (1, 0, 2)) for part in mod_parts]

    def across(values, k):
        return swap(values, "patch", n_patch, k)

    def line_of(values):
        return [values] + [across(values, k) for k in range(2 * PLANE, n_patch, 2 * PLANE)]

    def plane_of(values):
        return [values] + [across(values, k) for k in range(1, PLANE)]


    kv_shape = shaped((2, rows, cols), BF16)
    q, kv, kv1 = call(
        functools.partial(qkv_kernel, n_head),
        (kv_shape, shaped((4, rows, cols), BF16), kv_shape),
        [SMEM] + [VMEM] * (2 * n_head + 5),
        flops=2 * STEPS * rows * w_qkv.size,
        size=2 * w_qkv.size,
    )(head[None], ids, *x_parts, *mod_parts, w, cos, sin, stale)

    w_own, kv = lax.optimization_barrier((w_out.T, kv))
    kv_pair = line_of(kv)
    q_mate = across(q, PLANE)
    w_x = across(w_own, 1)
    w_late, kv_pair = lax.optimization_barrier((w_own, kv_pair))
    w_rest = jnp.stack(line_of(w_late)[1:])
    kv_plane = plane_of(jnp.stack(kv_pair))
    w_rest, q_mate = lax.optimization_barrier((w_rest, q_mate))
    w_y = across(jnp.stack([w_own, w_x]), 2)
    rest_y = across(w_rest, 2)
    tall = 2 * STEPS * rows
    part = call(
        attend_kernel,
        shaped((tall, cols + DH), BF16),
        [VMEM] * (3 + PLANE),
        flops=4 * STEPS * rows * n_patch * rows * cols,
    )(q, q_mate, kv1, *kv_plane)
    rest_y, part = lax.optimization_barrier((rest_y, part))
    rest_x = across(jnp.stack([w_rest, rest_y]), 1)
    o = call(merge_kernel, shaped((tall, cols), BF16), [VMEM] * 2)(part, across(part, PLANE))
    o, w_y, rest_x = lax.optimization_barrier((o, w_y, rest_x))
    near = [(w_own, w_rest), (w_x, rest_x[0]), (w_y[0], rest_y), (w_y[1], rest_x[1])]
    w_plane = [jnp.concatenate([first[None], others]) for first, others in near]
    wide = PLANE * piece

    half = tall // 2

    def project(mate, bit, dtype):
        return call(
            functools.partial(project_kernel, n_head, n_patch, bit, mate),
            shaped((half, wide), dtype),
            [SMEM] * 2 + [VMEM] * (1 + PLANE),
            [pltpu.VMEM((PLANE, half, piece), F32)],
            2 * half * wide * cols,
            2 * wide * cols,
        )(patch[None], head[None], o, *w_plane)

    def gated(mate):
        sent = [swap(project(mate, k, BF16), "head", n_head, k) for k in range(1, n_head)]
        return call(
            functools.partial(gate_kernel, n_patch),
            shaped((STEPS, rows, wide), BF16),
            [SMEM] + [VMEM] * (2 + n_head),
        )(patch[None], ids, mod_own, project(mate, 0, F32), *sent)

    out_back = across(gated(1), PLANE)
    out_own = gated(0)
    second = (patch // PLANE) % 2 == 1
    return jnp.concatenate(
        [jnp.where(second, out_back, out_own), jnp.where(second, out_own, out_back)], axis=2
    )


def solution(mesh):
    in_specs = (
        P(None, "patch", "head"),
        P(None, "patch", "head"),
        P(None, None, "head"),
        P("head", "patch"),
        P(None, None, "head"),
        P(),
        P("patch"),
    )
    run = functools.partial(body, mesh.shape["patch"], mesh.shape["head"])
    return jax.shard_map(
        run, mesh=mesh, in_specs=in_specs, out_specs=P(None, "patch", "head"), check_vma=False
    )
```

```python
import functools
import math

import jax
import jax.numpy as jnp
from jax import lax
from jax.experimental import pallas as pl
from jax.experimental.pallas import tpu as pltpu
from jax.sharding import PartitionSpec as P

DH = 128
STEPS = 2
PLANE = 4
MIB = 1024 * 1024
VMEM = pl.BlockSpec(memory_space=pltpu.VMEM)
SMEM = pl.BlockSpec(memory_space=pltpu.SMEM)
ANY = pl.BlockSpec(memory_space=pl.ANY)
BF16, F32 = jnp.bfloat16, jnp.float32
NT = (((1,), (1,)), ((), ()))


def swap(values, axis, count, bit):
    return lax.ppermute(values, axis, [(i, i ^ bit) for i in range(count)])


def load_kernel(ids, slab, w_ref, x_ref, mod_ref, stale_ref, w_out, x_out, mod_out, stale_out, *refs):
    ids_out, cos_ref, sin_ref, sems = refs
    copies = [
        pltpu.make_async_copy(w_ref.at[slot], w_out.at[slot], sems.at[slot])
        for slot in range(3)
    ]
    copies.append(pltpu.make_async_copy(x_ref, x_out, sems.at[3]))
    copies.append(pltpu.make_async_copy(mod_ref, mod_out, sems.at[4]))
    copies.append(pltpu.make_async_copy(stale_ref, stale_out, sems.at[5]))
    for copy in copies:
        copy.start()
    row = lax.broadcasted_iota(jnp.int32, ids_out.shape, 0)
    tile = jnp.zeros(ids_out.shape, jnp.int32)
    for step in range(STEPS):
        tile = jnp.where(row == step, ids[step], tile)
    ids_out[...] = tile
    rows, half = cos_ref.shape[0], DH // 2
    lane = lax.broadcasted_iota(jnp.int32, cos_ref.shape, 1)
    spot = slab[0] * rows + lax.broadcasted_iota(jnp.int32, cos_ref.shape, 0)
    power = jnp.where(lane < half, lane, lane - half).astype(F32) * (-2.0 / DH)
    angle = spot.astype(F32) * jnp.exp(power * math.log(10000.0))
    cos_ref[...] = jnp.cos(angle)
    sin = jnp.sin(angle)
    sin_ref[...] = jnp.where(lane < half, -sin, sin)
    for copy in copies:
        copy.wait()


def table_row(mod_ref, kind, ids_ref, step):
    chosen = ids_ref[step : step + 1, :1]
    table = mod_ref[kind]
    return sum(
        jnp.where(chosen == r, table[r : r + 1], 0.0) for r in range(table.shape[0])
    )


def normalized(step, x_refs, mod_refs, ids_ref):
    hidden = [ref[step].astype(F32) for ref in x_refs]
    width = sum(part.shape[1] for part in hidden)
    mean = sum(jnp.sum(part, axis=1, keepdims=True) for part in hidden) / width
    square = sum(jnp.sum(part * part, axis=1, keepdims=True) for part in hidden) / width
    inv = lax.rsqrt(square - mean * mean + 1e-06)
    parts = []
    for part, mod_ref in zip(hidden, mod_refs):
        shift = table_row(mod_ref, 0, ids_ref, step)
        scale = table_row(mod_ref, 1, ids_ref, step)
        parts.append(((part - mean) * inv * (1.0 + scale) + shift).astype(BF16))
    return parts


def projected(parts, w_ref, slot, head):
    feats = parts[0].shape[1]
    total = jnp.zeros((parts[0].shape[0], w_ref.shape[2]), F32)
    for number, part in enumerate(parts):
        start = pl.multiple_of((head[0] ^ number) * feats, feats)
        w = w_ref[slot, pl.ds(start, feats), :]
        total += jnp.dot(part, w, preferred_element_type=F32)
    return total


def rotated(values, cos, sin):
    blocks = []
    for start in range(0, values.shape[1], DH):
        u = values[:, start : start + DH]
        blocks.append(u * cos + pltpu.roll(u, DH // 2, 1) * sin)
    return jnp.concatenate(blocks, axis=1)


def fresh_kernel(n_head, head, ids_ref, *refs):
    x_refs, mod_refs = refs[:n_head], refs[n_head : 2 * n_head]
    w_ref, cos_ref, sin_ref, stale_ref, a_ref, kv_ref = refs[2 * n_head :]
    parts = normalized(0, x_refs, mod_refs, ids_ref)
    for number, part in enumerate(parts):
        a_ref[number] = part
    keys = rotated(projected(parts, w_ref, 1, head), cos_ref[...], sin_ref[...])
    kv_ref[:2] = stale_ref[...]
    kv_ref[2] = keys.astype(BF16)
    kv_ref[3] = projected(parts, w_ref, 2, head).astype(BF16)


def rest_kernel(n_head, head, ids_ref, *refs):
    x_refs, mod_refs = refs[:n_head], refs[n_head : 2 * n_head]
    w_ref, cos_ref, sin_ref, a_ref, q_ref, kv1_ref = refs[2 * n_head :]
    rows = a_ref.shape[1]
    parts = normalized(1, x_refs, mod_refs, ids_ref)
    cos, sin = cos_ref[...], sin_ref[...]
    both = [jnp.concatenate([a_ref[k], part], axis=0) for k, part in enumerate(parts)]
    queries = projected(both, w_ref, 0, head)
    for step in range(STEPS):
        spot = slice(step * rows, (step + 1) * rows)
        q_ref[step] = rotated(queries[spot], cos, sin).astype(BF16)
    kv1_ref[0] = rotated(projected(parts, w_ref, 1, head), cos, sin).astype(BF16)
    kv1_ref[1] = projected(parts, w_ref, 2, head).astype(BF16)


def split3(values):
    high = values.astype(BF16).astype(F32)
    middle = (values - high).astype(BF16).astype(F32)
    return [high, middle, values - high - middle]


def attend_kernel(q_ref, mate_ref, kv1_ref, *refs):
    kv_refs, out_ref = refs[:PLANE], refs[PLANE]
    blocks, _, rows, cols = kv_refs[0].shape
    old_rows = PLANE * blocks * rows
    shape = (2 * rows, old_rows + rows)
    mine = lax.broadcasted_iota(jnp.int32, shape, 0) < rows
    stray = jnp.where(mine, 0, PLANE * blocks)
    drop = lax.broadcasted_iota(jnp.int32, shape, 1) // rows == stray
    lane = lax.broadcasted_iota(jnp.int32, (2 * rows, DH), 1)
    for step in range(STEPS):
        fresh = (kv_refs[0].at[0, 2:], kv1_ref)[step]
        stats = jnp.zeros((2 * rows, DH), F32)
        mixed = []
        for head in range(cols // DH):
            lanes = slice(head * DH, (head + 1) * DH)

            def rows_of(kind):
                old = [ref[:, 2 * step + kind, :, lanes].reshape(blocks * rows, DH) for ref in kv_refs]
                return jnp.concatenate([*old, fresh[kind, :, lanes]], axis=0)

            queries = jnp.concatenate([q_ref[step, :, lanes], mate_ref[step, :, lanes]], axis=0)
            scores = lax.dot_general(queries, rows_of(0), NT, preferred_element_type=F32)
            scores = jnp.where(drop, -1e30, scores * (1.0 / math.sqrt(DH)))
            top = jnp.max(scores, axis=1, keepdims=True)
            weights = jnp.exp(scores - top)
            totals = jnp.sum(weights, axis=1, keepdims=True)
            mixed.append(
                jnp.dot(weights.astype(BF16), rows_of(1), preferred_element_type=F32) / totals
            )
            for place, piece in enumerate(split3(top) + split3(totals)):
                stats = jnp.where(lane == head * 8 + place, piece, stats)
        packed = jnp.concatenate([*mixed, stats], axis=1).astype(BF16)
        for mate in range(2):
            start = (mate * STEPS + step) * rows
            out_ref[start : start + rows, :] = packed[mate * rows : (mate + 1) * rows]


def merge_kernel(part_ref, other_ref, o_ref):
    rows = part_ref.shape[0] // 2
    cols = o_ref.shape[1]
    source = lax.broadcasted_iota(jnp.int32, (DH, DH), 0)
    parts = [
        part_ref[...],
        jnp.concatenate([other_ref[rows:], other_ref[:rows]], axis=0),
    ]
    for head in range(cols // DH):
        lanes = slice(head * DH, (head + 1) * DH)

        def spread(part, first):
            pick = (source >= head * 8 + first) & (source < head * 8 + first + 3)
            return jnp.dot(part[:, cols:], pick.astype(F32).astype(BF16), preferred_element_type=F32)

        tops = [spread(part, 0) for part in parts]
        best = functools.reduce(jnp.maximum, tops)
        scales = [spread(part, 3) * jnp.exp(t - best) for part, t in zip(parts, tops)]
        mixed = sum(s * part[:, lanes].astype(F32) for s, part in zip(scales, parts))
        o_ref[:, lanes] = (mixed / sum(scales)).astype(BF16)


def project_kernel(n_head, n_patch, bit, mate, patch, head, o_ref, *refs):
    w_refs, (out_ref, sums) = refs[:PLANE], refs[PLANE:]
    rows = out_ref.shape[0]
    slot = head[0] ^ bit ^ (patch[0] // (n_patch // n_head))
    for near in range(PLANE):
        sums[(patch[0] % PLANE) ^ near] = lax.dot_general(
            o_ref[mate * rows : (mate + 1) * rows, :],
            w_refs[near][slot],
            NT,
            preferred_element_type=F32,
        )
    out = jnp.concatenate([sums[c] for c in range(PLANE)], axis=1)
    out_ref[...] = out.astype(out_ref.dtype)


def gate_kernel(n_patch, patch, ids_ref, mod_ref, *refs):
    sum_refs, out_ref = refs[:-1], refs[-1]
    total = sum(ref[...].astype(F32) for ref in sum_refs)
    rows, width = total.shape
    each = rows // STEPS
    second = (patch[0] // PLANE) % 2 == 1
    for step in range(STEPS):
        gate = table_row(mod_ref, 2, ids_ref, step)
        gate = jnp.where(second, gate[:, width:], gate[:, :width])
        out_ref[step] = (gate * total[step * each : (step + 1) * each]).astype(BF16)


def in_hbm(values):
    return pltpu.with_memory_space_constraint(values, pltpu.HBM)


def call(kernel, shapes, ins, scratch=(), flops=0, size=0, limit=16):
    return pl.pallas_call(
        kernel,
        out_shape=shapes,
        in_specs=ins,
        out_specs=jax.tree.map(lambda _: VMEM, shapes),
        scratch_shapes=scratch,
        compiler_params=pltpu.CompilerParams(vmem_limit_bytes=limit * MIB),
        cost_estimate=pl.CostEstimate(flops=flops, bytes_accessed=size, transcendentals=0),
    )


def body(n_patch, n_head, inputs, stale_kv, w_qkv, w_out, mod_table, step_ids, slab_order):
    rows, feats = inputs.shape[1:]
    cols = w_qkv.shape[2]
    piece = w_out.shape[1]
    patch = lax.axis_index("patch").astype(jnp.int32)
    head = lax.axis_index("head").astype(jnp.int32)
    shaped = jax.ShapeDtypeStruct

    x_parts = [swap(inputs, "head", n_head, k) for k in range(1, n_head)]
    mod_parts = [swap(mod_table, "head", n_head, k) for k in range(1, n_head)]
    first = (jnp.transpose(w_qkv, (1, 0, 2)), inputs, jnp.transpose(mod_table, (1, 0, 2)), stale_kv)
    w, x_own, mod_own, stale, ids, cos, sin = call(
        load_kernel,
        tuple(pltpu.VMEM(v.shape, v.dtype) for v in first)
        + (shaped((8, DH), jnp.int32), shaped((rows, DH), F32), shaped((rows, DH), F32)),
        [SMEM] * 2 + [ANY] * len(first),
        [pltpu.SemaphoreType.DMA((6,))],
        size=2 * w_qkv.size,
    )(in_hbm(step_ids), slab_order, *map(in_hbm, first))
    x_parts = [x_own] + x_parts
    mod_parts = [mod_own] + [jnp.transpose(part, (1, 0, 2)) for part in mod_parts]

    def across(values, k):
        return swap(values, "patch", n_patch, k)

    def line_of(values):
        return [values] + [across(values, k) for k in range(2 * PLANE, n_patch, 2 * PLANE)]

    def plane_of(values):
        return [values] + [across(values, k) for k in range(1, PLANE)]


    kv_shape = shaped((2, rows, cols), BF16)
    common = (head[None], ids, *x_parts, *mod_parts, w, cos, sin)
    specs = [SMEM] + [VMEM] * (2 * n_head + 5)
    a, kv = call(
        functools.partial(fresh_kernel, n_head),
        (shaped((n_head, rows, feats), BF16), shaped((4, rows, cols), BF16)),
        specs,
        flops=4 * rows * w_qkv.size // 3,
        size=2 * w_qkv.size,
    )(*common, stale)
    q, kv1 = call(
        functools.partial(rest_kernel, n_head),
        (kv_shape, kv_shape),
        specs,
        flops=8 * rows * w_qkv.size // 3,
        size=2 * w_qkv.size,
    )(*common, a)

    w_own, kv1 = lax.optimization_barrier((w_out.T, kv1))
    kv_pair = line_of(kv)
    q_mate = across(q, PLANE)
    w_x = across(w_own, 1)
    w_late, q_mate = lax.optimization_barrier((w_own, q_mate))
    w_rest = jnp.stack(line_of(w_late)[1:])
    kv_plane = plane_of(jnp.stack(kv_pair))
    w_rest, q_mate = lax.optimization_barrier((w_rest, q_mate))
    w_y = across(jnp.stack([w_own, w_x]), 2)
    rest_y = across(w_rest, 2)
    tall = 2 * STEPS * rows
    part = call(
        attend_kernel,
        shaped((tall, cols + DH), BF16),
        [VMEM] * (3 + PLANE),
        flops=4 * STEPS * rows * n_patch * rows * cols,
    )(q, q_mate, kv1, *kv_plane)
    rest_y, part = lax.optimization_barrier((rest_y, part))
    rest_x = across(jnp.stack([w_rest, rest_y]), 1)
    o = call(merge_kernel, shaped((tall, cols), BF16), [VMEM] * 2)(part, across(part, PLANE))
    o, w_y, rest_x = lax.optimization_barrier((o, w_y, rest_x))
    near = [(w_own, w_rest), (w_x, rest_x[0]), (w_y[0], rest_y), (w_y[1], rest_x[1])]
    w_plane = [jnp.concatenate([first[None], others]) for first, others in near]
    wide = PLANE * piece

    half = tall // 2

    def project(mate, bit, dtype):
        return call(
            functools.partial(project_kernel, n_head, n_patch, bit, mate),
            shaped((half, wide), dtype),
            [SMEM] * 2 + [VMEM] * (1 + PLANE),
            [pltpu.VMEM((PLANE, half, piece), F32)],
            2 * half * wide * cols,
            2 * wide * cols,
        )(patch[None], head[None], o, *w_plane)

    def gated(mate):
        sent = [swap(project(mate, k, BF16), "head", n_head, k) for k in range(1, n_head)]
        return call(
            functools.partial(gate_kernel, n_patch),
            shaped((STEPS, rows, wide), BF16),
            [SMEM] + [VMEM] * (2 + n_head),
        )(patch[None], ids, mod_own, project(mate, 0, F32), *sent)

    out_back = across(gated(1), PLANE)
    out_own = gated(0)
    second = (patch // PLANE) % 2 == 1
    return jnp.concatenate(
        [jnp.where(second, out_back, out_own), jnp.where(second, out_own, out_back)], axis=2
    )


def solution(mesh):
    in_specs = (
        P(None, "patch", "head"),
        P(None, "patch", "head"),
        P(None, None, "head"),
        P("head", "patch"),
        P(None, None, "head"),
        P(),
        P("patch"),
    )
    run = functools.partial(body, mesh.shape["patch"], mesh.shape["head"])
    return jax.shard_map(
        run, mesh=mesh, in_specs=in_specs, out_specs=P(None, "patch", "head"), check_vma=False
    )
```

```python
import functools
import math

import jax
import jax.numpy as jnp
from jax import lax
from jax.experimental import pallas as pl
from jax.experimental.pallas import tpu as pltpu
from jax.sharding import PartitionSpec as P

DH = 128
STEPS = 2
PLANE = 4
MIB = 1024 * 1024
VMEM = pl.BlockSpec(memory_space=pltpu.VMEM)
SMEM = pl.BlockSpec(memory_space=pltpu.SMEM)
ANY = pl.BlockSpec(memory_space=pl.ANY)
BF16, F32 = jnp.bfloat16, jnp.float32
NT = (((1,), (1,)), ((), ()))


def swap(values, axis, count, bit):
    return lax.ppermute(values, axis, [(i, i ^ bit) for i in range(count)])


def load_kernel(ids, slab, w_ref, x_ref, mod_ref, stale_ref, w_out, x_out, mod_out, stale_out, *refs):
    ids_out, cos_ref, sin_ref, sems = refs
    copies = [
        pltpu.make_async_copy(w_ref.at[slot], w_out.at[slot], sems.at[slot])
        for slot in range(3)
    ]
    copies.append(pltpu.make_async_copy(x_ref, x_out, sems.at[3]))
    copies.append(pltpu.make_async_copy(mod_ref, mod_out, sems.at[4]))
    copies.append(pltpu.make_async_copy(stale_ref, stale_out, sems.at[5]))
    for copy in copies:
        copy.start()
    row = lax.broadcasted_iota(jnp.int32, ids_out.shape, 0)
    tile = jnp.zeros(ids_out.shape, jnp.int32)
    for step in range(STEPS):
        tile = jnp.where(row == step, ids[step], tile)
    ids_out[...] = tile
    rows, half = cos_ref.shape[0], DH // 2
    lane = lax.broadcasted_iota(jnp.int32, cos_ref.shape, 1)
    spot = slab[0] * rows + lax.broadcasted_iota(jnp.int32, cos_ref.shape, 0)
    power = jnp.where(lane < half, lane, lane - half).astype(F32) * (-2.0 / DH)
    angle = spot.astype(F32) * jnp.exp(power * math.log(10000.0))
    cos_ref[...] = jnp.cos(angle)
    sin = jnp.sin(angle)
    sin_ref[...] = jnp.where(lane < half, -sin, sin)
    for copy in copies:
        copy.wait()


def table_row(mod_ref, kind, ids_ref, step):
    chosen = ids_ref[step : step + 1, :1]
    table = mod_ref[kind]
    return sum(
        jnp.where(chosen == r, table[r : r + 1], 0.0) for r in range(table.shape[0])
    )


def normalized(step, x_refs, mod_refs, ids_ref):
    hidden = [ref[step].astype(F32) for ref in x_refs]
    width = sum(part.shape[1] for part in hidden)
    mean = sum(jnp.sum(part, axis=1, keepdims=True) for part in hidden) / width
    square = sum(jnp.sum(part * part, axis=1, keepdims=True) for part in hidden) / width
    inv = lax.rsqrt(square - mean * mean + 1e-06)
    parts = []
    for part, mod_ref in zip(hidden, mod_refs):
        shift = table_row(mod_ref, 0, ids_ref, step)
        scale = table_row(mod_ref, 1, ids_ref, step)
        parts.append(((part - mean) * inv * (1.0 + scale) + shift).astype(BF16))
    return parts


def projected(parts, w_ref, slot, head):
    feats = parts[0].shape[1]
    total = jnp.zeros((parts[0].shape[0], w_ref.shape[2]), F32)
    for number, part in enumerate(parts):
        start = pl.multiple_of((head[0] ^ number) * feats, feats)
        w = w_ref[slot, pl.ds(start, feats), :]
        total += jnp.dot(part, w, preferred_element_type=F32)
    return total


def rotated(values, cos, sin):
    blocks = []
    for start in range(0, values.shape[1], DH):
        u = values[:, start : start + DH]
        blocks.append(u * cos + pltpu.roll(u, DH // 2, 1) * sin)
    return jnp.concatenate(blocks, axis=1)


def qkv_kernel(n_head, head, ids_ref, *refs):
    x_refs, mod_refs = refs[:n_head], refs[n_head : 2 * n_head]
    w_ref, cos_ref, sin_ref, stale_ref, q_ref, kv_ref, kv1_ref = refs[2 * n_head :]
    rows = x_refs[0].shape[1]
    steps = [normalized(step, x_refs, mod_refs, ids_ref) for step in range(STEPS)]
    parts = [jnp.concatenate(pair, axis=0) for pair in zip(*steps)]
    cos = jnp.concatenate([cos_ref[...]] * STEPS, axis=0)
    sin = jnp.concatenate([sin_ref[...]] * STEPS, axis=0)
    queries = rotated(projected(parts, w_ref, 0, head), cos, sin).astype(BF16)
    keys = rotated(projected(parts, w_ref, 1, head), cos, sin).astype(BF16)
    values = projected(parts, w_ref, 2, head).astype(BF16)
    for step in range(STEPS):
        spot = slice(step * rows, (step + 1) * rows)
        q_ref[step] = queries[spot]
    kv_ref[:2] = stale_ref[...]
    kv_ref[2], kv_ref[3] = keys[:rows], values[:rows]
    kv1_ref[0], kv1_ref[1] = keys[rows:], values[rows:]


def split3(values):
    high = values.astype(BF16).astype(F32)
    middle = (values - high).astype(BF16).astype(F32)
    return [high, middle, values - high - middle]


def attend_kernel(q_ref, mate_ref, kv1_ref, *refs):
    kv_refs, out_ref = refs[:PLANE], refs[PLANE]
    blocks, _, rows, cols = kv_refs[0].shape
    old_rows = PLANE * blocks * rows
    shape = (2 * rows, old_rows + rows)
    mine = lax.broadcasted_iota(jnp.int32, shape, 0) < rows
    stray = jnp.where(mine, 0, PLANE * blocks)
    drop = lax.broadcasted_iota(jnp.int32, shape, 1) // rows == stray
    lane = lax.broadcasted_iota(jnp.int32, (2 * rows, DH), 1)
    for step in range(STEPS):
        fresh = (kv_refs[0].at[0, 2:], kv1_ref)[step]
        stats = jnp.zeros((2 * rows, DH), F32)
        mixed = []
        for head in range(cols // DH):
            lanes = slice(head * DH, (head + 1) * DH)

            def rows_of(kind):
                old = [ref[:, 2 * step + kind, :, lanes].reshape(blocks * rows, DH) for ref in kv_refs]
                return jnp.concatenate([*old, fresh[kind, :, lanes]], axis=0)

            queries = jnp.concatenate([q_ref[step, :, lanes], mate_ref[step, :, lanes]], axis=0)
            scores = lax.dot_general(queries, rows_of(0), NT, preferred_element_type=F32)
            scores = jnp.where(drop, -1e30, scores * (1.0 / math.sqrt(DH)))
            top = jnp.max(scores, axis=1, keepdims=True)
            weights = jnp.exp(scores - top)
            totals = jnp.sum(weights, axis=1, keepdims=True)
            mixed.append(
                jnp.dot(weights.astype(BF16), rows_of(1), preferred_element_type=F32) / totals
            )
            for place, piece in enumerate(split3(top) + split3(totals)):
                stats = jnp.where(lane == head * 8 + place, piece, stats)
        packed = jnp.concatenate([*mixed, stats], axis=1).astype(BF16)
        for mate in range(2):
            start = (mate * STEPS + step) * rows
            out_ref[start : start + rows, :] = packed[mate * rows : (mate + 1) * rows]


def merge_kernel(part_ref, other_ref, o_ref):
    rows = part_ref.shape[0] // 2
    cols = o_ref.shape[1]
    source = lax.broadcasted_iota(jnp.int32, (DH, DH), 0)
    parts = [
        part_ref[...],
        jnp.concatenate([other_ref[rows:], other_ref[:rows]], axis=0),
    ]
    for head in range(cols // DH):
        lanes = slice(head * DH, (head + 1) * DH)

        def spread(part, first):
            pick = (source >= head * 8 + first) & (source < head * 8 + first + 3)
            return jnp.dot(part[:, cols:], pick.astype(F32).astype(BF16), preferred_element_type=F32)

        tops = [spread(part, 0) for part in parts]
        best = functools.reduce(jnp.maximum, tops)
        scales = [spread(part, 3) * jnp.exp(t - best) for part, t in zip(parts, tops)]
        mixed = sum(s * part[:, lanes].astype(F32) for s, part in zip(scales, parts))
        o_ref[:, lanes] = (mixed / sum(scales)).astype(BF16)


def project_kernel(n_head, n_patch, bit, mate, patch, head, o_ref, *refs):
    w_refs, (out_ref, sums) = refs[:PLANE], refs[PLANE:]
    rows = out_ref.shape[0]
    slot = head[0] ^ bit ^ (patch[0] // (n_patch // n_head))
    for near in range(PLANE):
        sums[(patch[0] % PLANE) ^ near] = lax.dot_general(
            o_ref[mate * rows : (mate + 1) * rows, :],
            w_refs[near][slot],
            NT,
            preferred_element_type=F32,
        )
    out = jnp.concatenate([sums[c] for c in range(PLANE)], axis=1)
    out_ref[...] = out.astype(out_ref.dtype)


def gate_kernel(n_patch, patch, ids_ref, mod_ref, *refs):
    sum_refs, out_ref = refs[:-1], refs[-1]
    total = sum(ref[...].astype(F32) for ref in sum_refs)
    rows, width = total.shape
    each = rows // STEPS
    second = (patch[0] // PLANE) % 2 == 1
    for step in range(STEPS):
        gate = table_row(mod_ref, 2, ids_ref, step)
        gate = jnp.where(second, gate[:, width:], gate[:, :width])
        out_ref[step] = (gate * total[step * each : (step + 1) * each]).astype(BF16)


def in_hbm(values):
    return pltpu.with_memory_space_constraint(values, pltpu.HBM)


def call(kernel, shapes, ins, scratch=(), flops=0, size=0, limit=16):
    return pl.pallas_call(
        kernel,
        out_shape=shapes,
        in_specs=ins,
        out_specs=jax.tree.map(lambda _: VMEM, shapes),
        scratch_shapes=scratch,
        compiler_params=pltpu.CompilerParams(vmem_limit_bytes=limit * MIB),
        cost_estimate=pl.CostEstimate(flops=flops, bytes_accessed=size, transcendentals=0),
    )


def body(n_patch, n_head, inputs, stale_kv, w_qkv, w_out, mod_table, step_ids, slab_order):
    rows, feats = inputs.shape[1:]
    cols = w_qkv.shape[2]
    piece = w_out.shape[1]
    patch = lax.axis_index("patch").astype(jnp.int32)
    head = lax.axis_index("head").astype(jnp.int32)
    shaped = jax.ShapeDtypeStruct

    x_parts = [swap(inputs, "head", n_head, k) for k in range(1, n_head)]
    mod_parts = [swap(mod_table, "head", n_head, k) for k in range(1, n_head)]
    first = (jnp.transpose(w_qkv, (1, 0, 2)), inputs, jnp.transpose(mod_table, (1, 0, 2)), stale_kv)
    w, x_own, mod_own, stale, ids, cos, sin = call(
        load_kernel,
        tuple(pltpu.VMEM(v.shape, v.dtype) for v in first)
        + (shaped((8, DH), jnp.int32), shaped((rows, DH), F32), shaped((rows, DH), F32)),
        [SMEM] * 2 + [ANY] * len(first),
        [pltpu.SemaphoreType.DMA((6,))],
        size=2 * w_qkv.size,
    )(in_hbm(step_ids), slab_order, *map(in_hbm, first))
    x_parts = [x_own] + x_parts
    mod_parts = [mod_own] + [jnp.transpose(part, (1, 0, 2)) for part in mod_parts]

    def across(values, k):
        return swap(values, "patch", n_patch, k)

    def line_of(values):
        return [values] + [across(values, k) for k in range(2 * PLANE, n_patch, 2 * PLANE)]

    def plane_of(values):
        return [values] + [across(values, k) for k in range(1, PLANE)]


    kv_shape = shaped((2, rows, cols), BF16)
    q, kv, kv1 = call(
        functools.partial(qkv_kernel, n_head),
        (kv_shape, shaped((4, rows, cols), BF16), kv_shape),
        [SMEM] + [VMEM] * (2 * n_head + 5),
        flops=2 * STEPS * rows * w_qkv.size,
        size=2 * w_qkv.size,
    )(head[None], ids, *x_parts, *mod_parts, w, cos, sin, stale)

    w_own, kv = lax.optimization_barrier((w_out.T, kv))
    kv_pair = line_of(kv)
    q_mate = across(q, PLANE)
    w_x = across(w_own, 2)
    w_late, q_mate = lax.optimization_barrier((w_own, q_mate))
    w_rest = jnp.stack(line_of(w_late)[1:])
    kv_plane = plane_of(jnp.stack(kv_pair))
    w_rest, q_mate = lax.optimization_barrier((w_rest, q_mate))
    w_y = across(jnp.stack([w_own, w_x]), 1)
    rest_y = across(w_rest, 1)
    tall = 2 * STEPS * rows
    part = call(
        attend_kernel,
        shaped((tall, cols + DH), BF16),
        [VMEM] * (3 + PLANE),
        flops=4 * STEPS * rows * n_patch * rows * cols,
    )(q, q_mate, kv1, *kv_plane)
    rest_y, part = lax.optimization_barrier((rest_y, part))
    rest_x = across(jnp.stack([w_rest, rest_y]), 2)
    o = call(merge_kernel, shaped((tall, cols), BF16), [VMEM] * 2)(part, across(part, PLANE))
    o, w_y, rest_x = lax.optimization_barrier((o, w_y, rest_x))
    near = [(w_own, w_rest), (w_y[0], rest_y), (w_x, rest_x[0]), (w_y[1], rest_x[1])]
    w_plane = [jnp.concatenate([first[None], others]) for first, others in near]
    wide = PLANE * piece

    half = tall // 2

    def project(mate, bit, dtype):
        return call(
            functools.partial(project_kernel, n_head, n_patch, bit, mate),
            shaped((half, wide), dtype),
            [SMEM] * 2 + [VMEM] * (1 + PLANE),
            [pltpu.VMEM((PLANE, half, piece), F32)],
            2 * half * wide * cols,
            2 * wide * cols,
        )(patch[None], head[None], o, *w_plane)

    def gated(mate):
        sent = [swap(project(mate, k, BF16), "head", n_head, k) for k in range(1, n_head)]
        return call(
            functools.partial(gate_kernel, n_patch),
            shaped((STEPS, rows, wide), BF16),
            [SMEM] + [VMEM] * (2 + n_head),
        )(patch[None], ids, mod_own, project(mate, 0, F32), *sent)

    out_back = across(gated(1), PLANE)
    out_own = gated(0)
    second = (patch // PLANE) % 2 == 1
    return jnp.concatenate(
        [jnp.where(second, out_back, out_own), jnp.where(second, out_own, out_back)], axis=2
    )


def solution(mesh):
    in_specs = (
        P(None, "patch", "head"),
        P(None, "patch", "head"),
        P(None, None, "head"),
        P("head", "patch"),
        P(None, None, "head"),
        P(),
        P("patch"),
    )
    run = functools.partial(body, mesh.shape["patch"], mesh.shape["head"])
    return jax.shard_map(
        run, mesh=mesh, in_specs=in_specs, out_specs=P(None, "patch", "head"), check_vma=False
    )
```
